512 devices in a mesh: section: 16 (over y, core), expert: 32 (over z, x).
Axes of the slice: x: 4, y: 8, z: 8, core: 2. Of those that a mesh axis runs over, the one named last changes fastest.
Arguments:
- act_fwd: bfloat16 [16, 768, 3584], P('section', 'expert'), may hold values from -6 to 6
- route_fwd: int32 [16, 768, 2], P('section', 'expert'), may hold values from 0 to 3, all different within a row; in each aligned block of 24 rows (0 to 23, 24 to 47, ..., all dimensions but the last counted through in order) at most 14 rows name the same one
- weight_fwd: float32 [16, 768, 2], P('section', 'expert'), may hold values from 0.3 to 1.2
- act_bwd: bfloat16 [16, 768, 3584], P('section', 'expert'), may hold values from -6 to 6
- route_bwd: int32 [16, 768, 2], P('section', 'expert'), may hold values from 0 to 3, all different within a row; in each aligned block of 24 rows (0 to 23, 24 to 47, ..., all dimensions but the last counted through in order) at most 14 rows name the same one
- weight_bwd: float32 [16, 768, 2], P('section', 'expert'), may hold values from 0.3 to 1.2
- cot_bwd: bfloat16 [16, 768, 3584], P('section', 'expert'), may hold values from -6 to 6
- norm_gain: float32 [16, 3584], P('section'), may hold values from 0.25 to 1.75
- w_gate: bfloat16 [16, 32, 3584, 128], P('section', 'expert'), may hold values from -0.09375 to 0.09375
- w_up: bfloat16 [16, 32, 3584, 128], P('section', 'expert'), may hold values from -0.09375 to 0.09375
- w_down: bfloat16 [16, 32, 128, 3584], P('section', 'expert'), may hold values from -0.1875 to 0.1875
Outputs:
- act_next: bfloat16 [16, 768, 3584], P('section', 'expert')
- cot_next: bfloat16 [16, 768, 3584], P('section', 'expert')
- gate_grad: bfloat16 [16, 768, 2], P('section', 'expert')
The draws below stay inside these ranges and needn't reach their ends.
Inputs may be any that keep to these rules, and one draw needn't show every extreme that they name: `route_fwd`: each row names 2 different experts; among the 24 rows of one device no expert is named more than 14 times, and in some devices' rows some expert exactly 14 times. `route_bwd`: each row names 2 different experts; among the 24 rows of one device no expert is named more than 14 times, and in some devices' rows some expert exactly 14 times.
All inputs are finite; a program needn't handle non-finite values.
Results may differ from the reference program's by a relative error of at most 0.019.
Values may be sent and summed in bfloat16 or wider, within the bound.
No kernel may reach another device: no remote copies, remote signals or barrier semaphores. Data moves between devices by JAX's collectives and lax.ppermute only.
A program may use at most 64 MiB of HBM per device.

```python
import math
import jax
import jax.numpy as jnp
import numpy as np
from jax import lax

D = 3584
FE = 1024
TOPK = 2
EXPERTS = 4
TOK_DEV = 24
SLICES = 8
FE_DEV = 128
TOKENS = 768
CAP = 14
N_SECTION = 16
N_EXPERT = 32


def shard_levels(stream_key, dims, cuts, low, top_value):
    level = 1.0
    for axis_at, parts in cuts:
        steps = jax.random.uniform(jax.random.fold_in(jax.random.fold_in(stream_key, 6), axis_at), (parts,), jnp.float32, low / len(cuts), top_value / len(cuts))
        level = level * jnp.repeat(jnp.exp(steps), dims[axis_at] // parts).reshape((-1,) + (1,) * (len(dims) - 1 - axis_at))
    return level


def assign_block(own_key, own, number, rows, number_of, top, most, skew):
    order = jax.random.permutation(own_key, number_of)
    crowded, common = shares(number_of, rows * top, most, skew, True), shares(number_of, rows * top, most, skew, False)
    places = jnp.arange(number_of)

    def named(tallies, turn):
        used = int((tallies > 0).sum())
        fixed = max(1, used // 4)
        moved = fixed + (places - fixed + turn * (used - fixed)) % max(1, number_of - fixed)
        return jnp.zeros((number_of,), jnp.int32).at[order[jnp.where(places < fixed, places, moved)]].set(jnp.asarray(tallies, jnp.int32))

    tallies = jnp.where(number % 4 == 0, named(crowded, number // 4), named(common, number - number // 4 - 1))
    mixed = jax.random.permutation(jax.random.fold_in(own, 3), number_of)
    giver, taker = mixed[0:number_of // 2 * 2:2], mixed[1:number_of // 2 * 2:2]
    slack = jnp.minimum(tallies[giver] - 1, most - tallies[taker]) // 2
    slack = jnp.where((giver == order[0]) | (taker == order[0]) | (tallies[taker] == 0), 0, jnp.maximum(slack, 0))
    moved = jax.random.randint(jax.random.fold_in(own, 4), (number_of // 2,), 0, 1 << 20) % (slack + 1)
    tallies = tallies.at[giver].add(-moved).at[taker].add(moved)
    items = jnp.searchsorted(jnp.cumsum(tallies), jnp.arange(rows * top), side="right").astype(jnp.int32)
    table = items.reshape(top, rows).T
    table = table[jax.random.permutation(jax.random.fold_in(own, 1), rows)]
    turn = jax.random.randint(jax.random.fold_in(own, 2), (rows, 1), 0, top)
    return jnp.take_along_axis(table, (jnp.arange(top)[None, :] + turn) % top, axis=1)


def shares(number_of, total, bound, lean, full):
    loads = [(1 << 20) // math.isqrt(grade ** lean) + 1 for grade in range(1, number_of + 1)]
    largest = bound if full else min(bound, max(-(-total // number_of), total * loads[0] // sum(loads)))
    least = 1 if total - largest >= number_of - 1 else 0
    counts, surplus = [largest] + [least] * (number_of - 1), total - largest - least * (number_of - 1)
    while surplus > 0:
        free = [i for i in range(1, number_of) if counts[i] < largest] or [i for i in range(1, number_of) if counts[i] < bound]
        mass, remaining = sum([loads[i] for i in free]), surplus
        for i in free:
            more = min(bound - counts[i], max(1, remaining * loads[i] // mass), surplus)
            counts[i] = counts[i] + more
            surplus = surplus - more
    return np.array(counts)


def centred(own_key, shape, width, most, cuts=(), held_as=jnp.bfloat16):
    level = shard_levels(own_key, shape, cuts, -0.22, 0.18) if cuts else 1.0
    result = jax.random.normal(own_key, shape, jnp.float32) * width * level
    return jnp.minimum(jnp.maximum(result, -most), most).astype(held_as)


def setup_inputs(seed: int = 0) -> dict:
    seeds = jax.random.split(jax.random.key(seed), 12)
    act_fwd = centred(seeds[0], (N_SECTION, TOKENS, D), 1.0, 6.0, ((0, 16), (1, 32)))
    route_fwd_keys = jax.random.split(jax.random.fold_in(seeds[1], 1), N_SECTION * TOKENS // TOK_DEV)
    route_fwd_turns = jax.random.permutation(jax.random.fold_in(seeds[1], 3), N_SECTION * TOKENS // TOK_DEV)
    route_fwd = jax.vmap(lambda own, number: assign_block(jax.random.fold_in(seeds[1], 2), own, number, TOK_DEV, EXPERTS, TOPK, CAP, 2))(route_fwd_keys, route_fwd_turns).reshape((N_SECTION, TOKENS, TOPK))
    weight_fwd = jnp.clip(0.3 + 0.90000004 * jax.random.uniform(seeds[2], (N_SECTION, TOKENS, TOPK), jnp.float32) ** shard_levels(seeds[2], (N_SECTION, TOKENS, TOPK), ((0, 16), (1, 32)), -0.2, 0.2), 0.3, 1.2)
    act_bwd = centred(seeds[3], (N_SECTION, TOKENS, D), 1.0, 6.0, ((0, 16), (1, 32)))
    route_bwd_keys = jax.random.split(jax.random.fold_in(seeds[4], 1), N_SECTION * TOKENS // TOK_DEV)
    route_bwd_turns = jax.random.permutation(jax.random.fold_in(seeds[4], 3), N_SECTION * TOKENS // TOK_DEV)
    route_bwd = jax.vmap(lambda own, number: assign_block(jax.random.fold_in(seeds[4], 2), own, number, TOK_DEV, EXPERTS, TOPK, CAP, 2))(route_bwd_keys, route_bwd_turns).reshape((N_SECTION, TOKENS, TOPK))
    weight_bwd = jnp.clip(0.3 + 0.90000004 * jax.random.uniform(seeds[5], (N_SECTION, TOKENS, TOPK), jnp.float32) ** shard_levels(seeds[5], (N_SECTION, TOKENS, TOPK), ((0, 16), (1, 32)), -0.2, 0.2), 0.3, 1.2)
    cot_bwd = centred(seeds[6], (N_SECTION, TOKENS, D), 1.0, 6.0, ((0, 16), (1, 32)))
    norm_gain = jnp.clip(1.0 + 0.15 * jax.random.normal(seeds[7], (N_SECTION, D), jnp.float32), 0.25, 1.75)
    w_gate = centred(seeds[8], (N_SECTION, N_EXPERT, D, FE_DEV), D ** -0.5, 0.09375, ((0, 16), (1, 32)))
    w_up = centred(seeds[9], (N_SECTION, N_EXPERT, D, FE_DEV), D ** -0.5, 0.09375, ((0, 16), (1, 32)))
    w_down = centred(seeds[10], (N_SECTION, N_EXPERT, FE_DEV, D), FE ** -0.5, 0.1875, ((0, 16), (1, 32)))
    return dict(act_fwd=act_fwd, route_fwd=route_fwd, weight_fwd=weight_fwd, act_bwd=act_bwd, route_bwd=route_bwd, weight_bwd=weight_bwd, cot_bwd=cot_bwd, norm_gain=norm_gain, w_gate=w_gate, w_up=w_up, w_down=w_down)


def normalize(rows, gain):
    values = rows.astype(jnp.float32)
    scale = lax.rsqrt(lax.optimization_barrier(jnp.mean(values * values, axis=-1, keepdims=True)) + 1e-06)
    unit = values * scale
    return (unit, scale, (unit * gain).astype(jnp.bfloat16))

def slot_index(route):
    flat = route.reshape(N_EXPERT, TOK_DEV * TOPK)
    onehot = (flat[..., None] == jnp.arange(EXPERTS, dtype=jnp.int32)).astype(jnp.int32)
    before = jnp.cumsum(onehot, axis=1) - onehot
    rank = lax.optimization_barrier(jnp.sum(before * onehot, axis=2))
    source = jnp.arange(N_EXPERT, dtype=jnp.int32)[:, None]
    return (flat * (N_EXPERT * CAP) + source * CAP + rank).reshape(-1).astype(jnp.int32)

def packed(rows, slots):
    buffer = jnp.zeros((EXPERTS * N_EXPERT * CAP, D), rows.dtype)
    buffer = buffer.at[slots].set(jnp.repeat(rows, TOPK, axis=0))
    return buffer.reshape(EXPERTS, N_EXPERT * CAP, D)

def expert_pass(rows, wg, wu, wd):
    rows_f = rows.astype(jnp.float32)
    gate = jnp.einsum('erd,egdf->egrf', rows_f, wg.astype(jnp.float32))
    upper = jnp.einsum('erd,egdf->egrf', rows_f, wu.astype(jnp.float32))
    inner = (gate * jax.nn.sigmoid(gate) * upper).astype(jnp.bfloat16)
    part = jnp.einsum('egrf,egfd->egrd', inner.astype(jnp.float32), wd.astype(jnp.float32)).astype(jnp.bfloat16)
    return (gate, upper, part)

def one_section(inputs):
    x_a, route_a, weight_a, x_b, route_b, weight_b, cot, gain, w_g, w_u, w_d = inputs
    wg = w_g.reshape(EXPERTS, SLICES, D, FE_DEV)
    wu = w_u.reshape(EXPERTS, SLICES, D, FE_DEV)
    wd = w_d.reshape(EXPERTS, SLICES, FE_DEV, D)
    unit_a, scale_a, normed_a = normalize(x_a, gain)
    slots_a = slot_index(route_a)
    part_a = expert_pass(packed(normed_a, slots_a), wg, wu, wd)[2]
    out_sum = lax.optimization_barrier(jnp.sum(part_a.astype(jnp.float32), axis=1))
    picked = out_sum.reshape(-1, D)[slots_a].reshape(TOKENS, TOPK, D)
    layer_out = (x_a.astype(jnp.float32) + lax.optimization_barrier(jnp.sum(weight_a[..., None] * picked, axis=1))).astype(jnp.bfloat16)
    unit_b, scale_b, normed_b = normalize(x_b, gain)
    slots_b = slot_index(route_b)
    rows_c = packed(cot, slots_b)
    gate, upper, part_b = expert_pass(packed(normed_b, slots_b), wg, wu, wd)
    rows_cf = rows_c.astype(jnp.float32)
    grad_part = jnp.einsum('egrd,erd->egr', part_b.astype(jnp.float32), rows_cf).astype(jnp.bfloat16)
    grad_rows = lax.optimization_barrier(jnp.sum(grad_part.astype(jnp.float32), axis=1))
    d_inner = jnp.einsum('erd,egfd->egrf', rows_cf, wd.astype(jnp.float32))
    sig = jax.nn.sigmoid(gate)
    d_gate = (d_inner * upper * sig * (1.0 + gate * (1.0 - sig))).astype(jnp.bfloat16)
    d_up = (d_inner * gate * sig).astype(jnp.bfloat16)
    d_part = (jnp.einsum('egrf,egdf->egrd', d_gate.astype(jnp.float32), wg.astype(jnp.float32)) + jnp.einsum('egrf,egdf->egrd', d_up.astype(jnp.float32), wu.astype(jnp.float32))).astype(jnp.bfloat16)
    d_sum = lax.optimization_barrier(jnp.sum(d_part.astype(jnp.float32), axis=1))
    picked_b = d_sum.reshape(-1, D)[slots_b].reshape(TOKENS, TOPK, D)
    d_normed = lax.optimization_barrier(jnp.sum(weight_b[..., None] * picked_b, axis=1))
    gate_grad = grad_rows.reshape(-1)[slots_b].reshape(TOKENS, TOPK).astype(jnp.bfloat16)
    q_term = d_normed * gain
    d_input = cot.astype(jnp.float32) + scale_b * (q_term - unit_b * lax.optimization_barrier(jnp.mean(q_term * unit_b, axis=-1, keepdims=True)))
    return (layer_out, d_input.astype(jnp.bfloat16), gate_grad)

def reference(act_fwd, route_fwd, weight_fwd, act_bwd, route_bwd, weight_bwd, cot_bwd, norm_gain, w_gate, w_up, w_down):
    layer_out, d_input, gate_grad = lax.map(one_section, (act_fwd, route_fwd, weight_fwd, act_bwd, route_bwd, weight_bwd, cot_bwd, norm_gain, w_gate, w_up, w_down))
    zero_block = jnp.zeros((1, TOKENS, D), jnp.bfloat16)
    act_next = jnp.concatenate([zero_block, layer_out[:-1]], axis=0)
    cot_next = jnp.concatenate([d_input[1:], zero_block], axis=0)
    return (act_next, cot_next, gate_grad)
```

```python
import functools

import jax
import jax.numpy as jnp
from jax import lax
from jax.experimental import pallas as pl
from jax.experimental.pallas import tpu as pltpu
from jax.sharding import PartitionSpec as P

EXPERTS = 4
GRID_X = 4
GRID_Z = 8
SLOT = 16
F32 = jnp.float32
BF16 = jnp.bfloat16
NT = (((1,), (1,)), ((), ()))
TN = (((0,), (0,)), ((), ()))


def expert_pairs(move):
    pairs = []
    for z in range(GRID_Z):
        for x in range(GRID_X):
            to_z, to_x = move(z, x)
            pairs.append((z * GRID_X + x, to_z % GRID_Z * GRID_X + to_x))
    return pairs


def signed(z, even, odd):
    return z + (odd if z % 2 else even)


HOP_W = expert_pairs(lambda z, x: (z ^ 1, x))
HOP_A = expert_pairs(lambda z, x: (signed(z, -1, 1), x))
HOP_B = expert_pairs(lambda z, x: (signed(z, 2, -2), x))
HOP_B_BACK = expert_pairs(lambda z, x: (signed(z, -2, 2), x))
HOP_C = expert_pairs(lambda z, x: (signed(z, -3, 3), x))
HOP_X1 = expert_pairs(lambda z, x: (z, x ^ 1))
HOP_X3 = expert_pairs(lambda z, x: (z, x ^ 3))


def hop(value, pairs):
    return lax.ppermute(value, "expert", pairs)


def shifted(value, axis, by):
    devices = lax.axis_size(axis)
    pairs = [(i, i + by) for i in range(devices) if 0 <= i + by < devices]
    return lax.ppermute(value, axis, pairs)


def kernel_call(kernel, outs, n_in, scratch=(), info=True, limit=32):
    smem = pl.BlockSpec(memory_space=pltpu.SMEM)
    vmem = pl.BlockSpec(memory_space=pltpu.VMEM)
    return pl.pallas_call(
        kernel,
        out_shape=[jax.ShapeDtypeStruct(s, d) for s, d in outs],
        in_specs=[smem] * info + [vmem] * n_in,
        out_specs=[vmem] * len(outs),
        scratch_shapes=list(scratch),
        compiler_params=pltpu.CompilerParams(vmem_limit_bytes=limit * 1024 * 1024),
    )


def slot_masks(info_ref, route_ref):
    tokens = route_ref.shape[0]
    own, odd = info_ref[0], info_ref[1]
    lanes = lax.broadcasted_iota(jnp.int32, (tokens, 128), 1)
    route = route_ref[...]
    named = [(route[:, k : k + 1] == lanes).astype(F32) for k in range(2)]
    row = lax.broadcasted_iota(jnp.int32, (tokens, tokens), 0)
    col = lax.broadcasted_iota(jnp.int32, (tokens, tokens), 1)
    earlier = (col < row).astype(BF16)
    counts = jnp.dot(earlier, (named[0] + named[1]).astype(BF16), preferred_element_type=F32)
    out = []
    for k in range(2):
        rank = jnp.sum(named[k] * counts, axis=1, keepdims=True).astype(jnp.int32)
        away = (route[:, k : k + 1] - own) & 3
        side = jnp.where((away == 3) == (odd == 0), 1, 2)
        rel = jnp.where(away == 0, 0, jnp.where(away == 2, 3, side))
        slots = lax.broadcasted_iota(jnp.int32, (tokens, 4 * SLOT), 1)
        out.append((slots == rel * SLOT + rank, rel, rank))
    return out


def normalized(x, gain):
    values = x.astype(F32)
    scale = lax.rsqrt(jnp.mean(values * values, axis=-1, keepdims=True) + 1e-06)
    return values * scale, scale


def pack_kernel(info_ref, x_ref, route_ref, gain_ref, *rest):
    masks = slot_masks(info_ref, route_ref)
    place = (masks[0][0] | masks[1][0]).astype(F32).astype(BF16)
    unit, _ = normalized(x_ref[...], gain_ref[...])
    normed = (unit * gain_ref[...]).astype(BF16)
    sources = [normed]
    if len(rest) == 5:
        sources.append(rest[0][...])
    outs = rest[-4:]
    width = x_ref.shape[1]
    for i, rows in enumerate(sources):
        packed = lax.dot_general(place, rows, TN, preferred_element_type=F32).astype(BF16)
        for j in range(4):
            outs[j][:, i * width : (i + 1) * width] = packed[j * SLOT : (j + 1) * SLOT]


def hidden(rows, wg, wu):
    both = jnp.dot(rows, jnp.concatenate([wg, wu], axis=1), preferred_element_type=F32)
    return both[:, :128], both[:, 128:]


def fwd_kernel(c1, qr1, c2, pr2, wg, wu, wd, vg, vu, vd, keep1, send1, keep2, send2, rows):
    for i, ref in enumerate((c1, qr1, c2, pr2)):
        rows[64 * i : 64 * (i + 1), :] = ref[...]
    inner = []
    for g_ref, u_ref in ((wg, wu), (vg, vu)):
        gate, up = hidden(rows[...], g_ref[...], u_ref[...])
        inner.append((gate * jax.nn.sigmoid(gate) * up).astype(BF16))
    inner = jnp.concatenate(inner, axis=1)
    width = rows.shape[1]
    step = 512
    for at in range(0, width, step):
        cols = slice(at, at + step)
        down = jnp.concatenate([wd[:, cols], vd[:, cols]], axis=0)
        part = jnp.dot(inner, down, preferred_element_type=F32)
        keep1[:, cols] = part[0:64]
        send1[:, cols] = part[64:128].astype(BF16)
        keep2[:, cols] = part[128:192]
        send2[:, cols] = part[192:256].astype(BF16)


def bwd_kernel(c1, qr1, c2, pr2, wg, wu, wd, vg, vu, vd, keep1, send1, keep2, send2, rows, cots):
    width = rows.shape[1]
    for i, ref in enumerate((c1, qr1, c2, pr2)):
        rows[64 * i : 64 * (i + 1), :] = ref[:, :width]
        cots[64 * i : 64 * (i + 1), :] = ref[:, width:]
    back = []
    products = None
    for g_ref, u_ref, d_ref in ((wg, wu, wd), (vg, vu, vd)):
        gate, up = hidden(rows[...], g_ref[...], u_ref[...])
        d_inner = lax.dot_general(cots[...], d_ref[...], NT, preferred_element_type=F32)
        sig = jax.nn.sigmoid(gate)
        silu = gate * sig
        inner = (silu * up).astype(BF16).astype(F32)
        d_gate = (d_inner * up * sig * (1.0 + gate * (1.0 - sig))).astype(BF16)
        d_up = (d_inner * silu).astype(BF16)
        back.append(jnp.concatenate([d_gate, d_up], axis=1))
        product = inner * d_inner
        products = product if products is None else products + product
    count = products.shape[0]
    high = products.astype(BF16)
    low = (products - high.astype(F32)).astype(BF16)
    ones = jnp.ones((16, 128), BF16)
    grads = lax.dot_general(ones, high, NT, preferred_element_type=F32)
    grads = grads + lax.dot_general(ones, low, NT, preferred_element_type=F32)
    row = lax.broadcasted_iota(jnp.int32, (count, count), 0)
    col = lax.broadcasted_iota(jnp.int32, (count, count), 1)
    held = (row // SLOT == col // SLOT) & (row % SLOT == SLOT - 2)
    spread = jnp.where(held, grads[0:1, :], 0.0).astype(BF16)
    at_row = lax.broadcasted_iota(jnp.int32, (count, 128), 0)
    at_col = lax.broadcasted_iota(jnp.int32, (count, 128), 1)
    pick = (at_row % SLOT == at_col).astype(F32).astype(BF16)
    grad_rows = jnp.dot(spread, pick, preferred_element_type=F32)
    step = 512
    for at in range(0, width, step):
        cols = slice(at, at + step)
        part = None
        for grad, g_ref, u_ref in ((back[0], wg, wu), (back[1], vg, vu)):
            weight = jnp.concatenate([g_ref[cols, :], u_ref[cols, :]], axis=1)
            term = lax.dot_general(grad, weight, NT, preferred_element_type=F32)
            part = term if part is None else part + term
        if at == 0:
            part = jnp.concatenate([part[:, :128] + grad_rows, part[:, 128:]], axis=1)
        keep1[:, cols] = part[0:64]
        send1[:, cols] = part[64:128].astype(BF16)
        keep2[:, cols] = part[128:192]
        send2[:, cols] = part[192:256].astype(BF16)


def mixed_rows(masks, weight_ref, parts):
    weights = weight_ref[...]
    spread = jnp.where(masks[0][0], weights[:, 0:1], 0.0) + jnp.where(
        masks[1][0], weights[:, 1:2], 0.0
    )
    high = spread.astype(BF16)
    rest = spread - high.astype(F32)
    middle = rest.astype(BF16)
    low = (rest - middle.astype(F32)).astype(BF16)
    total = None
    for j, part in enumerate(parts):
        at = slice(j * SLOT, (j + 1) * SLOT)
        for piece in (high, middle, low):
            term = jnp.dot(piece[:, at], part, preferred_element_type=F32)
            total = term if total is None else total + term
    return total


def fwd_out_kernel(info_ref, x_ref, route_ref, weight_ref, own, a, b, c, out_ref):
    masks = slot_masks(info_ref, route_ref)
    parts = [own[...], a[...], b[...], c[...]]
    mixed = mixed_rows(masks, weight_ref, parts)
    out_ref[...] = (x_ref[...].astype(F32) + mixed).astype(BF16)


def bwd_out_kernel(
    info_ref, x_ref, route_ref, weight_ref, cot_ref, gain_ref, own, a, b, c, out_ref, grad_ref
):
    masks = slot_masks(info_ref, route_ref)
    parts = [own[...], a[...], b[...], c[...]]
    d_normed = mixed_rows(masks, weight_ref, parts)
    unit, scale = normalized(x_ref[...], gain_ref[...])
    q_term = d_normed * gain_ref[...]
    mean = jnp.mean(q_term * unit, axis=-1, keepdims=True)
    d_input = cot_ref[...].astype(F32) + scale * (q_term - unit * mean)
    out_ref[...] = d_input.astype(BF16)
    tokens = x_ref.shape[0]
    lanes = lax.broadcasted_iota(jnp.int32, (tokens, 128), 1)
    grads = []
    for _, rel, rank in masks:
        held = jnp.zeros((tokens, 128), F32)
        for j, part in enumerate(parts):
            row = part[:, :128].astype(F32)[SLOT - 2 : SLOT - 1, :]
            held = held + jnp.where(rel == j, row, 0.0)
        grads.append(jnp.sum(jnp.where(lanes == rank, held, 0.0), axis=1, keepdims=True))
    pair = lax.broadcasted_iota(jnp.int32, (tokens, 2), 1)
    grad_ref[...] = jnp.where(pair == 0, grads[0], grads[1]).astype(BF16)


def spread_rows(own, a, b, c):
    got_a, got_b, got_c = hop(a, HOP_A), hop(b, HOP_B), hop(c, HOP_C)
    half1 = jnp.concatenate([own, got_a], axis=0)
    half2 = jnp.concatenate([got_b, got_c], axis=0)
    p1 = hop(half1, HOP_X1)
    q2 = hop(half2, HOP_X3)
    c1 = jnp.concatenate([half1, p1], axis=0)
    c2 = jnp.concatenate([half2, q2], axis=0)
    return c1, hop(c1, HOP_X3), c2, hop(c2, HOP_X1)


def return_rows(keep1, send1, keep2, send2):
    sum1 = keep1 + hop(send1, HOP_X3).astype(F32)
    sum2 = keep2 + hop(send2, HOP_X1).astype(F32)
    full1 = sum1[:32] + hop(sum1[32:].astype(BF16), HOP_X1).astype(F32)
    full2 = sum2[:32] + hop(sum2[32:].astype(BF16), HOP_X3).astype(F32)
    full1 = full1.astype(BF16)
    full2 = full2.astype(BF16)
    back_a = hop(full1[SLOT:], HOP_A)
    back_b = hop(full2[:SLOT], HOP_B_BACK)
    back_c = hop(full2[SLOT:], HOP_C)
    return full1[:SLOT], back_a, back_b, back_c


def body(
    act_fwd,
    route_fwd,
    weight_fwd,
    act_bwd,
    route_bwd,
    weight_bwd,
    cot_bwd,
    norm_gain,
    w_gate,
    w_up,
    w_down,
):
    tokens, width = act_fwd.shape[1:]
    index = lax.axis_index("expert")
    z = index // GRID_X
    info = jnp.stack([z // 2, z % 2]).astype(jnp.int32)
    wg, wu, wd = w_gate[0, 0], w_up[0, 0], w_down[0, 0]
    wide = [((SLOT, width), BF16)] * 4
    sent_a = kernel_call(pack_kernel, wide, 3)(info, act_fwd[0], route_fwd[0], norm_gain)
    wide = [((SLOT, 2 * width), BF16)] * 4
    sent_b = kernel_call(pack_kernel, wide, 4)(
        info, act_bwd[0], route_bwd[0], norm_gain, cot_bwd[0]
    )
    rows_a = spread_rows(*sent_a)
    weights = (wg, wu, wd, hop(wg, HOP_W), hop(wu, HOP_W), hop(wd, HOP_W))
    rows_b = spread_rows(*sent_b)
    outs = [((64, width), F32), ((64, width), BF16)] * 2
    scratch = pltpu.VMEM((256, width), BF16)
    parts_a = kernel_call(fwd_kernel, outs, 10, [scratch], info=False)(*rows_a, *weights)
    parts_b = kernel_call(bwd_kernel, outs, 10, [scratch] * 2, info=False)(*rows_b, *weights)
    back_a = return_rows(*parts_a)
    (layer_out,) = kernel_call(fwd_out_kernel, [((tokens, width), BF16)], 7)(
        info, act_fwd[0], route_fwd[0], weight_fwd[0], *back_a
    )
    act_next = shifted(layer_out, "section", 1)
    back_b = return_rows(*parts_b)
    d_input, gate_grad = kernel_call(
        bwd_out_kernel, [((tokens, width), BF16), ((tokens, 2), BF16)], 9
    )(info, act_bwd[0], route_bwd[0], weight_bwd[0], cot_bwd[0], norm_gain, *back_b)
    cot_next = shifted(d_input, "section", -1)
    return (act_next[None], cot_next[None], gate_grad[None])


def solution(mesh):
    return jax.shard_map(
        body,
        mesh=mesh,
        in_specs=(
            P("section", "expert", None),
            P("section", "expert", None),
            P("section", "expert", None),
            P("section", "expert", None),
            P("section", "expert", None),
            P("section", "expert", None),
            P("section", "expert", None),
            P("section", None),
            P("section", "expert", None, None),
            P("section", "expert", None, None),
            P("section", "expert", None, None),
        ),
        out_specs=(
            P("section", "expert", None),
            P("section", "expert", None),
            P("section", "expert", None),
        ),
        check_vma=False,
    )
```

```python
import jax
import jax.numpy as jnp
from jax import lax
from jax.experimental import pallas as pl
from jax.experimental.pallas import tpu as pltpu
from jax.sharding import PartitionSpec as P

EXPERTS = 4
GRID_X = 4
GRID_Z = 8
SLOT = 16
F32 = jnp.float32
BF16 = jnp.bfloat16
NT = (((1,), (1,)), ((), ()))
TN = (((0,), (0,)), ((), ()))


def expert_pairs(move):
    pairs = []
    for z in range(GRID_Z):
        for x in range(GRID_X):
            to_z, to_x = move(z, x)
            pairs.append((z * GRID_X + x, to_z % GRID_Z * GRID_X + to_x))
    return pairs


def signed(z, even, odd):
    return z + (odd if z % 2 else even)


HOP_W = expert_pairs(lambda z, x: (z ^ 1, x))
HOP_A = expert_pairs(lambda z, x: (signed(z, -1, 1), x))
HOP_B = expert_pairs(lambda z, x: (signed(z, 2, -2), x))
HOP_B_BACK = expert_pairs(lambda z, x: (signed(z, -2, 2), x))
HOP_C = expert_pairs(lambda z, x: (signed(z, -3, 3), x))
HOP_X1 = expert_pairs(lambda z, x: (z, x ^ 1))
HOP_X3 = expert_pairs(lambda z, x: (z, x ^ 3))


def hop(value, pairs):
    return lax.ppermute(value, "expert", pairs)


def shifted(value, axis, by):
    devices = lax.axis_size(axis)
    pairs = [(i, i + by) for i in range(devices) if 0 <= i + by < devices]
    return lax.ppermute(value, axis, pairs)


def kernel_call(kernel, outs, n_in, scratch=(), info=True, limit=32):
    smem = pl.BlockSpec(memory_space=pltpu.SMEM)
    vmem = pl.BlockSpec(memory_space=pltpu.VMEM)
    return pl.pallas_call(
        kernel,
        out_shape=[jax.ShapeDtypeStruct(s, d) for s, d in outs],
        in_specs=[smem] * info + [vmem] * n_in,
        out_specs=[vmem] * len(outs),
        scratch_shapes=list(scratch),
        compiler_params=pltpu.CompilerParams(vmem_limit_bytes=limit * 1024 * 1024),
    )


def slot_masks(info_ref, route_ref):
    tokens = route_ref.shape[0]
    own, odd = info_ref[0], info_ref[1]
    lanes = lax.broadcasted_iota(jnp.int32, (tokens, 128), 1)
    route = route_ref[...]
    named = [(route[:, k : k + 1] == lanes).astype(F32) for k in range(2)]
    row = lax.broadcasted_iota(jnp.int32, (tokens, tokens), 0)
    col = lax.broadcasted_iota(jnp.int32, (tokens, tokens), 1)
    earlier = (col < row).astype(BF16)
    counts = jnp.dot(earlier, (named[0] + named[1]).astype(BF16), preferred_element_type=F32)
    out = []
    for k in range(2):
        rank = jnp.sum(named[k] * counts, axis=1, keepdims=True).astype(jnp.int32)
        away = (route[:, k : k + 1] - own) & 3
        side = jnp.where((away == 3) == (odd == 0), 1, 2)
        rel = jnp.where(away == 0, 0, jnp.where(away == 2, 3, side))
        slots = lax.broadcasted_iota(jnp.int32, (tokens, 4 * SLOT), 1)
        out.append((slots == rel * SLOT + rank, rel, rank))
    return out


def normalized(x):
    values = x.astype(F32)
    scale = lax.rsqrt(jnp.mean(values * values, axis=-1, keepdims=True) + 1e-06)
    return values * scale, scale


def pack_kernel(info_ref, xa_ref, ra_ref, xb_ref, rb_ref, cot_ref, gain_ref, *outs):
    width = xa_ref.shape[1]
    places = []
    for route_ref in (ra_ref, rb_ref):
        masks = slot_masks(info_ref, route_ref)
        places.append((masks[0][0] | masks[1][0]).astype(F32).astype(BF16))
    gain = gain_ref[...]
    normed_a = (normalized(xa_ref[...])[0] * gain).astype(BF16)
    normed_b = (normalized(xb_ref[...])[0] * gain).astype(BF16)
    sources = ((places[0], normed_a), (places[1], normed_b), (places[1], cot_ref[...]))
    for i, (place, rows) in enumerate(sources):
        packed = lax.dot_general(place, rows, TN, preferred_element_type=F32).astype(BF16)
        for j in range(4):
            outs[j][:, i * width : (i + 1) * width] = packed[j * SLOT : (j + 1) * SLOT]


def merge_kernel(wg, wu, wd, out, sems):
    width, units = wg.shape
    copies = [
        pltpu.make_async_copy(wg, out.at[pl.ds(0, width)], sems.at[0]),
        pltpu.make_async_copy(wu, out.at[pl.ds(width, width)], sems.at[1]),
    ]
    for i in range(width // units):
        to = out.at[pl.ds(2 * width + i * units, units)]
        copies.append(pltpu.make_async_copy(wd.at[:, pl.ds(i * units, units)], to, sems.at[2 + i]))
    for copy in copies:
        copy.start()
    for copy in copies:
        copy.wait()


def hidden(rows, wg, wu):
    both = jnp.dot(rows, jnp.concatenate([wg, wu], axis=1), preferred_element_type=F32)
    return both[:, :128], both[:, 128:]


def down_columns(merged, at, count):
    width = merged.shape[0] // 3
    starts = range(2 * width + at, 2 * width + at + count, 128)
    return jnp.concatenate([merged[start : start + 128, :] for start in starts], axis=1)


def gather_rows(refs, at, width, scratch):
    cols = slice(at, at + width)
    places = ((0, 64), (128, 192), (32, 160), (96, 224))
    for ref, (one, two) in zip(refs, places):
        scratch[one : one + 32, :] = ref[0:32, cols]
        scratch[two : two + 32, :] = ref[32:64, cols]


def fwd_kernel(c1, qr1, c2, pr2, wg, wu, wd, other, keep, send, rows):
    width = rows.shape[1]
    gather_rows((c1, qr1, c2, pr2), 0, width, rows)
    inner = []
    for weights in ((wg[...], wu[...]), (other[0:width, :], other[width : 2 * width, :])):
        gate, up = hidden(rows[...], *weights)
        inner.append((gate * jax.nn.sigmoid(gate) * up).astype(BF16))
    inner = jnp.concatenate(inner, axis=1)
    step = 512
    for at in range(0, width, step):
        cols = slice(at, at + step)
        down = jnp.concatenate([wd[:, cols], down_columns(other, at, step)], axis=0)
        part = jnp.dot(inner, down, preferred_element_type=F32)
        keep[:, cols] = part[0:128]
        send[:, cols] = part[128:256].astype(BF16)


def bwd_kernel(c1, qr1, c2, pr2, wg, wu, wd, other, keep, send, rows, cots):
    width = rows.shape[1]
    gather_rows((c1, qr1, c2, pr2), width, width, rows)
    gather_rows((c1, qr1, c2, pr2), 2 * width, width, cots)
    back = []
    products = None
    sources = (
        (wg[...], wu[...], wd[...]),
        (other[0:width, :], other[width : 2 * width, :], down_columns(other, 0, width)),
    )
    for gate_w, up_w, down_w in sources:
        gate, up = hidden(rows[...], gate_w, up_w)
        d_inner = lax.dot_general(cots[...], down_w, NT, preferred_element_type=F32)
        sig = jax.nn.sigmoid(gate)
        silu = gate * sig
        inner = (silu * up).astype(BF16).astype(F32)
        d_gate = (d_inner * up * sig * (1.0 + gate * (1.0 - sig))).astype(BF16)
        d_up = (d_inner * silu).astype(BF16)
        back.append(jnp.concatenate([d_gate, d_up], axis=1))
        product = inner * d_inner
        products = product if products is None else products + product
    count = products.shape[0]
    high = products.astype(BF16)
    low = (products - high.astype(F32)).astype(BF16)
    ones = jnp.ones((16, 128), BF16)
    grads = lax.dot_general(ones, high, NT, preferred_element_type=F32)
    grads = grads + lax.dot_general(ones, low, NT, preferred_element_type=F32)
    row = lax.broadcasted_iota(jnp.int32, (count, count), 0)
    col = lax.broadcasted_iota(jnp.int32, (count, count), 1)
    held = (row // SLOT == col // SLOT) & (row % SLOT == SLOT - 2)
    spread = jnp.where(held, grads[0:1, :], 0.0).astype(BF16)
    at_row = lax.broadcasted_iota(jnp.int32, (count, 128), 0)
    at_col = lax.broadcasted_iota(jnp.int32, (count, 128), 1)
    pick = (at_row % SLOT == at_col).astype(F32).astype(BF16)
    grad_rows = jnp.dot(spread, pick, preferred_element_type=F32)
    step = 512
    for at in range(0, width, step):
        cols = slice(at, at + step)
        there = slice(width + at, width + at + step)
        weights = (
            jnp.concatenate([wg[cols, :], wu[cols, :]], axis=1),
            jnp.concatenate([other[cols, :], other[there, :]], axis=1),
        )
        part = None
        for grad, weight in zip(back, weights):
            term = lax.dot_general(grad, weight, NT, preferred_element_type=F32)
            part = term if part is None else part + term
        if at == 0:
            part = jnp.concatenate([part[:, :128] + grad_rows, part[:, 128:]], axis=1)
        keep[0:64, cols] = part[0:64]
        send[0:64, cols] = part[64:128].astype(BF16)
        keep[64:128, cols] = part[128:192]
        send[64:128, cols] = part[192:256].astype(BF16)


def mixed_rows(masks, weight_ref, parts):
    weights = weight_ref[...]
    spread = jnp.where(masks[0][0], weights[:, 0:1], 0.0) + jnp.where(
        masks[1][0], weights[:, 1:2], 0.0
    )
    high = spread.astype(BF16)
    rest = spread - high.astype(F32)
    middle = rest.astype(BF16)
    low = (rest - middle.astype(F32)).astype(BF16)
    total = None
    for j, part in enumerate(parts):
        at = slice(j * SLOT, (j + 1) * SLOT)
        for piece in (high, middle, low):
            term = jnp.dot(piece[:, at], part, preferred_element_type=F32)
            total = term if total is None else total + term
    return total


def fwd_out_kernel(info_ref, x_ref, route_ref, weight_ref, own, a, b, c, out_ref):
    masks = slot_masks(info_ref, route_ref)
    parts = [own[...], a[...], b[...], c[...]]
    mixed = mixed_rows(masks, weight_ref, parts)
    out_ref[...] = (x_ref[...].astype(F32) + mixed).astype(BF16)


def bwd_out_kernel(
    info_ref, x_ref, route_ref, weight_ref, cot_ref, gain_ref, own, a, b, c, out_ref, grad_ref
):
    masks = slot_masks(info_ref, route_ref)
    parts = [own[...], a[...], b[...], c[...]]
    d_normed = mixed_rows(masks, weight_ref, parts)
    unit, scale = normalized(x_ref[...])
    q_term = d_normed * gain_ref[...]
    mean = jnp.mean(q_term * unit, axis=-1, keepdims=True)
    d_input = cot_ref[...].astype(F32) + scale * (q_term - unit * mean)
    out_ref[...] = d_input.astype(BF16)
    tokens = x_ref.shape[0]
    lanes = lax.broadcasted_iota(jnp.int32, (tokens, 128), 1)
    grads = []
    for _, rel, rank in masks:
        held = jnp.zeros((tokens, 128), F32)
        for j, part in enumerate(parts):
            row = part[:, :128].astype(F32)[SLOT - 2 : SLOT - 1, :]
            held = held + jnp.where(rel == j, row, 0.0)
        grads.append(jnp.sum(jnp.where(lanes == rank, held, 0.0), axis=1, keepdims=True))
    pair = lax.broadcasted_iota(jnp.int32, (tokens, 2), 1)
    grad_ref[...] = jnp.where(pair == 0, grads[0], grads[1]).astype(BF16)


def spread_rows(own, a, b, c):
    got_a, got_b, got_c = hop(a, HOP_A), hop(b, HOP_B), hop(c, HOP_C)
    half1 = jnp.concatenate([own, got_a], axis=0)
    half2 = jnp.concatenate([got_b, got_c], axis=0)
    p1 = hop(half1, HOP_X1)
    q2 = hop(half2, HOP_X3)
    c1 = jnp.concatenate([half1, p1], axis=0)
    c2 = jnp.concatenate([half2, q2], axis=0)
    return c1, hop(c1, HOP_X3), c2, hop(c2, HOP_X1)


def return_rows(keep, send, first, second):
    total = keep + hop(send, first).astype(F32)
    whole = total[:64] + hop(total[64:].astype(BF16), second).astype(F32)
    whole = whole.astype(BF16)
    own, a, b, c = (whole[j * SLOT : (j + 1) * SLOT] for j in range(4))
    return own, hop(a, HOP_A), hop(b, HOP_B_BACK), hop(c, HOP_C)


def body(
    act_fwd,
    route_fwd,
    weight_fwd,
    act_bwd,
    route_bwd,
    weight_bwd,
    cot_bwd,
    norm_gain,
    w_gate,
    w_up,
    w_down,
):
    tokens, width = act_fwd.shape[1:]
    index = lax.axis_index("expert")
    z = index // GRID_X
    info = jnp.stack([z // 2, z % 2]).astype(jnp.int32)
    weights = (w_gate[0, 0], w_up[0, 0], w_down[0, 0])
    units = w_down.shape[2]
    hbm = pl.BlockSpec(memory_space=pl.ANY)
    merged = pl.pallas_call(
        merge_kernel,
        out_shape=jax.ShapeDtypeStruct((3 * width, units), BF16),
        in_specs=[hbm] * 3,
        out_specs=hbm,
        scratch_shapes=[pltpu.SemaphoreType.DMA((2 + width // units,))],
    )(*weights)
    other = hop(merged, HOP_W)
    wide = [((SLOT, 3 * width), BF16)] * 4
    sent = kernel_call(pack_kernel, wide, 6)(
        info, act_fwd[0], route_fwd[0], act_bwd[0], route_bwd[0], cot_bwd[0], norm_gain
    )
    rows = spread_rows(*sent)
    outs = [((128, width), F32), ((128, width), BF16)]
    scratch = pltpu.VMEM((256, width), BF16)
    part_a = kernel_call(fwd_kernel, outs, 8, [scratch], info=False)(*rows, *weights, other)
    part_b = kernel_call(bwd_kernel, outs, 8, [scratch] * 2, info=False)(*rows, *weights, other)
    back_a = return_rows(*part_a, HOP_X3, HOP_X1)
    back_b = return_rows(*part_b, HOP_X1, HOP_X3)
    (layer_out,) = kernel_call(fwd_out_kernel, [((tokens, width), BF16)], 7)(
        info, act_fwd[0], route_fwd[0], weight_fwd[0], *back_a
    )
    act_next = shifted(layer_out, "section", 1)
    d_input, gate_grad = kernel_call(
        bwd_out_kernel, [((tokens, width), BF16), ((tokens, 2), BF16)], 9
    )(info, act_bwd[0], route_bwd[0], weight_bwd[0], cot_bwd[0], norm_gain, *back_b)
    cot_next = shifted(d_input, "section", -1)
    return (act_next[None], cot_next[None], gate_grad[None])


def solution(mesh):
    return jax.shard_map(
        body,
        mesh=mesh,
        in_specs=(
            P("section", "expert", None),
            P("section", "expert", None),
            P("section", "expert", None),
            P("section", "expert", None),
            P("section", "expert", None),
            P("section", "expert", None),
            P("section", "expert", None),
            P("section", None),
            P("section", "expert", None, None),
            P("section", "expert", None, None),
            P("section", "expert", None, None),
        ),
        out_specs=(
            P("section", "expert", None),
            P("section", "expert", None),
            P("section", "expert", None),
        ),
        check_vma=False,
    )
```

```python
import jax
import jax.numpy as jnp
from jax import lax
from jax.experimental import pallas as pl
from jax.experimental.pallas import tpu as pltpu
from jax.sharding import PartitionSpec as P

EXPERTS = 4
GRID_X = 4
GRID_Z = 8
SLOT = 16
F32 = jnp.float32
BF16 = jnp.bfloat16
NT = (((1,), (1,)), ((), ()))
TN = (((0,), (0,)), ((), ()))


def expert_pairs(move):
    pairs = []
    for z in range(GRID_Z):
        for x in range(GRID_X):
            to_z, to_x = move(z, x)
            pairs.append((z * GRID_X + x, to_z % GRID_Z * GRID_X + to_x))
    return pairs


def signed(z, even, odd):
    return z + (odd if z % 2 else even)


HOP_W = expert_pairs(lambda z, x: (z ^ 1, x))
HOP_A = expert_pairs(lambda z, x: (signed(z, -1, 1), x))
HOP_B = expert_pairs(lambda z, x: (signed(z, 2, -2), x))
HOP_B_BACK = expert_pairs(lambda z, x: (signed(z, -2, 2), x))
HOP_C = expert_pairs(lambda z, x: (signed(z, -3, 3), x))
HOP_X1 = expert_pairs(lambda z, x: (z, x ^ 1))
HOP_X3 = expert_pairs(lambda z, x: (z, x ^ 3))


def hop(value, pairs):
    return lax.ppermute(value, "expert", pairs)


def shifted(value, axis, by):
    devices = lax.axis_size(axis)
    pairs = [(i, i + by) for i in range(devices) if 0 <= i + by < devices]
    return lax.ppermute(value, axis, pairs)


def kernel_call(kernel, outs, n_in, scratch=(), info=True, limit=32):
    smem = pl.BlockSpec(memory_space=pltpu.SMEM)
    vmem = pl.BlockSpec(memory_space=pltpu.VMEM)
    return pl.pallas_call(
        kernel,
        out_shape=[jax.ShapeDtypeStruct(s, d) for s, d in outs],
        in_specs=[smem] * info + [vmem] * n_in,
        out_specs=[vmem] * len(outs),
        scratch_shapes=list(scratch),
        compiler_params=pltpu.CompilerParams(vmem_limit_bytes=limit * 1024 * 1024),
    )


def slot_masks(info_ref, route_ref):
    tokens = route_ref.shape[0]
    own, odd = info_ref[0], info_ref[1]
    lanes = lax.broadcasted_iota(jnp.int32, (tokens, 128), 1)
    route = route_ref[...]
    named = [(route[:, k : k + 1] == lanes).astype(F32) for k in range(2)]
    row = lax.broadcasted_iota(jnp.int32, (tokens, tokens), 0)
    col = lax.broadcasted_iota(jnp.int32, (tokens, tokens), 1)
    earlier = (col < row).astype(BF16)
    counts = jnp.dot(earlier, (named[0] + named[1]).astype(BF16), preferred_element_type=F32)
    out = []
    for k in range(2):
        rank = jnp.sum(named[k] * counts, axis=1, keepdims=True).astype(jnp.int32)
        away = (route[:, k : k + 1] - own) & 3
        side = jnp.where((away == 3) == (odd == 0), 1, 2)
        rel = jnp.where(away == 0, 0, jnp.where(away == 2, 3, side))
        slots = lax.broadcasted_iota(jnp.int32, (tokens, 4 * SLOT), 1)
        out.append((slots == rel * SLOT + rank, rel, rank))
    return out


def normalized(x):
    values = x.astype(F32)
    scale = lax.rsqrt(jnp.mean(values * values, axis=-1, keepdims=True) + 1e-06)
    return values * scale, scale


def pack_kernel(info_ref, xa_ref, ra_ref, xb_ref, rb_ref, cot_ref, gain_ref, *outs):
    width = xa_ref.shape[1]
    places = []
    for route_ref in (ra_ref, rb_ref):
        masks = slot_masks(info_ref, route_ref)
        places.append((masks[0][0] | masks[1][0]).astype(F32).astype(BF16))
    gain = gain_ref[...]
    normed_a = (normalized(xa_ref[...])[0] * gain).astype(BF16)
    normed_b = (normalized(xb_ref[...])[0] * gain).astype(BF16)
    sources = ((places[0], normed_a), (places[1], normed_b), (places[1], cot_ref[...]))
    for i, (place, rows) in enumerate(sources):
        packed = lax.dot_general(place, rows, TN, preferred_element_type=F32).astype(BF16)
        for j in range(4):
            outs[j][:, i * width : (i + 1) * width] = packed[j * SLOT : (j + 1) * SLOT]


def merge_kernel(wg, wu, wd, out):
    width, units = wg.shape
    out[0:width, :] = wg[...]
    out[width : 2 * width, :] = wu[...]
    for at in range(0, width, units):
        out[2 * width + at : 2 * width + at + units, :] = wd[:, at : at + units]


def hidden(rows, wg, wu):
    both = jnp.dot(rows, jnp.concatenate([wg, wu], axis=1), preferred_element_type=F32)
    return both[:, :128], both[:, 128:]


def down_columns(merged, at, count):
    width = merged.shape[0] // 3
    starts = range(2 * width + at, 2 * width + at + count, 128)
    return jnp.concatenate([merged[start : start + 128, :] for start in starts], axis=1)


def gather_rows(refs, at, width, scratch):
    for i, ref in enumerate(refs):
        scratch[64 * i : 64 * (i + 1), :] = ref[:, at : at + width]


def store_parts(part, cols, keep1, send1, keep2, send2):
    keep1[:, cols] = part[0:64]
    send1[:, cols] = part[64:128].astype(BF16)
    keep2[:, cols] = part[128:192]
    send2[:, cols] = part[192:256].astype(BF16)


def fwd_kernel(c1, qr1, c2, pr2, wg, wu, wd, other, keep1, send1, keep2, send2, rows):
    width = rows.shape[1]
    gather_rows((c1, qr1, c2, pr2), 0, width, rows)
    inner = []
    for weights in ((wg[...], wu[...]), (other[0:width, :], other[width : 2 * width, :])):
        gate, up = hidden(rows[...], *weights)
        inner.append((gate * jax.nn.sigmoid(gate) * up).astype(BF16))
    inner = jnp.concatenate(inner, axis=1)
    step = 512
    for at in range(0, width, step):
        cols = slice(at, at + step)
        down = jnp.concatenate([wd[:, cols], down_columns(other, at, step)], axis=0)
        part = jnp.dot(inner, down, preferred_element_type=F32)
        store_parts(part, cols, keep1, send1, keep2, send2)


def bwd_kernel(
    c1, qr1, c2, pr2, wg, wu, wd, other, _, keep1, send1, keep2, send2, rows, cots
):
    width = rows.shape[1]
    gather_rows((c1, qr1, c2, pr2), width, width, rows)
    gather_rows((c1, qr1, c2, pr2), 2 * width, width, cots)
    back = []
    products = None
    sources = (
        (wg[...], wu[...], wd[...]),
        (other[0:width, :], other[width : 2 * width, :], down_columns(other, 0, width)),
    )
    for gate_w, up_w, down_w in sources:
        gate, up = hidden(rows[...], gate_w, up_w)
        d_inner = lax.dot_general(cots[...], down_w, NT, preferred_element_type=F32)
        sig = jax.nn.sigmoid(gate)
        silu = gate * sig
        inner = (silu * up).astype(BF16).astype(F32)
        d_gate = (d_inner * up * sig * (1.0 + gate * (1.0 - sig))).astype(BF16)
        d_up = (d_inner * silu).astype(BF16)
        back.append(jnp.concatenate([d_gate, d_up], axis=1))
        product = inner * d_inner
        products = product if products is None else products + product
    count = products.shape[0]
    high = products.astype(BF16)
    low = (products - high.astype(F32)).astype(BF16)
    ones = jnp.ones((16, 128), BF16)
    grads = lax.dot_general(ones, high, NT, preferred_element_type=F32)
    grads = grads + lax.dot_general(ones, low, NT, preferred_element_type=F32)
    row = lax.broadcasted_iota(jnp.int32, (count, count), 0)
    col = lax.broadcasted_iota(jnp.int32, (count, count), 1)
    held = (row // SLOT == col // SLOT) & (row % SLOT == SLOT - 2)
    spread = jnp.where(held, grads[0:1, :], 0.0).astype(BF16)
    at_row = lax.broadcasted_iota(jnp.int32, (count, 128), 0)
    at_col = lax.broadcasted_iota(jnp.int32, (count, 128), 1)
    pick = (at_row % SLOT == at_col).astype(F32).astype(BF16)
    grad_rows = jnp.dot(spread, pick, preferred_element_type=F32)
    step = 512
    for at in range(0, width, step):
        cols = slice(at, at + step)
        there = slice(width + at, width + at + step)
        weights = (
            jnp.concatenate([wg[cols, :], wu[cols, :]], axis=1),
            jnp.concatenate([other[cols, :], other[there, :]], axis=1),
        )
        part = None
        for grad, weight in zip(back, weights):
            term = lax.dot_general(grad, weight, NT, preferred_element_type=F32)
            part = term if part is None else part + term
        if at == 0:
            part = jnp.concatenate([part[:, :128] + grad_rows, part[:, 128:]], axis=1)
        store_parts(part, cols, keep1, send1, keep2, send2)


def mixed_rows(masks, weight_ref, parts):
    weights = weight_ref[...]
    spread = jnp.where(masks[0][0], weights[:, 0:1], 0.0) + jnp.where(
        masks[1][0], weights[:, 1:2], 0.0
    )
    high = spread.astype(BF16)
    rest = spread - high.astype(F32)
    middle = rest.astype(BF16)
    low = (rest - middle.astype(F32)).astype(BF16)
    total = None
    for j, part in enumerate(parts):
        at = slice(j * SLOT, (j + 1) * SLOT)
        for piece in (high, middle, low):
            term = jnp.dot(piece[:, at], part, preferred_element_type=F32)
            total = term if total is None else total + term
    return total


def fwd_out_kernel(info_ref, x_ref, route_ref, weight_ref, own, a, b, c, out_ref):
    masks = slot_masks(info_ref, route_ref)
    parts = [own[...], a[...], b[...], c[...]]
    mixed = mixed_rows(masks, weight_ref, parts)
    out_ref[...] = (x_ref[...].astype(F32) + mixed).astype(BF16)


def bwd_out_kernel(
    info_ref, x_ref, route_ref, weight_ref, cot_ref, gain_ref, own, a, b, c, out_ref, grad_ref
):
    masks = slot_masks(info_ref, route_ref)
    parts = [own[...], a[...], b[...], c[...]]
    d_normed = mixed_rows(masks, weight_ref, parts)
    unit, scale = normalized(x_ref[...])
    q_term = d_normed * gain_ref[...]
    mean = jnp.mean(q_term * unit, axis=-1, keepdims=True)
    d_input = cot_ref[...].astype(F32) + scale * (q_term - unit * mean)
    out_ref[...] = d_input.astype(BF16)
    tokens = x_ref.shape[0]
    lanes = lax.broadcasted_iota(jnp.int32, (tokens, 128), 1)
    grads = []
    for _, rel, rank in masks:
        held = jnp.zeros((tokens, 128), F32)
        for j, part in enumerate(parts):
            row = part[:, :128].astype(F32)[SLOT - 2 : SLOT - 1, :]
            held = held + jnp.where(rel == j, row, 0.0)
        grads.append(jnp.sum(jnp.where(lanes == rank, held, 0.0), axis=1, keepdims=True))
    pair = lax.broadcasted_iota(jnp.int32, (tokens, 2), 1)
    grad_ref[...] = jnp.where(pair == 0, grads[0], grads[1]).astype(BF16)


def spread_rows(own, a, b, c):
    got_a, got_b, got_c = hop(a, HOP_A), hop(b, HOP_B), hop(c, HOP_C)
    half1 = jnp.concatenate([own, got_a], axis=0)
    half2 = jnp.concatenate([got_b, got_c], axis=0)
    p1 = hop(half1, HOP_X1)
    q2 = hop(half2, HOP_X3)
    c1 = jnp.concatenate([half1, p1], axis=0)
    c2 = jnp.concatenate([half2, q2], axis=0)
    return c1, hop(c1, HOP_X3), c2, hop(c2, HOP_X1)


def return_rows(keep1, send1, keep2, send2):
    sum1 = keep1 + hop(send1, HOP_X3).astype(F32)
    sum2 = keep2 + hop(send2, HOP_X1).astype(F32)
    full1 = sum1[:32] + hop(sum1[32:].astype(BF16), HOP_X1).astype(F32)
    full2 = sum2[:32] + hop(sum2[32:].astype(BF16), HOP_X3).astype(F32)
    full1 = full1.astype(BF16)
    full2 = full2.astype(BF16)
    back_a = hop(full1[SLOT:], HOP_A)
    back_b = hop(full2[:SLOT], HOP_B_BACK)
    back_c = hop(full2[SLOT:], HOP_C)
    return full1[:SLOT], back_a, back_b, back_c


def body(
    act_fwd,
    route_fwd,
    weight_fwd,
    act_bwd,
    route_bwd,
    weight_bwd,
    cot_bwd,
    norm_gain,
    w_gate,
    w_up,
    w_down,
):
    tokens, width = act_fwd.shape[1:]
    index = lax.axis_index("expert")
    z = index // GRID_X
    info = jnp.stack([z // 2, z % 2]).astype(jnp.int32)
    weights = (w_gate[0, 0], w_up[0, 0], w_down[0, 0])
    units = w_down.shape[2]
    (merged,) = kernel_call(merge_kernel, [((3 * width, units), BF16)], 3, info=False)(*weights)
    other = hop(merged, HOP_W)
    wide = [((SLOT, 3 * width), BF16)] * 4
    sent = kernel_call(pack_kernel, wide, 6)(
        info, act_fwd[0], route_fwd[0], act_bwd[0], route_bwd[0], cot_bwd[0], norm_gain
    )
    rows = spread_rows(*sent)
    outs = [((64, width), F32), ((64, width), BF16)] * 2
    scratch = pltpu.VMEM((256, width), BF16)
    part_a = kernel_call(fwd_kernel, outs, 8, [scratch], info=False)(*rows, *weights, other)
    part_b = kernel_call(bwd_kernel, outs, 9, [scratch] * 2, info=False)(
        *rows, *weights, other, part_a[1]
    )
    back_a = return_rows(*part_a)
    back_b = return_rows(*part_b)
    (layer_out,) = kernel_call(fwd_out_kernel, [((tokens, width), BF16)], 7)(
        info, act_fwd[0], route_fwd[0], weight_fwd[0], *back_a
    )
    act_next = shifted(layer_out, "section", 1)
    d_input, gate_grad = kernel_call(
        bwd_out_kernel, [((tokens, width), BF16), ((tokens, 2), BF16)], 9
    )(info, act_bwd[0], route_bwd[0], weight_bwd[0], cot_bwd[0], norm_gain, *back_b)
    cot_next = shifted(d_input, "section", -1)
    return (act_next[None], cot_next[None], gate_grad[None])


def solution(mesh):
    return jax.shard_map(
        body,
        mesh=mesh,
        in_specs=(
            P("section", "expert", None),
            P("section", "expert", None),
            P("section", "expert", None),
            P("section", "expert", None),
            P("section", "expert", None),
            P("section", "expert", None),
            P("section", "expert", None),
            P("section", None),
            P("section", "expert", None, None),
            P("section", "expert", None, None),
            P("section", "expert", None, None),
        ),
        out_specs=(
            P("section", "expert", None),
            P("section", "expert", None),
            P("section", "expert", None),
        ),
        check_vma=False,
    )
```

```python
import jax
import jax.numpy as jnp
from jax import lax
from jax.experimental import pallas as pl
from jax.experimental.pallas import tpu as pltpu
from jax.sharding import PartitionSpec as P

EXPERTS = 4
GRID_X = 4
GRID_Z = 8
SLOT = 16
F32 = jnp.float32
BF16 = jnp.bfloat16
NT = (((1,), (1,)), ((), ()))
TN = (((0,), (0,)), ((), ()))


def expert_pairs(move):
    pairs = []
    for z in range(GRID_Z):
        for x in range(GRID_X):
            to_z, to_x = move(z, x)
            pairs.append((z * GRID_X + x, to_z % GRID_Z * GRID_X + to_x))
    return pairs


def signed(z, even, odd):
    return z + (odd if z % 2 else even)


HOP_W = expert_pairs(lambda z, x: (z ^ 1, x))
HOP_A = expert_pairs(lambda z, x: (signed(z, -1, 1), x))
HOP_B = expert_pairs(lambda z, x: (signed(z, 2, -2), x))
HOP_B_BACK = expert_pairs(lambda z, x: (signed(z, -2, 2), x))
HOP_C = expert_pairs(lambda z, x: (signed(z, -3, 3), x))
HOP_X1 = expert_pairs(lambda z, x: (z, x ^ 1))
HOP_X3 = expert_pairs(lambda z, x: (z, x ^ 3))


def hop(value, pairs):
    return lax.ppermute(value, "expert", pairs)


def shifted(value, axis, by):
    devices = lax.axis_size(axis)
    pairs = [(i, i + by) for i in range(devices) if 0 <= i + by < devices]
    return lax.ppermute(value, axis, pairs)


def kernel_call(kernel, outs, n_in, scratch=(), info=True, limit=32):
    smem = pl.BlockSpec(memory_space=pltpu.SMEM)
    vmem = pl.BlockSpec(memory_space=pltpu.VMEM)
    return pl.pallas_call(
        kernel,
        out_shape=[jax.ShapeDtypeStruct(s, d) for s, d in outs],
        in_specs=[smem] * info + [vmem] * n_in,
        out_specs=[vmem] * len(outs),
        scratch_shapes=list(scratch),
        compiler_params=pltpu.CompilerParams(vmem_limit_bytes=limit * 1024 * 1024),
    )


def slot_masks(info_ref, route_ref):
    tokens = route_ref.shape[0]
    own, odd = info_ref[0], info_ref[1]
    lanes = lax.broadcasted_iota(jnp.int32, (tokens, 128), 1)
    route = route_ref[...]
    named = [(route[:, k : k + 1] == lanes).astype(F32) for k in range(2)]
    row = lax.broadcasted_iota(jnp.int32, (tokens, tokens), 0)
    col = lax.broadcasted_iota(jnp.int32, (tokens, tokens), 1)
    earlier = (col < row).astype(BF16)
    counts = jnp.dot(earlier, (named[0] + named[1]).astype(BF16), preferred_element_type=F32)
    out = []
    for k in range(2):
        rank = jnp.sum(named[k] * counts, axis=1, keepdims=True).astype(jnp.int32)
        away = (route[:, k : k + 1] - own) & 3
        side = jnp.where((away == 3) == (odd == 0), 1, 2)
        rel = jnp.where(away == 0, 0, jnp.where(away == 2, 3, side))
        slots = lax.broadcasted_iota(jnp.int32, (tokens, 4 * SLOT), 1)
        out.append((slots == rel * SLOT + rank, rel, rank))
    return out


def normalized(x):
    values = x.astype(F32)
    scale = lax.rsqrt(jnp.mean(values * values, axis=-1, keepdims=True) + 1e-06)
    return values * scale, scale


def first_kernel(info_ref, ra_ref, rb_ref, xa, xb, cot, gain_in, wg, wu, wd, *rest):
    outs, (xa_ref, xb_ref, cot_ref, gain_ref, down, sems) = rest[:5], rest[5:]
    width, units = wg.shape
    merged = outs[4]
    moves = (
        (xa, xa_ref),
        (gain_in, gain_ref),
        (xb, xb_ref),
        (cot, cot_ref),
        (wd, down),
        (wg, merged.at[pl.ds(0, width)]),
        (wu, merged.at[pl.ds(width, width)]),
    )
    copies = [pltpu.make_async_copy(*move, sems.at[i]) for i, move in enumerate(moves)]
    for copy in copies:
        copy.start()
    for copy in copies[:4]:
        copy.wait()
    places = []
    for route_ref in (ra_ref, rb_ref):
        masks = slot_masks(info_ref, route_ref)
        places.append((masks[0][0] | masks[1][0]).astype(F32).astype(BF16))
    gain = gain_ref[...]
    normed_a = (normalized(xa_ref[...])[0] * gain).astype(BF16)
    normed_b = (normalized(xb_ref[...])[0] * gain).astype(BF16)
    sources = ((places[0], normed_a), (places[1], normed_b), (places[1], cot_ref[...]))
    for i, (place, rows) in enumerate(sources):
        packed = lax.dot_general(place, rows, TN, preferred_element_type=F32).astype(BF16)
        for j in range(4):
            outs[j][:, i * width : (i + 1) * width] = packed[j * SLOT : (j + 1) * SLOT]
    copies[4].wait()
    for at in range(0, width, units):
        merged[2 * width + at : 2 * width + at + units, :] = down[:, at : at + units]
    copies[5].wait()
    copies[6].wait()


def stage_kernel(own, a, b, c, left, right, last):
    half = left.shape[1]
    for i, ref in enumerate((own, a, b)):
        rows = slice(i * SLOT, (i + 1) * SLOT)
        left[rows, :] = ref[:, :half]
        right[rows, :] = ref[:, half:]
    last[...] = c[...]


def hidden(rows, wg, wu):
    both = jnp.dot(rows, jnp.concatenate([wg, wu], axis=1), preferred_element_type=F32)
    return both[:, :128], both[:, 128:]


def down_columns(merged, at, count):
    width = merged.shape[0] // 3
    starts = range(2 * width + at, 2 * width + at + count, 128)
    return jnp.concatenate([merged[start : start + 128, :] for start in starts], axis=1)


def gather_rows(refs, at, scratch, to, width):
    *refs, order = refs
    cols = slice(at, at + width)
    into = slice(to, to + width)
    for i, source in enumerate(order):
        first, last = refs[i // 2], refs[2 + i // 2]
        one, two = 3 * SLOT * (i % 2), SLOT * (i % 2)
        row = 4 * SLOT * source
        scratch[row : row + 3 * SLOT, into] = first[one : one + 3 * SLOT, cols]
        scratch[row + 3 * SLOT : row + 4 * SLOT, into] = last[two : two + SLOT, cols]


LEFT = (0, 1, 2, 3)
RIGHT = (0, 2, 1, 3)


def store_parts(part, cols, keep1, send1, keep2, send2):
    for ref, starts in ((keep1, (0, 64)), (send1, (128, 192)), (keep2, (32, 160)), (send2, (96, 224))):
        for i, start in enumerate(starts):
            ref[32 * i : 32 * (i + 1), cols] = part[start : start + 32].astype(ref.dtype)


def fwd_kernel(l1, l2, l3, l4, wg, wu, wd, other, keep1, send1, keep2, send2, rows):
    width = rows.shape[1]
    gather_rows((l1, l2, l3, l4, LEFT), 0, rows, 0, width)
    inner = []
    for weights in ((wg[...], wu[...]), (other[0:width, :], other[width : 2 * width, :])):
        gate, up = hidden(rows[...], *weights)
        inner.append((gate * jax.nn.sigmoid(gate) * up).astype(BF16))
    inner = jnp.concatenate(inner, axis=1)
    step = 512
    for at in range(0, width, step):
        cols = slice(at, at + step)
        down = jnp.concatenate([wd[:, cols], down_columns(other, at, step)], axis=0)
        part = jnp.dot(inner, down, preferred_element_type=F32)
        store_parts(part, cols, keep1, send1, keep2, send2)


def bwd_kernel(
    l1, l2, l3, l4, r1, r2, r3, r4, wg, wu, wd, other, _, keep1, send1, keep2, send2, rows, cots
):
    width = rows.shape[1]
    half = width // 2
    gather_rows((l1, l2, l3, l4, LEFT), width, rows, 0, half)
    gather_rows((r1, r2, r3, r4, RIGHT), 0, rows, half, half)
    gather_rows((r1, r2, r3, r4, RIGHT), half, cots, 0, width)
    back = []
    products = None
    sources = (
        (wg[...], wu[...], wd[...]),
        (other[0:width, :], other[width : 2 * width, :], down_columns(other, 0, width)),
    )
    for gate_w, up_w, down_w in sources:
        gate, up = hidden(rows[...], gate_w, up_w)
        d_inner = lax.dot_general(cots[...], down_w, NT, preferred_element_type=F32)
        sig = jax.nn.sigmoid(gate)
        silu = gate * sig
        inner = (silu * up).astype(BF16).astype(F32)
        d_gate = (d_inner * up * sig * (1.0 + gate * (1.0 - sig))).astype(BF16)
        d_up = (d_inner * silu).astype(BF16)
        back.append(jnp.concatenate([d_gate, d_up], axis=1))
        product = inner * d_inner
        products = product if products is None else products + product
    count = products.shape[0]
    high = products.astype(BF16)
    low = (products - high.astype(F32)).astype(BF16)
    ones = jnp.ones((16, 128), BF16)
    grads = lax.dot_general(ones, high, NT, preferred_element_type=F32)
    grads = grads + lax.dot_general(ones, low, NT, preferred_element_type=F32)
    row = lax.broadcasted_iota(jnp.int32, (count, count), 0)
    col = lax.broadcasted_iota(jnp.int32, (count, count), 1)
    held = (row // SLOT == col // SLOT) & (row % SLOT == SLOT - 2)
    spread = jnp.where(held, grads[0:1, :], 0.0).astype(BF16)
    at_row = lax.broadcasted_iota(jnp.int32, (count, 128), 0)
    at_col = lax.broadcasted_iota(jnp.int32, (count, 128), 1)
    pick = (at_row % SLOT == at_col).astype(F32).astype(BF16)
    grad_rows = jnp.dot(spread, pick, preferred_element_type=F32)
    step = 512
    for at in range(0, width, step):
        cols = slice(at, at + step)
        there = slice(width + at, width + at + step)
        weights = (
            jnp.concatenate([wg[cols, :], wu[cols, :]], axis=1),
            jnp.concatenate([other[cols, :], other[there, :]], axis=1),
        )
        part = None
        for grad, weight in zip(back, weights):
            term = lax.dot_general(grad, weight, NT, preferred_element_type=F32)
            part = term if part is None else part + term
        if at == 0:
            part = jnp.concatenate([part[:, :128] + grad_rows, part[:, 128:]], axis=1)
        store_parts(part, cols, keep1, send1, keep2, send2)


def mixed_rows(masks, weight_ref, parts):
    weights = weight_ref[...]
    spread = jnp.where(masks[0][0], weights[:, 0:1], 0.0) + jnp.where(
        masks[1][0], weights[:, 1:2], 0.0
    )
    high = spread.astype(BF16)
    rest = spread - high.astype(F32)
    middle = rest.astype(BF16)
    low = (rest - middle.astype(F32)).astype(BF16)
    total = None
    for j, part in enumerate(parts):
        at = slice(j * SLOT, (j + 1) * SLOT)
        for piece in (high, middle, low):
            term = jnp.dot(piece[:, at], part, preferred_element_type=F32)
            total = term if total is None else total + term
    return total


def fwd_out_kernel(info_ref, x_ref, route_ref, weight_ref, own, a, b, c, out_ref):
    masks = slot_masks(info_ref, route_ref)
    parts = [own[...], a[...], b[...], c[...]]
    mixed = mixed_rows(masks, weight_ref, parts)
    out_ref[...] = (x_ref[...].astype(F32) + mixed).astype(BF16)


def bwd_out_kernel(
    info_ref, x_ref, route_ref, weight_ref, cot_ref, gain_ref, own, a, b, c, out_ref, grad_ref
):
    masks = slot_masks(info_ref, route_ref)
    parts = [own[...], a[...], b[...], c[...]]
    d_normed = mixed_rows(masks, weight_ref, parts)
    unit, scale = normalized(x_ref[...])
    q_term = d_normed * gain_ref[...]
    mean = jnp.mean(q_term * unit, axis=-1, keepdims=True)
    d_input = cot_ref[...].astype(F32) + scale * (q_term - unit * mean)
    out_ref[...] = d_input.astype(BF16)
    tokens = x_ref.shape[0]
    lanes = lax.broadcasted_iota(jnp.int32, (tokens, 128), 1)
    grads = []
    for _, rel, rank in masks:
        held = jnp.zeros((tokens, 128), F32)
        for j, part in enumerate(parts):
            row = part[:, :128].astype(F32)[SLOT - 2 : SLOT - 1, :]
            held = held + jnp.where(rel == j, row, 0.0)
        grads.append(jnp.sum(jnp.where(lanes == rank, held, 0.0), axis=1, keepdims=True))
    pair = lax.broadcasted_iota(jnp.int32, (tokens, 2), 1)
    grad_ref[...] = jnp.where(pair == 0, grads[0], grads[1]).astype(BF16)


def spread_x(value, first, second):
    near = jnp.concatenate([value, hop(value, first)], axis=0)
    return near, hop(near, second)


def spread_rows(own, a, b, c):
    half = own.shape[1] // 2
    got_a, got_b = hop(a, HOP_A), hop(b, HOP_B)
    left, right, c = kernel_call(
        stage_kernel, [((3 * SLOT, half), BF16)] * 2 + [(c.shape, BF16)], 4, info=False
    )(own, got_a, got_b, c)
    got_c = hop(c, HOP_C)
    lefts = spread_x(left, HOP_X1, HOP_X3)
    rights = spread_x(right, HOP_X3, HOP_X1)
    lefts += spread_x(got_c[:, :half], HOP_X1, HOP_X3)
    rights += spread_x(got_c[:, half:], HOP_X3, HOP_X1)
    return lefts, rights


def return_rows(keep1, send1, keep2, send2):
    sum1 = keep1 + hop(send1, HOP_X3).astype(F32)
    sum2 = keep2 + hop(send2, HOP_X1).astype(F32)
    full1 = sum1[:32] + hop(sum1[32:].astype(BF16), HOP_X1).astype(F32)
    full2 = sum2[:32] + hop(sum2[32:].astype(BF16), HOP_X3).astype(F32)
    full1 = full1.astype(BF16)
    full2 = full2.astype(BF16)
    back_a = hop(full1[SLOT:], HOP_A)
    back_b = hop(full2[:SLOT], HOP_B_BACK)
    back_c = hop(full2[SLOT:], HOP_C)
    return full1[:SLOT], back_a, back_b, back_c


def body(
    act_fwd,
    route_fwd,
    weight_fwd,
    act_bwd,
    route_bwd,
    weight_bwd,
    cot_bwd,
    norm_gain,
    w_gate,
    w_up,
    w_down,
):
    tokens, width = act_fwd.shape[1:]
    index = lax.axis_index("expert")
    info = jnp.stack([index >> 3, (index >> 2) & 1]).astype(jnp.int32)
    weights = (w_gate[0, 0], w_up[0, 0], w_down[0, 0])
    units = w_down.shape[2]
    wide = [((SLOT, 3 * width), BF16)] * 4 + [((3 * width, units), BF16)]
    sources = (act_fwd[0], act_bwd[0], cot_bwd[0], norm_gain, *weights)
    vmem = pl.BlockSpec(memory_space=pltpu.VMEM)
    *sent, merged = pl.pallas_call(
        first_kernel,
        out_shape=[jax.ShapeDtypeStruct(s, d) for s, d in wide],
        in_specs=[pl.BlockSpec(memory_space=pltpu.SMEM), vmem, vmem]
        + [pl.BlockSpec(memory_space=pltpu.HBM)] * 7,
        out_specs=[vmem] * len(wide),
        scratch_shapes=[pltpu.VMEM((tokens, width), BF16)] * 3
        + [
            pltpu.VMEM((1, width), F32),
            pltpu.VMEM((units, width), BF16),
            pltpu.SemaphoreType.DMA((7,)),
        ],
        compiler_params=pltpu.CompilerParams(vmem_limit_bytes=32 * 1024 * 1024),
    )(info, route_fwd[0], route_bwd[0], *sources)
    other = hop(merged, HOP_W)
    lefts, rights = spread_rows(*sent)
    outs = [((64, width), F32), ((64, width), BF16)] * 2
    scratch = pltpu.VMEM((256, width), BF16)
    part_a = kernel_call(fwd_kernel, outs, 8, [scratch], info=False)(*lefts, *weights, other)
    part_b = kernel_call(bwd_kernel, outs, 13, [scratch] * 2, info=False)(
        *lefts, *rights, *weights, other, part_a[1]
    )
    back_a = return_rows(*part_a)
    back_b = return_rows(*part_b)
    (layer_out,) = kernel_call(fwd_out_kernel, [((tokens, width), BF16)], 7)(
        info, act_fwd[0], route_fwd[0], weight_fwd[0], *back_a
    )
    act_next = shifted(layer_out, "section", 1)
    d_input, gate_grad = kernel_call(
        bwd_out_kernel, [((tokens, width), BF16), ((tokens, 2), BF16)], 9
    )(info, act_bwd[0], route_bwd[0], weight_bwd[0], cot_bwd[0], norm_gain, *back_b)
    cot_next = shifted(d_input, "section", -1)
    return (act_next[None], cot_next[None], gate_grad[None])


def solution(mesh):
    return jax.shard_map(
        body,
        mesh=mesh,
        in_specs=(
            P("section", "expert", None),
            P("section", "expert", None),
            P("section", "expert", None),
            P("section", "expert", None),
            P("section", "expert", None),
            P("section", "expert", None),
            P("section", "expert", None),
            P("section", None),
            P("section", "expert", None, None),
            P("section", "expert", None, None),
            P("section", "expert", None, None),
        ),
        out_specs=(
            P("section", "expert", None),
            P("section", "expert", None),
            P("section", "expert", None),
        ),
        check_vma=False,
    )
```

```python
import jax
import jax.numpy as jnp
from jax import lax
from jax.experimental import pallas as pl
from jax.experimental.pallas import tpu as pltpu
from jax.sharding import PartitionSpec as P

EXPERTS = 4
GRID_X = 4
GRID_Z = 8
SLOT = 16
F32 = jnp.float32
BF16 = jnp.bfloat16
NT = (((1,), (1,)), ((), ()))
TN = (((0,), (0,)), ((), ()))


def expert_pairs(move):
    pairs = []
    for z in range(GRID_Z):
        for x in range(GRID_X):
            to_z, to_x = move(z, x)
            pairs.append((z * GRID_X + x, to_z % GRID_Z * GRID_X + to_x))
    return pairs


def signed(z, even, odd):
    return z + (odd if z % 2 else even)


HOP_W = expert_pairs(lambda z, x: (z ^ 1, x))
HOP_A = expert_pairs(lambda z, x: (signed(z, -1, 1), x))
HOP_B = expert_pairs(lambda z, x: (signed(z, 2, -2), x))
HOP_B_BACK = expert_pairs(lambda z, x: (signed(z, -2, 2), x))
HOP_C = expert_pairs(lambda z, x: (signed(z, -3, 3), x))
HOP_X1 = expert_pairs(lambda z, x: (z, x ^ 1))
HOP_X3 = expert_pairs(lambda z, x: (z, x ^ 3))


def hop(value, pairs):
    return lax.ppermute(value, "expert", pairs)


def shifted(value, axis, by):
    devices = lax.axis_size(axis)
    pairs = [(i, i + by) for i in range(devices) if 0 <= i + by < devices]
    return lax.ppermute(value, axis, pairs)


def kernel_call(kernel, outs, n_in, scratch=(), info=True, limit=32):
    smem = pl.BlockSpec(memory_space=pltpu.SMEM)
    vmem = pl.BlockSpec(memory_space=pltpu.VMEM)
    return pl.pallas_call(
        kernel,
        out_shape=[jax.ShapeDtypeStruct(s, d) for s, d in outs],
        in_specs=[smem] * info + [vmem] * n_in,
        out_specs=[vmem] * len(outs),
        scratch_shapes=list(scratch),
        compiler_params=pltpu.CompilerParams(vmem_limit_bytes=limit * 1024 * 1024),
    )


def slot_masks(info_ref, route_ref):
    tokens = route_ref.shape[0]
    own, odd = info_ref[0], info_ref[1]
    lanes = lax.broadcasted_iota(jnp.int32, (tokens, 128), 1)
    route = route_ref[...]
    named = [(route[:, k : k + 1] == lanes).astype(F32) for k in range(2)]
    row = lax.broadcasted_iota(jnp.int32, (tokens, tokens), 0)
    col = lax.broadcasted_iota(jnp.int32, (tokens, tokens), 1)
    earlier = (col < row).astype(BF16)
    counts = jnp.dot(earlier, (named[0] + named[1]).astype(BF16), preferred_element_type=F32)
    out = []
    for k in range(2):
        rank = jnp.sum(named[k] * counts, axis=1, keepdims=True).astype(jnp.int32)
        away = (route[:, k : k + 1] - own) & 3
        side = jnp.where((away == 3) == (odd == 0), 1, 2)
        rel = jnp.where(away == 0, 0, jnp.where(away == 2, 3, side))
        slots = lax.broadcasted_iota(jnp.int32, (tokens, 4 * SLOT), 1)
        out.append((slots == rel * SLOT + rank, rel, rank))
    return out


def normalized(x):
    values = x.astype(F32)
    scale = lax.rsqrt(jnp.mean(values * values, axis=-1, keepdims=True) + 1e-06)
    return values * scale, scale


def first_kernel(info_ref, ra_ref, rb_ref, xa, xb, cot, gain_in, wg, wu, wd, *rest):
    outs, (xa_ref, xb_ref, cot_ref, gain_ref, down, sems) = rest[:5], rest[5:]
    width, units = wg.shape
    merged = outs[4]
    moves = (
        (xa, xa_ref),
        (gain_in, gain_ref),
        (xb, xb_ref),
        (cot, cot_ref),
        (wd, down),
        (wg, merged.at[pl.ds(0, width)]),
        (wu, merged.at[pl.ds(width, width)]),
    )
    copies = [pltpu.make_async_copy(*move, sems.at[i]) for i, move in enumerate(moves)]
    for copy in copies:
        copy.start()
    for copy in copies[:4]:
        copy.wait()
    places = []
    for route_ref in (ra_ref, rb_ref):
        masks = slot_masks(info_ref, route_ref)
        places.append((masks[0][0] | masks[1][0]).astype(F32).astype(BF16))
    gain = gain_ref[...]
    normed_a = (normalized(xa_ref[...])[0] * gain).astype(BF16)
    normed_b = (normalized(xb_ref[...])[0] * gain).astype(BF16)
    sources = ((places[0], normed_a), (places[1], normed_b), (places[1], cot_ref[...]))
    for i, (place, rows) in enumerate(sources):
        packed = lax.dot_general(place, rows, TN, preferred_element_type=F32).astype(BF16)
        for j in range(4):
            outs[j][:, i * width : (i + 1) * width] = packed[j * SLOT : (j + 1) * SLOT]
    copies[4].wait()
    for at in range(0, width, units):
        merged[2 * width + at : 2 * width + at + units, :] = down[:, at : at + units]
    copies[5].wait()
    copies[6].wait()


def hidden(rows, wg, wu):
    both = jnp.dot(rows, jnp.concatenate([wg, wu], axis=1), preferred_element_type=F32)
    return both[:, :128], both[:, 128:]


def down_columns(merged, at, count):
    width = merged.shape[0] // 3
    starts = range(2 * width + at, 2 * width + at + count, 128)
    return jnp.concatenate([merged[start : start + 128, :] for start in starts], axis=1)


def gather_rows(refs, at, width, scratch):
    for i, ref in enumerate(refs):
        scratch[64 * i : 64 * (i + 1), :] = ref[:, at : at + width]


def store_parts(part, cols, keep1, send1, keep2, send2):
    keep1[:, cols] = part[0:64]
    send1[:, cols] = part[64:128].astype(BF16)
    keep2[:, cols] = part[128:192]
    send2[:, cols] = part[192:256].astype(BF16)


def fwd_kernel(c1, qr1, c2, pr2, wg, wu, wd, other, keep1, send1, keep2, send2, rows):
    width = rows.shape[1]
    gather_rows((c1, qr1, c2, pr2), 0, width, rows)
    inner = []
    for weights in ((wg[...], wu[...]), (other[0:width, :], other[width : 2 * width, :])):
        gate, up = hidden(rows[...], *weights)
        inner.append((gate * jax.nn.sigmoid(gate) * up).astype(BF16))
    inner = jnp.concatenate(inner, axis=1)
    step = 512
    for at in range(0, width, step):
        cols = slice(at, at + step)
        down = jnp.concatenate([wd[:, cols], down_columns(other, at, step)], axis=0)
        part = jnp.dot(inner, down, preferred_element_type=F32)
        store_parts(part, cols, keep1, send1, keep2, send2)


def bwd_kernel(
    c1, qr1, c2, pr2, wg, wu, wd, other, _1, _2, keep1, send1, keep2, send2, rows, cots
):
    width = rows.shape[1]
    gather_rows((c1, qr1, c2, pr2), 0, width, rows)
    gather_rows((c1, qr1, c2, pr2), width, width, cots)
    back = []
    products = None
    sources = (
        (wg[...], wu[...], wd[...]),
        (other[0:width, :], other[width : 2 * width, :], down_columns(other, 0, width)),
    )
    for gate_w, up_w, down_w in sources:
        gate, up = hidden(rows[...], gate_w, up_w)
        d_inner = lax.dot_general(cots[...], down_w, NT, preferred_element_type=F32)
        sig = jax.nn.sigmoid(gate)
        silu = gate * sig
        inner = (silu * up).astype(BF16).astype(F32)
        d_gate = (d_inner * up * sig * (1.0 + gate * (1.0 - sig))).astype(BF16)
        d_up = (d_inner * silu).astype(BF16)
        back.append(jnp.concatenate([d_gate, d_up], axis=1))
        product = inner * d_inner
        products = product if products is None else products + product
    count = products.shape[0]
    high = products.astype(BF16)
    low = (products - high.astype(F32)).astype(BF16)
    ones = jnp.ones((16, 128), BF16)
    grads = lax.dot_general(ones, high, NT, preferred_element_type=F32)
    grads = grads + lax.dot_general(ones, low, NT, preferred_element_type=F32)
    row = lax.broadcasted_iota(jnp.int32, (count, count), 0)
    col = lax.broadcasted_iota(jnp.int32, (count, count), 1)
    held = (row // SLOT == col // SLOT) & (row % SLOT == SLOT - 2)
    spread = jnp.where(held, grads[0:1, :], 0.0).astype(BF16)
    at_row = lax.broadcasted_iota(jnp.int32, (count, 128), 0)
    at_col = lax.broadcasted_iota(jnp.int32, (count, 128), 1)
    pick = (at_row % SLOT == at_col).astype(F32).astype(BF16)
    grad_rows = jnp.dot(spread, pick, preferred_element_type=F32)
    step = 512
    for at in range(0, width, step):
        cols = slice(at, at + step)
        there = slice(width + at, width + at + step)
        weights = (
            jnp.concatenate([wg[cols, :], wu[cols, :]], axis=1),
            jnp.concatenate([other[cols, :], other[there, :]], axis=1),
        )
        part = None
        for grad, weight in zip(back, weights):
            term = lax.dot_general(grad, weight, NT, preferred_element_type=F32)
            part = term if part is None else part + term
        if at == 0:
            part = jnp.concatenate([part[:, :128] + grad_rows, part[:, 128:]], axis=1)
        store_parts(part, cols, keep1, send1, keep2, send2)


def mixed_rows(masks, weight_ref, parts):
    weights = weight_ref[...]
    spread = jnp.where(masks[0][0], weights[:, 0:1], 0.0) + jnp.where(
        masks[1][0], weights[:, 1:2], 0.0
    )
    high = spread.astype(BF16)
    rest = spread - high.astype(F32)
    middle = rest.astype(BF16)
    low = (rest - middle.astype(F32)).astype(BF16)
    total = None
    for j, part in enumerate(parts):
        at = slice(j * SLOT, (j + 1) * SLOT)
        for piece in (high, middle, low):
            term = jnp.dot(piece[:, at], part, preferred_element_type=F32)
            total = term if total is None else total + term
    return total


def last_kernel(
    info_ref, xa_ref, ra_ref, wa_ref, x_ref, route_ref, weight_ref, cot_ref, gain_ref, *rest
):
    parts_a, parts = [r[...] for r in rest[:4]], [r[...] for r in rest[4:8]]
    out_a_ref, out_ref, grad_ref = rest[8:]
    mixed = mixed_rows(slot_masks(info_ref, ra_ref), wa_ref, parts_a)
    out_a_ref[...] = (xa_ref[...].astype(F32) + mixed).astype(BF16)
    masks = slot_masks(info_ref, route_ref)
    d_normed = mixed_rows(masks, weight_ref, parts)
    unit, scale = normalized(x_ref[...])
    q_term = d_normed * gain_ref[...]
    mean = jnp.mean(q_term * unit, axis=-1, keepdims=True)
    d_input = cot_ref[...].astype(F32) + scale * (q_term - unit * mean)
    out_ref[...] = d_input.astype(BF16)
    tokens = x_ref.shape[0]
    lanes = lax.broadcasted_iota(jnp.int32, (tokens, 128), 1)
    grads = []
    for _, rel, rank in masks:
        held = jnp.zeros((tokens, 128), F32)
        for j, part in enumerate(parts):
            row = part[:, :128].astype(F32)[SLOT - 2 : SLOT - 1, :]
            held = held + jnp.where(rel == j, row, 0.0)
        grads.append(jnp.sum(jnp.where(lanes == rank, held, 0.0), axis=1, keepdims=True))
    pair = lax.broadcasted_iota(jnp.int32, (tokens, 2), 1)
    grad_ref[...] = jnp.where(pair == 0, grads[0], grads[1]).astype(BF16)


def spread_x(half1, half2):
    c1 = jnp.concatenate([half1, hop(half1, HOP_X1)], axis=0)
    c2 = jnp.concatenate([half2, hop(half2, HOP_X3)], axis=0)
    return c1, hop(c1, HOP_X3), c2, hop(c2, HOP_X1)


def spread_rows(own, a, b, c):
    got_a, got_b, got_c = hop(a, HOP_A), hop(b, HOP_B), hop(c, HOP_C)
    half1 = jnp.concatenate([own, got_a], axis=0)
    half2 = jnp.concatenate([got_b, got_c], axis=0)
    width = own.shape[1] // 3
    return (
        spread_x(half1[:, :width], half2[:, :width]),
        spread_x(half1[:, width:], half2[:, width:]),
    )


def first_sums(keep1, send1, keep2, send2):
    sum1 = keep1 + hop(send1, HOP_X3).astype(F32)
    sum2 = keep2 + hop(send2, HOP_X1).astype(F32)
    return sum1, sum2


def return_rows(sum1, sum2):
    full1 = sum1[:32] + hop(sum1[32:].astype(BF16), HOP_X1).astype(F32)
    full2 = sum2[:32] + hop(sum2[32:].astype(BF16), HOP_X3).astype(F32)
    full1 = full1.astype(BF16)
    full2 = full2.astype(BF16)
    back_a = hop(full1[SLOT:], HOP_A)
    back_b = hop(full2[:SLOT], HOP_B_BACK)
    back_c = hop(full2[SLOT:], HOP_C)
    return full1[:SLOT], back_a, back_b, back_c


def body(
    act_fwd,
    route_fwd,
    weight_fwd,
    act_bwd,
    route_bwd,
    weight_bwd,
    cot_bwd,
    norm_gain,
    w_gate,
    w_up,
    w_down,
):
    tokens, width = act_fwd.shape[1:]
    index = lax.axis_index("expert")
    info = jnp.stack([index >> 3, (index >> 2) & 1]).astype(jnp.int32)
    weights = (w_gate[0, 0], w_up[0, 0], w_down[0, 0])
    units = w_down.shape[2]
    wide = [((SLOT, 3 * width), BF16)] * 4 + [((3 * width, units), BF16)]
    sources = (act_fwd[0], act_bwd[0], cot_bwd[0], norm_gain, *weights)
    vmem = pl.BlockSpec(memory_space=pltpu.VMEM)
    *sent, merged = pl.pallas_call(
        first_kernel,
        out_shape=[jax.ShapeDtypeStruct(s, d) for s, d in wide],
        in_specs=[pl.BlockSpec(memory_space=pltpu.SMEM), vmem, vmem]
        + [pl.BlockSpec(memory_space=pltpu.HBM)] * 7,
        out_specs=[vmem] * len(wide),
        scratch_shapes=[pltpu.VMEM((tokens, width), BF16)] * 3
        + [
            pltpu.VMEM((1, width), F32),
            pltpu.VMEM((units, width), BF16),
            pltpu.SemaphoreType.DMA((7,)),
        ],
        compiler_params=pltpu.CompilerParams(vmem_limit_bytes=60 * 1024 * 1024),
    )(info, route_fwd[0], route_bwd[0], *sources)
    other = hop(merged, HOP_W)
    rows_a, rows_b = spread_rows(*sent)
    outs = [((64, width), F32), ((64, width), BF16)] * 2
    scratch = pltpu.VMEM((256, width), BF16)
    part_a = kernel_call(fwd_kernel, outs, 8, [scratch], info=False)(*rows_a, *weights, other)
    sums_a = first_sums(*part_a)
    part_b = kernel_call(bwd_kernel, outs, 10, [scratch] * 2, info=False)(
        *rows_b, *weights, other, *sums_a
    )
    back_a = return_rows(*sums_a)
    back_b = return_rows(*first_sums(*part_b))
    layer_out, d_input, gate_grad = kernel_call(
        last_kernel, [((tokens, width), BF16)] * 2 + [((tokens, 2), BF16)], 16
    )(
        info,
        act_fwd[0],
        route_fwd[0],
        weight_fwd[0],
        act_bwd[0],
        route_bwd[0],
        weight_bwd[0],
        cot_bwd[0],
        norm_gain,
        *back_a,
        *back_b,
    )
    act_next = shifted(layer_out, "section", 1)
    cot_next = shifted(d_input, "section", -1)
    return (act_next[None], cot_next[None], gate_grad[None])


def solution(mesh):
    return jax.shard_map(
        body,
        mesh=mesh,
        in_specs=(
            P("section", "expert", None),
            P("section", "expert", None),
            P("section", "expert", None),
            P("section", "expert", None),
            P("section", "expert", None),
            P("section", "expert", None),
            P("section", "expert", None),
            P("section", None),
            P("section", "expert", None, None),
            P("section", "expert", None, None),
            P("section", "expert", None, None),
        ),
        out_specs=(
            P("section", "expert", None),
            P("section", "expert", None),
            P("section", "expert", None),
        ),
        check_vma=False,
    )
```

```python
import jax
import jax.numpy as jnp
from jax import lax
from jax.experimental import pallas as pl
from jax.experimental.pallas import tpu as pltpu
from jax.sharding import PartitionSpec as P

EXPERTS = 4
GRID_X = 4
GRID_Z = 8
SLOT = 16
F32 = jnp.float32
BF16 = jnp.bfloat16
NT = (((1,), (1,)), ((), ()))
TN = (((0,), (0,)), ((), ()))


def expert_pairs(move):
    pairs = []
    for z in range(GRID_Z):
        for x in range(GRID_X):
            to_z, to_x = move(z, x)
            pairs.append((z * GRID_X + x, to_z % GRID_Z * GRID_X + to_x))
    return pairs


def signed(z, even, odd):
    return z + (odd if z % 2 else even)


HOP_W = expert_pairs(lambda z, x: (z ^ 1, x))
HOP_A = expert_pairs(lambda z, x: (signed(z, -1, 1), x))
HOP_B = expert_pairs(lambda z, x: (signed(z, 2, -2), x))
HOP_B_BACK = expert_pairs(lambda z, x: (signed(z, -2, 2), x))
HOP_C = expert_pairs(lambda z, x: (signed(z, -3, 3), x))
HOP_X1 = expert_pairs(lambda z, x: (z, x ^ 1))
HOP_X3 = expert_pairs(lambda z, x: (z, x ^ 3))


def hop(value, pairs):
    return lax.ppermute(value, "expert", pairs)


def shifted(value, axis, by):
    devices = lax.axis_size(axis)
    pairs = [(i, i + by) for i in range(devices) if 0 <= i + by < devices]
    return lax.ppermute(value, axis, pairs)


def kernel_call(kernel, outs, n_in, scratch=(), info=True, limit=32):
    smem = pl.BlockSpec(memory_space=pltpu.SMEM)
    vmem = pl.BlockSpec(memory_space=pltpu.VMEM)
    return pl.pallas_call(
        kernel,
        out_shape=[jax.ShapeDtypeStruct(s, d) for s, d in outs],
        in_specs=[smem] * info + [vmem] * n_in,
        out_specs=[vmem] * len(outs),
        scratch_shapes=list(scratch),
        compiler_params=pltpu.CompilerParams(vmem_limit_bytes=limit * 1024 * 1024),
    )


def slot_masks(info_ref, route_ref):
    tokens = route_ref.shape[0]
    own, odd = info_ref[0], info_ref[1]
    lanes = lax.broadcasted_iota(jnp.int32, (tokens, 128), 1)
    route = route_ref[...]
    named = [(route[:, k : k + 1] == lanes).astype(F32) for k in range(2)]
    row = lax.broadcasted_iota(jnp.int32, (tokens, tokens), 0)
    col = lax.broadcasted_iota(jnp.int32, (tokens, tokens), 1)
    earlier = (col < row).astype(BF16)
    counts = jnp.dot(earlier, (named[0] + named[1]).astype(BF16), preferred_element_type=F32)
    out = []
    for k in range(2):
        rank = jnp.sum(named[k] * counts, axis=1, keepdims=True).astype(jnp.int32)
        away = (route[:, k : k + 1] - own) & 3
        side = jnp.where((away == 3) == (odd == 0), 1, 2)
        rel = jnp.where(away == 0, 0, jnp.where(away == 2, 3, side))
        slots = lax.broadcasted_iota(jnp.int32, (tokens, 4 * SLOT), 1)
        out.append((slots == rel * SLOT + rank, rel, rank))
    return out


def normalized(x):
    values = x.astype(F32)
    scale = lax.rsqrt(jnp.mean(values * values, axis=-1, keepdims=True) + 1e-06)
    return values * scale, scale


def pack_kernel(info_ref, xa_ref, ra_ref, xb_ref, rb_ref, cot_ref, gain_ref, *outs):
    width = xa_ref.shape[1]
    places = []
    for route_ref in (ra_ref, rb_ref):
        masks = slot_masks(info_ref, route_ref)
        places.append((masks[0][0] | masks[1][0]).astype(F32).astype(BF16))
    gain = gain_ref[...]
    normed_a = (normalized(xa_ref[...])[0] * gain).astype(BF16)
    normed_b = (normalized(xb_ref[...])[0] * gain).astype(BF16)
    sources = ((places[0], normed_a), (places[1], normed_b), (places[1], cot_ref[...]))
    for i, (place, rows) in enumerate(sources):
        packed = lax.dot_general(place, rows, TN, preferred_element_type=F32).astype(BF16)
        for j in range(4):
            outs[j][:, i * width : (i + 1) * width] = packed[j * SLOT : (j + 1) * SLOT]


def merge_kernel(wg, wu, wd, out):
    width, units = wg.shape
    out[0:width, :] = wg[...]
    out[width : 2 * width, :] = wu[...]
    for at in range(0, width, units):
        out[2 * width + at : 2 * width + at + units, :] = wd[:, at : at + units]


def hidden(rows, wg, wu):
    both = jnp.dot(rows, jnp.concatenate([wg, wu], axis=1), preferred_element_type=F32)
    return both[:, :128], both[:, 128:]


def down_columns(merged, at, count):
    width = merged.shape[0] // 3
    starts = range(2 * width + at, 2 * width + at + count, 128)
    return jnp.concatenate([merged[start : start + 128, :] for start in starts], axis=1)


def gather_rows(refs, at, width, scratch):
    for i, ref in enumerate(refs):
        scratch[64 * i : 64 * (i + 1), :] = ref[:, at : at + width]


def store_parts(part, cols, keep1, send1, keep2, send2):
    keep1[:, cols] = part[0:64]
    send1[:, cols] = part[64:128].astype(BF16)
    keep2[:, cols] = part[128:192]
    send2[:, cols] = part[192:256].astype(BF16)


def fwd_kernel(c1, qr1, c2, pr2, wg, wu, wd, other, keep1, send1, keep2, send2, rows):
    width = rows.shape[1]
    gather_rows((c1, qr1, c2, pr2), 0, width, rows)
    inner = []
    for weights in ((wg[...], wu[...]), (other[0:width, :], other[width : 2 * width, :])):
        gate, up = hidden(rows[...], *weights)
        inner.append((gate * jax.nn.sigmoid(gate) * up).astype(BF16))
    inner = jnp.concatenate(inner, axis=1)
    step = 512
    for at in range(0, width, step):
        cols = slice(at, at + step)
        down = jnp.concatenate([wd[:, cols], down_columns(other, at, step)], axis=0)
        part = jnp.dot(inner, down, preferred_element_type=F32)
        store_parts(part, cols, keep1, send1, keep2, send2)


def bwd_kernel(
    c1, qr1, c2, pr2, wg, wu, wd, other, _, keep1, send1, keep2, send2, rows, cots
):
    width = rows.shape[1]
    gather_rows((c1, qr1, c2, pr2), width, width, rows)
    gather_rows((c1, qr1, c2, pr2), 2 * width, width, cots)
    back = []
    products = None
    sources = (
        (wg[...], wu[...], wd[...]),
        (other[0:width, :], other[width : 2 * width, :], down_columns(other, 0, width)),
    )
    for gate_w, up_w, down_w in sources:
        gate, up = hidden(rows[...], gate_w, up_w)
        d_inner = lax.dot_general(cots[...], down_w, NT, preferred_element_type=F32)
        sig = jax.nn.sigmoid(gate)
        silu = gate * sig
        inner = (silu * up).astype(BF16).astype(F32)
        d_gate = (d_inner * up * sig * (1.0 + gate * (1.0 - sig))).astype(BF16)
        d_up = (d_inner * silu).astype(BF16)
        back.append(jnp.concatenate([d_gate, d_up], axis=1))
        product = inner * d_inner
        products = product if products is None else products + product
    count = products.shape[0]
    high = products.astype(BF16)
    low = (products - high.astype(F32)).astype(BF16)
    ones = jnp.ones((16, 128), BF16)
    grads = lax.dot_general(ones, high, NT, preferred_element_type=F32)
    grads = grads + lax.dot_general(ones, low, NT, preferred_element_type=F32)
    row = lax.broadcasted_iota(jnp.int32, (count, count), 0)
    col = lax.broadcasted_iota(jnp.int32, (count, count), 1)
    held = (row // SLOT == col // SLOT) & (row % SLOT == SLOT - 2)
    spread = jnp.where(held, grads[0:1, :], 0.0).astype(BF16)
    at_row = lax.broadcasted_iota(jnp.int32, (count, 128), 0)
    at_col = lax.broadcasted_iota(jnp.int32, (count, 128), 1)
    pick = (at_row % SLOT == at_col).astype(F32).astype(BF16)
    grad_rows = jnp.dot(spread, pick, preferred_element_type=F32)
    step = 512
    for at in range(0, width, step):
        cols = slice(at, at + step)
        there = slice(width + at, width + at + step)
        weights = (
            jnp.concatenate([wg[cols, :], wu[cols, :]], axis=1),
            jnp.concatenate([other[cols, :], other[there, :]], axis=1),
        )
        part = None
        for grad, weight in zip(back, weights):
            term = lax.dot_general(grad, weight, NT, preferred_element_type=F32)
            part = term if part is None else part + term
        if at == 0:
            part = jnp.concatenate([part[:, :128] + grad_rows, part[:, 128:]], axis=1)
        store_parts(part, cols, keep1, send1, keep2, send2)


def mixed_rows(masks, weight_ref, parts):
    weights = weight_ref[...]
    spread = jnp.where(masks[0][0], weights[:, 0:1], 0.0) + jnp.where(
        masks[1][0], weights[:, 1:2], 0.0
    )
    high = spread.astype(BF16)
    rest = spread - high.astype(F32)
    middle = rest.astype(BF16)
    low = (rest - middle.astype(F32)).astype(BF16)
    total = None
    for j, part in enumerate(parts):
        at = slice(j * SLOT, (j + 1) * SLOT)
        for piece in (high, middle, low):
            term = jnp.dot(piece[:, at], part, preferred_element_type=F32)
            total = term if total is None else total + term
    return total


def last_kernel(
    info_ref, xa_ref, ra_ref, wa_ref, x_ref, route_ref, weight_ref, cot_ref, gain_ref, *rest
):
    width = x_ref.shape[1]
    parts_a = [ref[:, :width] for ref in rest[:4]]
    parts = [ref[:, width:] for ref in rest[:4]]
    out_a_ref, out_ref, grad_ref = rest[4:]
    mixed = mixed_rows(slot_masks(info_ref, ra_ref), wa_ref, parts_a)
    out_a_ref[...] = (xa_ref[...].astype(F32) + mixed).astype(BF16)
    masks = slot_masks(info_ref, route_ref)
    d_normed = mixed_rows(masks, weight_ref, parts)
    unit, scale = normalized(x_ref[...])
    q_term = d_normed * gain_ref[...]
    mean = jnp.mean(q_term * unit, axis=-1, keepdims=True)
    d_input = cot_ref[...].astype(F32) + scale * (q_term - unit * mean)
    out_ref[...] = d_input.astype(BF16)
    tokens = x_ref.shape[0]
    lanes = lax.broadcasted_iota(jnp.int32, (tokens, 128), 1)
    grads = []
    for _, rel, rank in masks:
        held = jnp.zeros((tokens, 128), F32)
        for j, part in enumerate(parts):
            row = part[:, :128].astype(F32)[SLOT - 2 : SLOT - 1, :]
            held = held + jnp.where(rel == j, row, 0.0)
        grads.append(jnp.sum(jnp.where(lanes == rank, held, 0.0), axis=1, keepdims=True))
    pair = lax.broadcasted_iota(jnp.int32, (tokens, 2), 1)
    grad_ref[...] = jnp.where(pair == 0, grads[0], grads[1]).astype(BF16)


def spread_rows(own, a, b, c):
    got_a, got_b, got_c = hop(a, HOP_A), hop(b, HOP_B), hop(c, HOP_C)
    half1 = jnp.concatenate([own, got_a], axis=0)
    half2 = jnp.concatenate([got_b, got_c], axis=0)
    p1 = hop(half1, HOP_X1)
    q2 = hop(half2, HOP_X3)
    c1 = jnp.concatenate([half1, p1], axis=0)
    c2 = jnp.concatenate([half2, q2], axis=0)
    return c1, hop(c1, HOP_X3), c2, hop(c2, HOP_X1)


def return_x(keep1, send1, keep2, send2):
    sum1 = keep1 + hop(send1, HOP_X3).astype(F32)
    sum2 = keep2 + hop(send2, HOP_X1).astype(F32)
    full1 = sum1[:32] + hop(sum1[32:].astype(BF16), HOP_X1).astype(F32)
    full2 = sum2[:32] + hop(sum2[32:].astype(BF16), HOP_X3).astype(F32)
    return full1.astype(BF16), full2.astype(BF16)


def return_z(full1, full2):
    back_c = hop(full2[SLOT:], HOP_C)
    back_b = hop(full2[:SLOT], HOP_B_BACK)
    back_a = hop(full1[SLOT:], HOP_A)
    return full1[:SLOT], back_a, back_b, back_c


def body(
    act_fwd,
    route_fwd,
    weight_fwd,
    act_bwd,
    route_bwd,
    weight_bwd,
    cot_bwd,
    norm_gain,
    w_gate,
    w_up,
    w_down,
):
    tokens, width = act_fwd.shape[1:]
    index = lax.axis_index("expert")
    info = jnp.stack([index >> 3, (index >> 2) & 1]).astype(jnp.int32)
    weights = (w_gate[0, 0], w_up[0, 0], w_down[0, 0])
    units = w_down.shape[2]
    (merged,) = kernel_call(merge_kernel, [((3 * width, units), BF16)], 3, info=False)(*weights)
    other = hop(merged, HOP_W)
    wide = [((SLOT, 3 * width), BF16)] * 4
    sent = kernel_call(pack_kernel, wide, 6)(
        info, act_fwd[0], route_fwd[0], act_bwd[0], route_bwd[0], cot_bwd[0], norm_gain
    )
    rows = spread_rows(*sent)
    outs = [((64, width), F32), ((64, width), BF16)] * 2
    scratch = pltpu.VMEM((256, width), BF16)
    part_a = kernel_call(fwd_kernel, outs, 8, [scratch], info=False)(*rows, *weights, other)
    part_b = kernel_call(bwd_kernel, outs, 9, [scratch] * 2, info=False)(
        *rows, *weights, other, part_a[1]
    )
    halves = zip(return_x(*part_a), return_x(*part_b))
    back = return_z(*[jnp.concatenate(pair, axis=1) for pair in halves])
    layer_out, d_input, gate_grad = kernel_call(
        last_kernel, [((tokens, width), BF16)] * 2 + [((tokens, 2), BF16)], 12
    )(
        info,
        act_fwd[0],
        route_fwd[0],
        weight_fwd[0],
        act_bwd[0],
        route_bwd[0],
        weight_bwd[0],
        cot_bwd[0],
        norm_gain,
        *back,
    )
    act_next = shifted(layer_out, "section", 1)
    cot_next = shifted(d_input, "section", -1)
    return (act_next[None], cot_next[None], gate_grad[None])


def solution(mesh):
    return jax.shard_map(
        body,
        mesh=mesh,
        in_specs=(
            P("section", "expert", None),
            P("section", "expert", None),
            P("section", "expert", None),
            P("section", "expert", None),
            P("section", "expert", None),
            P("section", "expert", None),
            P("section", "expert", None),
            P("section", None),
            P("section", "expert", None, None),
            P("section", "expert", None, None),
            P("section", "expert", None, None),
        ),
        out_specs=(
            P("section", "expert", None),
            P("section", "expert", None),
            P("section", "expert", None),
        ),
        check_vma=False,
    )
```

```python
import jax
import jax.numpy as jnp
from jax import lax
from jax.experimental import pallas as pl
from jax.experimental.pallas import tpu as pltpu
from jax.sharding import PartitionSpec as P

EXPERTS = 4
GRID_X = 4
GRID_Z = 8
SLOT = 16
F32 = jnp.float32
BF16 = jnp.bfloat16
NT = (((1,), (1,)), ((), ()))
TN = (((0,), (0,)), ((), ()))


def expert_pairs(move):
    pairs = []
    for z in range(GRID_Z):
        for x in range(GRID_X):
            to_z, to_x = move(z, x)
            pairs.append((z * GRID_X + x, to_z % GRID_Z * GRID_X + to_x))
    return pairs


def signed(z, even, odd):
    return z + (odd if z % 2 else even)


HOP_W = expert_pairs(lambda z, x: (z ^ 1, x))
HOP_A = expert_pairs(lambda z, x: (signed(z, -1, 1), x))
HOP_B = expert_pairs(lambda z, x: (signed(z, 2, -2), x))
HOP_B_BACK = expert_pairs(lambda z, x: (signed(z, -2, 2), x))
HOP_C = expert_pairs(lambda z, x: (signed(z, -3, 3), x))
HOP_X1 = expert_pairs(lambda z, x: (z, x ^ 1))
HOP_X3 = expert_pairs(lambda z, x: (z, x ^ 3))


def hop(value, pairs):
    return lax.ppermute(value, "expert", pairs)


def shifted(value, axis, by):
    devices = lax.axis_size(axis)
    pairs = [(i, i + by) for i in range(devices) if 0 <= i + by < devices]
    return lax.ppermute(value, axis, pairs)


def kernel_call(kernel, outs, n_in, scratch=(), info=True, limit=32):
    smem = pl.BlockSpec(memory_space=pltpu.SMEM)
    vmem = pl.BlockSpec(memory_space=pltpu.VMEM)
    return pl.pallas_call(
        kernel,
        out_shape=[jax.ShapeDtypeStruct(s, d) for s, d in outs],
        in_specs=[smem] * info + [vmem] * n_in,
        out_specs=[vmem] * len(outs),
        scratch_shapes=list(scratch),
        compiler_params=pltpu.CompilerParams(vmem_limit_bytes=limit * 1024 * 1024),
    )


def slot_masks(info_ref, route_ref):
    tokens = route_ref.shape[0]
    own, odd = info_ref[0], info_ref[1]
    lanes = lax.broadcasted_iota(jnp.int32, (tokens, 128), 1)
    route = route_ref[...]
    named = [(route[:, k : k + 1] == lanes).astype(F32) for k in range(2)]
    row = lax.broadcasted_iota(jnp.int32, (tokens, tokens), 0)
    col = lax.broadcasted_iota(jnp.int32, (tokens, tokens), 1)
    earlier = (col < row).astype(BF16)
    counts = jnp.dot(earlier, (named[0] + named[1]).astype(BF16), preferred_element_type=F32)
    out = []
    for k in range(2):
        rank = jnp.sum(named[k] * counts, axis=1, keepdims=True).astype(jnp.int32)
        away = (route[:, k : k + 1] - own) & 3
        side = jnp.where((away == 3) == (odd == 0), 1, 2)
        rel = jnp.where(away == 0, 0, jnp.where(away == 2, 3, side))
        slots = lax.broadcasted_iota(jnp.int32, (tokens, 4 * SLOT), 1)
        out.append((slots == rel * SLOT + rank, rel, rank))
    return out


def normalized(x):
    values = x.astype(F32)
    scale = lax.rsqrt(jnp.mean(values * values, axis=-1, keepdims=True) + 1e-06)
    return values * scale, scale


def pack_kernel(info_ref, xa_ref, ra_ref, xb_ref, rb_ref, cot_ref, gain_ref, *outs):
    width = xa_ref.shape[1]
    places = []
    for route_ref in (ra_ref, rb_ref):
        masks = slot_masks(info_ref, route_ref)
        places.append((masks[0][0] | masks[1][0]).astype(F32).astype(BF16))
    gain = gain_ref[...]
    normed_a = (normalized(xa_ref[...])[0] * gain).astype(BF16)
    normed_b = (normalized(xb_ref[...])[0] * gain).astype(BF16)
    sources = ((places[0], normed_a), (places[1], normed_b), (places[1], cot_ref[...]))
    for i, (place, rows) in enumerate(sources):
        packed = lax.dot_general(place, rows, TN, preferred_element_type=F32).astype(BF16)
        for j in range(4):
            outs[j][:, i * width : (i + 1) * width] = packed[j * SLOT : (j + 1) * SLOT]


def merge_kernel(wg, wu, wd, out):
    width, units = wg.shape
    out[0:width, :] = wg[...]
    out[width : 2 * width, :] = wu[...]
    for at in range(0, width, units):
        out[2 * width + at : 2 * width + at + units, :] = wd[:, at : at + units]


def hidden(rows, wg, wu):
    both = jnp.dot(rows, jnp.concatenate([wg, wu], axis=1), preferred_element_type=F32)
    return both[:, :128], both[:, 128:]


def down_columns(merged, at, count):
    width = merged.shape[0] // 3
    starts = range(2 * width + at, 2 * width + at + count, 128)
    return jnp.concatenate([merged[start : start + 128, :] for start in starts], axis=1)


def gather_rows(refs, at, width, scratch):
    for i, ref in enumerate(refs):
        scratch[64 * i : 64 * (i + 1), :] = ref[:, at : at + width]


def store_parts(part, cols, keep1, send1, keep2, send2):
    for ref, starts in ((keep1, (128, 192)), (send1, (160, 224)), (keep2, (0, 64)), (send2, (32, 96))):
        for i, start in enumerate(starts):
            ref[32 * i : 32 * (i + 1), cols] = part[start : start + 32].astype(ref.dtype)


def fwd_kernel(c1, qr1, c2, pr2, wg, wu, wd, other, keep1, send1, keep2, send2, rows):
    width = rows.shape[1]
    gather_rows((c1, qr1, c2, pr2), 0, width, rows)
    inner = []
    for weights in ((wg[...], wu[...]), (other[0:width, :], other[width : 2 * width, :])):
        gate, up = hidden(rows[...], *weights)
        inner.append((gate * jax.nn.sigmoid(gate) * up).astype(BF16))
    inner = jnp.concatenate(inner, axis=1)
    step = 512
    for at in range(0, width, step):
        cols = slice(at, at + step)
        down = jnp.concatenate([wd[:, cols], down_columns(other, at, step)], axis=0)
        part = jnp.dot(inner, down, preferred_element_type=F32)
        store_parts(part, cols, keep1, send1, keep2, send2)


def bwd_kernel(
    c1, qr1, c2, pr2, wg, wu, wd, other, _, keep1, send1, keep2, send2, rows, cots
):
    width = rows.shape[1]
    gather_rows((c1, qr1, c2, pr2), width, width, rows)
    gather_rows((c1, qr1, c2, pr2), 2 * width, width, cots)
    back = []
    products = None
    sources = (
        (wg[...], wu[...], wd[...]),
        (other[0:width, :], other[width : 2 * width, :], down_columns(other, 0, width)),
    )
    for gate_w, up_w, down_w in sources:
        gate, up = hidden(rows[...], gate_w, up_w)
        d_inner = lax.dot_general(cots[...], down_w, NT, preferred_element_type=F32)
        sig = jax.nn.sigmoid(gate)
        silu = gate * sig
        inner = (silu * up).astype(BF16).astype(F32)
        d_gate = (d_inner * up * sig * (1.0 + gate * (1.0 - sig))).astype(BF16)
        d_up = (d_inner * silu).astype(BF16)
        back.append(jnp.concatenate([d_gate, d_up], axis=1))
        product = inner * d_inner
        products = product if products is None else products + product
    count = products.shape[0]
    high = products.astype(BF16)
    low = (products - high.astype(F32)).astype(BF16)
    ones = jnp.ones((16, 128), BF16)
    grads = lax.dot_general(ones, high, NT, preferred_element_type=F32)
    grads = grads + lax.dot_general(ones, low, NT, preferred_element_type=F32)
    row = lax.broadcasted_iota(jnp.int32, (count, count), 0)
    col = lax.broadcasted_iota(jnp.int32, (count, count), 1)
    held = (row // SLOT == col // SLOT) & (row % SLOT == SLOT - 2)
    spread = jnp.where(held, grads[0:1, :], 0.0).astype(BF16)
    at_row = lax.broadcasted_iota(jnp.int32, (count, 128), 0)
    at_col = lax.broadcasted_iota(jnp.int32, (count, 128), 1)
    pick = (at_row % SLOT == at_col).astype(F32).astype(BF16)
    grad_rows = jnp.dot(spread, pick, preferred_element_type=F32)
    step = 512
    for at in range(0, width, step):
        cols = slice(at, at + step)
        there = slice(width + at, width + at + step)
        weights = (
            jnp.concatenate([wg[cols, :], wu[cols, :]], axis=1),
            jnp.concatenate([other[cols, :], other[there, :]], axis=1),
        )
        part = None
        for grad, weight in zip(back, weights):
            term = lax.dot_general(grad, weight, NT, preferred_element_type=F32)
            part = term if part is None else part + term
        if at == 0:
            part = jnp.concatenate([part[:, :128] + grad_rows, part[:, 128:]], axis=1)
        store_parts(part, cols, keep1, send1, keep2, send2)


def mixed_rows(masks, weight_ref, parts):
    weights = weight_ref[...]
    spread = jnp.where(masks[0][0], weights[:, 0:1], 0.0) + jnp.where(
        masks[1][0], weights[:, 1:2], 0.0
    )
    high = spread.astype(BF16)
    rest = spread - high.astype(F32)
    middle = rest.astype(BF16)
    low = (rest - middle.astype(F32)).astype(BF16)
    total = None
    for j, part in enumerate(parts):
        at = slice(j * SLOT, (j + 1) * SLOT)
        for piece in (high, middle, low):
            term = jnp.dot(piece[:, at], part, preferred_element_type=F32)
            total = term if total is None else total + term
    return total


def last_kernel(
    info_ref, xa_ref, ra_ref, wa_ref, x_ref, route_ref, weight_ref, cot_ref, gain_ref, *rest
):
    width = x_ref.shape[1]
    arrived = [rest[0], rest[1], rest[3], rest[2]]
    parts_a = [ref[:, :width] for ref in arrived]
    parts = [ref[:, width:] for ref in arrived]
    out_a_ref, out_ref, grad_ref = rest[4:]
    mixed = mixed_rows(slot_masks(info_ref, ra_ref), wa_ref, parts_a)
    out_a_ref[...] = (xa_ref[...].astype(F32) + mixed).astype(BF16)
    masks = slot_masks(info_ref, route_ref)
    d_normed = mixed_rows(masks, weight_ref, parts)
    unit, scale = normalized(x_ref[...])
    q_term = d_normed * gain_ref[...]
    mean = jnp.mean(q_term * unit, axis=-1, keepdims=True)
    d_input = cot_ref[...].astype(F32) + scale * (q_term - unit * mean)
    out_ref[...] = d_input.astype(BF16)
    tokens = x_ref.shape[0]
    lanes = lax.broadcasted_iota(jnp.int32, (tokens, 128), 1)
    grads = []
    for _, rel, rank in masks:
        held = jnp.zeros((tokens, 128), F32)
        for j, part in enumerate(parts):
            row = part[:, :128].astype(F32)[SLOT - 2 : SLOT - 1, :]
            held = held + jnp.where(rel == j, row, 0.0)
        grads.append(jnp.sum(jnp.where(lanes == rank, held, 0.0), axis=1, keepdims=True))
    pair = lax.broadcasted_iota(jnp.int32, (tokens, 2), 1)
    grad_ref[...] = jnp.where(pair == 0, grads[0], grads[1]).astype(BF16)


def spread_rows(own, a, b, c):
    got_a, got_b, got_c = hop(a, HOP_A), hop(b, HOP_B), hop(c, HOP_C)
    half1 = jnp.concatenate([got_b, got_c], axis=0)
    half2 = jnp.concatenate([own, got_a], axis=0)
    p1 = hop(half1, HOP_X1)
    q2 = hop(half2, HOP_X3)
    c1 = jnp.concatenate([half1, p1], axis=0)
    c2 = jnp.concatenate([half2, q2], axis=0)
    return c1, hop(c1, HOP_X3), c2, hop(c2, HOP_X1)


def return_x(keep1, send1, keep2, send2):
    sum1 = keep1 + hop(send1, HOP_X3).astype(F32)
    sum2 = keep2 + hop(send2, HOP_X1).astype(F32)
    full1 = sum1[:32] + hop(sum1[32:].astype(BF16), HOP_X1).astype(F32)
    full2 = sum2[:32] + hop(sum2[32:].astype(BF16), HOP_X3).astype(F32)
    return full1.astype(BF16), full2.astype(BF16)


def return_z(full1, full2):
    back_c = hop(full2[SLOT:], HOP_C)
    back_b = hop(full2[:SLOT], HOP_B_BACK)
    back_a = hop(full1[SLOT:], HOP_A)
    return full1[:SLOT], back_a, back_c, back_b


def body(
    act_fwd,
    route_fwd,
    weight_fwd,
    act_bwd,
    route_bwd,
    weight_bwd,
    cot_bwd,
    norm_gain,
    w_gate,
    w_up,
    w_down,
):
    tokens, width = act_fwd.shape[1:]
    index = lax.axis_index("expert")
    info = jnp.stack([index >> 3, (index >> 2) & 1]).astype(jnp.int32)
    weights = (w_gate[0, 0], w_up[0, 0], w_down[0, 0])
    units = w_down.shape[2]
    (merged,) = kernel_call(merge_kernel, [((3 * width, units), BF16)], 3, info=False)(*weights)
    other = hop(merged, HOP_W)
    wide = [((SLOT, 3 * width), BF16)] * 4
    sent = kernel_call(pack_kernel, wide, 6)(
        info, act_fwd[0], route_fwd[0], act_bwd[0], route_bwd[0], cot_bwd[0], norm_gain
    )
    rows = spread_rows(*sent)
    outs = [((64, width), F32), ((64, width), BF16)] * 2
    scratch = pltpu.VMEM((256, width), BF16)
    part_a = kernel_call(fwd_kernel, outs, 8, [scratch], info=False)(*rows, *weights, other)
    part_b = kernel_call(bwd_kernel, outs, 9, [scratch] * 2, info=False)(
        *rows, *weights, other, part_a[1]
    )
    halves = zip(return_x(*part_a), return_x(*part_b))
    back = return_z(*[jnp.concatenate(pair, axis=1) for pair in halves])
    layer_out, d_input, gate_grad = kernel_call(
        last_kernel, [((tokens, width), BF16)] * 2 + [((tokens, 2), BF16)], 12
    )(
        info,
        act_fwd[0],
        route_fwd[0],
        weight_fwd[0],
        act_bwd[0],
        route_bwd[0],
        weight_bwd[0],
        cot_bwd[0],
        norm_gain,
        *back,
    )
    act_next = shifted(layer_out, "section", 1)
    cot_next = shifted(d_input, "section", -1)
    return (act_next[None], cot_next[None], gate_grad[None])


def solution(mesh):
    return jax.shard_map(
        body,
        mesh=mesh,
        in_specs=(
            P("section", "expert", None),
            P("section", "expert", None),
            P("section", "expert", None),
            P("section", "expert", None),
            P("section", "expert", None),
            P("section", "expert", None),
            P("section", "expert", None),
            P("section", None),
            P("section", "expert", None, None),
            P("section", "expert", None, None),
            P("section", "expert", None, None),
        ),
        out_specs=(
            P("section", "expert", None),
            P("section", "expert", None),
            P("section", "expert", None),
        ),
        check_vma=False,
    )
```

```python
import jax
import jax.numpy as jnp
from jax import lax
from jax.experimental import pallas as pl
from jax.experimental.pallas import tpu as pltpu
from jax.sharding import PartitionSpec as P

EXPERTS = 4
GRID_X = 4
GRID_Z = 8
SLOT = 16
CAP = 14
F32 = jnp.float32
BF16 = jnp.bfloat16
NT = (((1,), (1,)), ((), ()))
TN = (((0,), (0,)), ((), ()))


def expert_pairs(move):
    pairs = []
    for z in range(GRID_Z):
        for x in range(GRID_X):
            to_z, to_x = move(z, x)
            pairs.append((z * GRID_X + x, to_z % GRID_Z * GRID_X + to_x))
    return pairs


def signed(z, even, odd):
    return z + (odd if z % 2 else even)


HOP_W = expert_pairs(lambda z, x: (z ^ 1, x))
HOP_A = expert_pairs(lambda z, x: (signed(z, -1, 1), x))
HOP_B = expert_pairs(lambda z, x: (signed(z, 2, -2), x))
HOP_B_BACK = expert_pairs(lambda z, x: (signed(z, -2, 2), x))
HOP_C = expert_pairs(lambda z, x: (signed(z, -3, 3), x))
HOP_X1 = expert_pairs(lambda z, x: (z, x ^ 1))
HOP_X3 = expert_pairs(lambda z, x: (z, x ^ 3))


def hop(value, pairs):
    return lax.ppermute(value, "expert", pairs)


def shifted(value, axis, by):
    devices = lax.axis_size(axis)
    pairs = [(i, i + by) for i in range(devices) if 0 <= i + by < devices]
    return lax.ppermute(value, axis, pairs)


def kernel_call(kernel, outs, n_in, scratch=(), info=True, limit=32):
    smem = pl.BlockSpec(memory_space=pltpu.SMEM)
    vmem = pl.BlockSpec(memory_space=pltpu.VMEM)
    return pl.pallas_call(
        kernel,
        out_shape=[jax.ShapeDtypeStruct(s, d) for s, d in outs],
        in_specs=[smem] * info + [vmem] * n_in,
        out_specs=[vmem] * len(outs),
        scratch_shapes=list(scratch),
        compiler_params=pltpu.CompilerParams(vmem_limit_bytes=limit * 1024 * 1024),
    )


def slot_places(info_ref, route_ref):
    tokens = route_ref.shape[0]
    own, odd = info_ref[0], info_ref[1]
    lanes = lax.broadcasted_iota(jnp.int32, (tokens, 128), 1)
    route = route_ref[...]
    named = [(route[:, k : k + 1] == lanes).astype(F32) for k in range(2)]
    row = lax.broadcasted_iota(jnp.int32, (tokens, tokens), 0)
    col = lax.broadcasted_iota(jnp.int32, (tokens, tokens), 1)
    earlier = (col < row).astype(F32).astype(BF16)
    counts = jnp.dot(earlier, (named[0] + named[1]).astype(BF16), preferred_element_type=F32)
    out = []
    for k in range(2):
        rank = jnp.sum(named[k] * counts, axis=1, keepdims=True).astype(jnp.int32)
        away = (route[:, k : k + 1] - own) & 3
        side = jnp.where((away == 3) == (odd == 0), 1, 2)
        rel = jnp.where(away == 0, 0, jnp.where(away == 2, 3, side))
        out.append((rel, rank))
    return out


def slot_masks(info_ref, route_ref):
    tokens = route_ref.shape[0]
    slots = lax.broadcasted_iota(jnp.int32, (tokens, 4 * SLOT), 1)
    places = slot_places(info_ref, route_ref)
    return [(slots == rel * SLOT + rank, rel, rank) for rel, rank in places]


def split(index, size):
    whole = sum((index >= size * i).astype(jnp.int32) for i in (1, 2, 3))
    return whole, index - size * whole


def normalized(x):
    values = x.astype(F32)
    scale = lax.rsqrt(jnp.mean(values * values, axis=-1, keepdims=True) + 1e-06)
    return values * scale, scale


def pack_kernel(info_ref, xa_ref, ra_ref, xb_ref, rb_ref, cot_ref, gain_ref, _, *outs):
    tokens, width = xa_ref.shape
    quarter = width // 4
    lane = lax.broadcasted_iota(jnp.int32, (tokens, 16 * CAP), 1)
    block, rest = split(lane, 4 * CAP)
    part, slot = split(rest, CAP)
    held = []
    for route_ref in (ra_ref, rb_ref):
        (rel0, rank0), (rel1, rank1) = slot_places(info_ref, route_ref)
        held.append(
            ((block == rel0) & (slot == rank0)) | ((block == rel1) & (slot == rank1))
        )
    gain = gain_ref[...]
    normed_a = (normalized(xa_ref[...])[0] * gain).astype(BF16)
    normed_b = (normalized(xb_ref[...])[0] * gain).astype(BF16)
    sources = ((held[0], normed_a), (held[1], normed_b), (held[1], cot_ref[...]))
    for i, (mask, rows) in enumerate(sources):
        packed = None
        for q in range(4):
            place = (mask & (part == q)).astype(F32).astype(BF16)
            chunk = rows[:, q * quarter : (q + 1) * quarter]
            term = lax.dot_general(place, chunk, TN, preferred_element_type=F32)
            packed = term if packed is None else packed + term
        for j in range(4):
            piece = packed[4 * CAP * j : 4 * CAP * (j + 1)]
            outs[j][:, i * quarter : (i + 1) * quarter] = piece.astype(BF16)


def merge_kernel(wg, wu, out):
    width = wg.shape[0]
    out[0:width, :] = wg[...]
    out[width : 2 * width, :] = wu[...]


def near_kernel(half, got, _, out):
    count = half.shape[0]
    out[0:count, :] = half[...]
    out[count : 2 * count, :] = got[...]


def hidden(rows, wg, wu):
    both = jnp.dot(rows, jnp.concatenate([wg, wu], axis=1), preferred_element_type=F32)
    return both[:, :128], both[:, 128:]


def unpack_places():
    row = lax.broadcasted_iota(jnp.int32, (16 * SLOT, 16 * CAP), 0)
    col = lax.broadcasted_iota(jnp.int32, (16 * SLOT, 16 * CAP), 1)
    block, rest = split(col, 4 * CAP)
    part, slot = split(rest, CAP)
    return (row == part * 4 * SLOT + block * SLOT + slot).astype(F32).astype(BF16)


def gather_rows(refs, which, places, scratch):
    quarter = scratch.shape[1] // 4
    count = 4 * SLOT
    for i, ref in enumerate(refs):
        blocks = ref[:, which * quarter : (which + 1) * quarter]
        rows = jnp.dot(places, blocks, preferred_element_type=F32).astype(BF16)
        for q in range(4):
            cols = slice(q * quarter, (q + 1) * quarter)
            scratch[count * i : count * (i + 1), cols] = rows[count * q : count * (q + 1)]


def store_parts(part, cols, keep1, send1, keep2, send2):
    for ref, starts in ((keep1, (128, 192)), (send1, (160, 224)), (keep2, (0, 64)), (send2, (32, 96))):
        for i, start in enumerate(starts):
            ref[32 * i : 32 * (i + 1), cols] = part[start : start + 32].astype(ref.dtype)


def fwd_kernel(c1, qr1, c2, pr2, wg, wu, wd, other, vd, keep1, send1, keep2, send2, rows):
    width = rows.shape[1]
    gather_rows((c1, qr1, c2, pr2), 0, unpack_places(), rows)
    inner = []
    for weights in ((wg[...], wu[...]), (other[0:width, :], other[width : 2 * width, :])):
        gate, up = hidden(rows[...], *weights)
        inner.append((gate * jax.nn.sigmoid(gate) * up).astype(BF16))
    inner = jnp.concatenate(inner, axis=1)
    step = 512
    for at in range(0, width, step):
        cols = slice(at, at + step)
        down = jnp.concatenate([wd[:, cols], vd[:, cols]], axis=0)
        part = jnp.dot(inner, down, preferred_element_type=F32)
        store_parts(part, cols, keep1, send1, keep2, send2)


def bwd_kernel(
    c1, qr1, c2, pr2, wg, wu, wd, other, vd, _, keep1, send1, keep2, send2, rows, cots
):
    width = rows.shape[1]
    places = unpack_places()
    gather_rows((c1, qr1, c2, pr2), 1, places, rows)
    gather_rows((c1, qr1, c2, pr2), 2, places, cots)
    back = []
    products = None
    sources = (
        (wg[...], wu[...], wd[...]),
        (other[0:width, :], other[width : 2 * width, :], vd[...]),
    )
    for gate_w, up_w, down_w in sources:
        gate, up = hidden(rows[...], gate_w, up_w)
        d_inner = lax.dot_general(cots[...], down_w, NT, preferred_element_type=F32)
        sig = jax.nn.sigmoid(gate)
        silu = gate * sig
        inner = (silu * up).astype(BF16).astype(F32)
        d_gate = (d_inner * up * sig * (1.0 + gate * (1.0 - sig))).astype(BF16)
        d_up = (d_inner * silu).astype(BF16)
        back.append(jnp.concatenate([d_gate, d_up], axis=1))
        product = inner * d_inner
        products = product if products is None else products + product
    count = products.shape[0]
    high = products.astype(BF16)
    low = (products - high.astype(F32)).astype(BF16)
    ones = jnp.ones((16, 128), BF16)
    grads = lax.dot_general(ones, high, NT, preferred_element_type=F32)
    grads = grads + lax.dot_general(ones, low, NT, preferred_element_type=F32)
    row = lax.broadcasted_iota(jnp.int32, (count, count), 0)
    col = lax.broadcasted_iota(jnp.int32, (count, count), 1)
    held = (row // SLOT == col // SLOT) & (row % SLOT == SLOT - 2)
    spread = jnp.where(held, grads[0:1, :], 0.0).astype(BF16)
    at_row = lax.broadcasted_iota(jnp.int32, (count, 128), 0)
    at_col = lax.broadcasted_iota(jnp.int32, (count, 128), 1)
    pick = (at_row % SLOT == at_col).astype(F32).astype(BF16)
    grad_rows = jnp.dot(spread, pick, preferred_element_type=F32)
    step = 512
    for at in range(0, width, step):
        cols = slice(at, at + step)
        there = slice(width + at, width + at + step)
        weights = (
            jnp.concatenate([wg[cols, :], wu[cols, :]], axis=1),
            jnp.concatenate([other[cols, :], other[there, :]], axis=1),
        )
        part = None
        for grad, weight in zip(back, weights):
            term = lax.dot_general(grad, weight, NT, preferred_element_type=F32)
            part = term if part is None else part + term
        if at == 0:
            part = jnp.concatenate([part[:, :128] + grad_rows, part[:, 128:]], axis=1)
        store_parts(part, cols, keep1, send1, keep2, send2)


def mixed_rows(masks, weight_ref, parts):
    weights = weight_ref[...]
    spread = jnp.where(masks[0][0], weights[:, 0:1], 0.0) + jnp.where(
        masks[1][0], weights[:, 1:2], 0.0
    )
    high = spread.astype(BF16)
    rest = spread - high.astype(F32)
    middle = rest.astype(BF16)
    low = (rest - middle.astype(F32)).astype(BF16)
    total = None
    for j, part in enumerate(parts):
        at = slice(j * SLOT, (j + 1) * SLOT)
        for piece in (high, middle, low):
            term = jnp.dot(piece[:, at], part, preferred_element_type=F32)
            total = term if total is None else total + term
    return total


def last_kernel(
    info_ref, xa_ref, ra_ref, wa_ref, x_ref, route_ref, weight_ref, cot_ref, gain_ref, *rest
):
    width = x_ref.shape[1]
    arrived = [rest[0], rest[1], rest[3], rest[2]]
    parts_a = [ref[:, :width] for ref in arrived]
    parts = [ref[:, width:] for ref in arrived]
    out_a_ref, out_ref, grad_ref = rest[4:]
    mixed = mixed_rows(slot_masks(info_ref, ra_ref), wa_ref, parts_a)
    out_a_ref[...] = (xa_ref[...].astype(F32) + mixed).astype(BF16)
    masks = slot_masks(info_ref, route_ref)
    d_normed = mixed_rows(masks, weight_ref, parts)
    unit, scale = normalized(x_ref[...])
    q_term = d_normed * gain_ref[...]
    mean = jnp.mean(q_term * unit, axis=-1, keepdims=True)
    d_input = cot_ref[...].astype(F32) + scale * (q_term - unit * mean)
    out_ref[...] = d_input.astype(BF16)
    tokens = x_ref.shape[0]
    lanes = lax.broadcasted_iota(jnp.int32, (tokens, 128), 1)
    grads = []
    for _, rel, rank in masks:
        held = jnp.zeros((tokens, 128), F32)
        for j, part in enumerate(parts):
            row = part[:, :128].astype(F32)[SLOT - 2 : SLOT - 1, :]
            held = held + jnp.where(rel == j, row, 0.0)
        grads.append(jnp.sum(jnp.where(lanes == rank, held, 0.0), axis=1, keepdims=True))
    pair = lax.broadcasted_iota(jnp.int32, (tokens, 2), 1)
    grad_ref[...] = jnp.where(pair == 0, grads[0], grads[1]).astype(BF16)


def spread_rows(own, a, b, c, other):
    got_a, got_b, got_c = hop(a, HOP_A), hop(b, HOP_B), hop(c, HOP_C)
    half1 = jnp.concatenate([got_b, got_c], axis=0)
    half2 = jnp.concatenate([own, got_a], axis=0)
    p1 = hop(half1, HOP_X1)
    q2 = hop(half2, HOP_X3)
    vmem = pl.BlockSpec(memory_space=pltpu.VMEM)
    c1 = pl.pallas_call(
        near_kernel,
        out_shape=jax.ShapeDtypeStruct((2 * half1.shape[0], half1.shape[1]), BF16),
        in_specs=[vmem, vmem, pl.BlockSpec(memory_space=pl.ANY)],
        out_specs=vmem,
    )(half1, p1, other)
    c2 = jnp.concatenate([half2, q2], axis=0)
    return c1, hop(c1, HOP_X3), c2, hop(c2, HOP_X1)


def return_x(keep1, send1, keep2, send2):
    sum1 = keep1 + hop(send1, HOP_X3).astype(F32)
    sum2 = keep2 + hop(send2, HOP_X1).astype(F32)
    full1 = sum1[:32] + hop(sum1[32:].astype(BF16), HOP_X1).astype(F32)
    full2 = sum2[:32] + hop(sum2[32:].astype(BF16), HOP_X3).astype(F32)
    return full1.astype(BF16), full2.astype(BF16)


def return_z(full1, full2):
    back_c = hop(full2[SLOT:], HOP_C)
    back_b = hop(full2[:SLOT], HOP_B_BACK)
    back_a = hop(full1[SLOT:], HOP_A)
    return full1[:SLOT], back_a, back_c, back_b


def body(
    act_fwd,
    route_fwd,
    weight_fwd,
    act_bwd,
    route_bwd,
    weight_bwd,
    cot_bwd,
    norm_gain,
    w_gate,
    w_up,
    w_down,
):
    tokens, width = act_fwd.shape[1:]
    index = lax.axis_index("expert")
    info = jnp.stack([index >> 3, (index >> 2) & 1]).astype(jnp.int32)
    weights = (w_gate[0, 0], w_up[0, 0], w_down[0, 0])
    units = w_down.shape[2]
    (merged,) = kernel_call(merge_kernel, [((2 * width, units), BF16)], 2, info=False)(*weights[:2])
    other = hop(merged, HOP_W)
    other_down = hop(weights[2], HOP_W)
    wide = [((4 * CAP, 3 * width // 4), BF16)] * 4
    sent = kernel_call(pack_kernel, wide, 7)(
        info, act_fwd[0], route_fwd[0], act_bwd[0], route_bwd[0], cot_bwd[0], norm_gain, merged
    )
    rows = spread_rows(*sent, other)
    weights += (other, other_down)
    outs = [((64, width), F32), ((64, width), BF16)] * 2
    scratch = pltpu.VMEM((256, width), BF16)
    part_a = kernel_call(fwd_kernel, outs, 9, [scratch], info=False)(*rows, *weights)
    part_b = kernel_call(bwd_kernel, outs, 10, [scratch] * 2, info=False)(
        *rows, *weights, part_a[1]
    )
    halves = zip(return_x(*part_a), return_x(*part_b))
    back = return_z(*[jnp.concatenate(pair, axis=1) for pair in halves])
    layer_out, d_input, gate_grad = kernel_call(
        last_kernel, [((tokens, width), BF16)] * 2 + [((tokens, 2), BF16)], 12
    )(
        info,
        act_fwd[0],
        route_fwd[0],
        weight_fwd[0],
        act_bwd[0],
        route_bwd[0],
        weight_bwd[0],
        cot_bwd[0],
        norm_gain,
        *back,
    )
    act_next = shifted(layer_out, "section", 1)
    cot_next = shifted(d_input, "section", -1)
    return (act_next[None], cot_next[None], gate_grad[None])


def solution(mesh):
    return jax.shard_map(
        body,
        mesh=mesh,
        in_specs=(
            P("section", "expert", None),
            P("section", "expert", None),
            P("section", "expert", None),
            P("section", "expert", None),
            P("section", "expert", None),
            P("section", "expert", None),
            P("section", "expert", None),
            P("section", None),
            P("section", "expert", None, None),
            P("section", "expert", None, None),
            P("section", "expert", None, None),
        ),
        out_specs=(
            P("section", "expert", None),
            P("section", "expert", None),
            P("section", "expert", None),
        ),
        check_vma=False,
    )
```

```python
import jax
import jax.numpy as jnp
from jax import lax
from jax.experimental import pallas as pl
from jax.experimental.pallas import tpu as pltpu
from jax.sharding import PartitionSpec as P

EXPERTS = 4
GRID_X = 4
GRID_Z = 8
SLOT = 16
F32 = jnp.float32
BF16 = jnp.bfloat16
NT = (((1,), (1,)), ((), ()))
TN = (((0,), (0,)), ((), ()))


def expert_pairs(move):
    pairs = []
    for z in range(GRID_Z):
        for x in range(GRID_X):
            to_z, to_x = move(z, x)
            pairs.append((z * GRID_X + x, to_z % GRID_Z * GRID_X + to_x))
    return pairs


def signed(z, even, odd):
    return z + (odd if z % 2 else even)


HOP_W = expert_pairs(lambda z, x: (z ^ 1, x))
HOP_A = expert_pairs(lambda z, x: (signed(z, -1, 1), x))
HOP_B = expert_pairs(lambda z, x: (signed(z, 2, -2), x))
HOP_B_BACK = expert_pairs(lambda z, x: (signed(z, -2, 2), x))
HOP_C = expert_pairs(lambda z, x: (signed(z, -3, 3), x))
HOP_X1 = expert_pairs(lambda z, x: (z, x ^ 1))
HOP_X3 = expert_pairs(lambda z, x: (z, x ^ 3))


def hop(value, pairs):
    return lax.ppermute(value, "expert", pairs)


def shifted(value, axis, by):
    devices = lax.axis_size(axis)
    pairs = [(i, i + by) for i in range(devices) if 0 <= i + by < devices]
    return lax.ppermute(value, axis, pairs)


def kernel_call(kernel, outs, n_in, scratch=(), info=True, limit=32):
    smem = pl.BlockSpec(memory_space=pltpu.SMEM)
    vmem = pl.BlockSpec(memory_space=pltpu.VMEM)
    return pl.pallas_call(
        kernel,
        out_shape=[jax.ShapeDtypeStruct(s, d) for s, d in outs],
        in_specs=[smem] * info + [vmem] * n_in,
        out_specs=[vmem] * len(outs),
        scratch_shapes=list(scratch),
        compiler_params=pltpu.CompilerParams(vmem_limit_bytes=limit * 1024 * 1024),
    )


def local_copy_call(kernel, outs, n_near, scratch):
    n_far = 4 if n_near else 3
    smem = pl.BlockSpec(memory_space=pltpu.SMEM)
    vmem = pl.BlockSpec(memory_space=pltpu.VMEM)
    near = ([smem] + [vmem] * (n_near - 1)) if n_near else []
    return pl.pallas_call(
        kernel,
        out_shape=[jax.ShapeDtypeStruct(s, d) for s, d in outs],
        in_specs=near + [pl.BlockSpec(memory_space=pl.ANY)] * n_far,
        out_specs=[vmem] * len(outs),
        scratch_shapes=scratch,
        compiler_params=pltpu.CompilerParams(vmem_limit_bytes=60 * 1024 * 1024),
    )


def columns(ref):
    count = ref.shape[1]
    row = lax.broadcasted_iota(jnp.int32, (count, count), 0)
    col = lax.broadcasted_iota(jnp.int32, (count, count), 1)
    values = ref[...].astype(F32)
    return [
        jnp.sum(jnp.where(row == col, values[k : k + 1, :], 0.0), axis=1, keepdims=True)
        for k in range(2)
    ]


def slot_masks(info_ref, route_ref):
    tokens = route_ref.shape[1]
    own, odd = info_ref[0], info_ref[1]
    lanes = lax.broadcasted_iota(jnp.int32, (tokens, 128), 1)
    route = [column.astype(jnp.int32) for column in columns(route_ref)]
    named = [(route[k] == lanes).astype(F32) for k in range(2)]
    row = lax.broadcasted_iota(jnp.int32, (tokens, tokens), 0)
    col = lax.broadcasted_iota(jnp.int32, (tokens, tokens), 1)
    earlier = (col < row).astype(BF16)
    counts = jnp.dot(earlier, (named[0] + named[1]).astype(BF16), preferred_element_type=F32)
    out = []
    for k in range(2):
        rank = jnp.sum(named[k] * counts, axis=1, keepdims=True).astype(jnp.int32)
        away = (route[k] - own) & 3
        side = jnp.where((away == 3) == (odd == 0), 1, 2)
        rel = jnp.where(away == 0, 0, jnp.where(away == 2, 3, side))
        slots = lax.broadcasted_iota(jnp.int32, (tokens, 4 * SLOT), 1)
        out.append((slots == rel * SLOT + rank, rel, rank))
    return out


def normalized(x):
    values = x.astype(F32)
    scale = lax.rsqrt(jnp.mean(values * values, axis=-1, keepdims=True) + 1e-06)
    return values * scale, scale


def pack_kernel(info_ref, ra_ref, rb_ref, xa, gain_in, xb, cot, *rest):
    outs, (xa_ref, gain_ref, xb_ref, cot_ref, sems) = rest[:4], rest[4:]
    width = xa.shape[1]
    moves = ((xa, xa_ref), (gain_in, gain_ref), (xb, xb_ref), (cot, cot_ref))
    copies = [pltpu.make_async_copy(*move, sems.at[i]) for i, move in enumerate(moves)]
    for copy in copies:
        copy.start()
    places = []
    for route_ref in (ra_ref, rb_ref):
        masks = slot_masks(info_ref, route_ref)
        places.append((masks[0][0] | masks[1][0]).astype(F32).astype(BF16))
    for copy in copies:
        copy.wait()
    gain = gain_ref[...]
    normed_a = (normalized(xa_ref[...])[0] * gain).astype(BF16)
    normed_b = (normalized(xb_ref[...])[0] * gain).astype(BF16)
    sources = ((places[0], normed_a), (places[1], normed_b), (places[1], cot_ref[...]))
    for i, (place, rows) in enumerate(sources):
        packed = lax.dot_general(place, rows, TN, preferred_element_type=F32).astype(BF16)
        for j in range(4):
            outs[j][:, i * width : (i + 1) * width] = packed[j * SLOT : (j + 1) * SLOT]


def merge_kernel(wg, wu, wd, out, down, sems):
    width, units = wg.shape
    moves = ((wd, down), (wg, out.at[pl.ds(0, width)]), (wu, out.at[pl.ds(width, width)]))
    copies = [pltpu.make_async_copy(*move, sems.at[i]) for i, move in enumerate(moves)]
    for copy in copies:
        copy.start()
    copies[0].wait()
    for at in range(0, width, units):
        out[2 * width + at : 2 * width + at + units, :] = down[:, at : at + units]
    copies[1].wait()
    copies[2].wait()


def hidden(rows, wg, wu):
    both = jnp.dot(rows, jnp.concatenate([wg, wu], axis=1), preferred_element_type=F32)
    return both[:, :128], both[:, 128:]


def down_columns(merged, at, count):
    width = merged.shape[0] // 3
    starts = range(2 * width + at, 2 * width + at + count, 128)
    return jnp.concatenate([merged[start : start + 128, :] for start in starts], axis=1)


def gather_rows(refs, at, width, scratch):
    for i, ref in enumerate(refs):
        scratch[64 * i : 64 * (i + 1), :] = ref[:, at : at + width]


def store_parts(part, cols, keep1, send1, keep2, send2):
    for ref, starts in ((keep1, (128, 160)), (send1, (192, 224)), (keep2, (0, 32)), (send2, (64, 96))):
        for i, start in enumerate(starts):
            ref[32 * i : 32 * (i + 1), cols] = part[start : start + 32].astype(ref.dtype)


def fwd_kernel(c1, qr1, c2, pr2, wg, wu, wd, other, keep1, send1, keep2, send2, rows):
    width = rows.shape[1]
    gather_rows((c1, qr1, c2, pr2), 0, width, rows)
    inner = []
    for weights in ((wg[...], wu[...]), (other[0:width, :], other[width : 2 * width, :])):
        gate, up = hidden(rows[...], *weights)
        inner.append((gate * jax.nn.sigmoid(gate) * up).astype(BF16))
    inner = jnp.concatenate(inner, axis=1)
    step = 512
    for at in range(0, width, step):
        cols = slice(at, at + step)
        down = jnp.concatenate([wd[:, cols], down_columns(other, at, step)], axis=0)
        part = jnp.dot(inner, down, preferred_element_type=F32)
        store_parts(part, cols, keep1, send1, keep2, send2)


def bwd_kernel(
    c1, qr1, c2, pr2, wg, wu, wd, other, _, keep1, send1, keep2, send2, rows, cots
):
    width = rows.shape[1]
    gather_rows((c1, qr1, c2, pr2), width, width, rows)
    gather_rows((c1, qr1, c2, pr2), 2 * width, width, cots)
    back = []
    products = None
    sources = (
        (wg[...], wu[...], wd[...]),
        (other[0:width, :], other[width : 2 * width, :], down_columns(other, 0, width)),
    )
    for gate_w, up_w, down_w in sources:
        gate, up = hidden(rows[...], gate_w, up_w)
        d_inner = lax.dot_general(cots[...], down_w, NT, preferred_element_type=F32)
        sig = jax.nn.sigmoid(gate)
        silu = gate * sig
        inner = (silu * up).astype(BF16).astype(F32)
        d_gate = (d_inner * up * sig * (1.0 + gate * (1.0 - sig))).astype(BF16)
        d_up = (d_inner * silu).astype(BF16)
        back.append(jnp.concatenate([d_gate, d_up], axis=1))
        product = inner * d_inner
        products = product if products is None else products + product
    count = products.shape[0]
    high = products.astype(BF16)
    low = (products - high.astype(F32)).astype(BF16)
    ones = jnp.ones((16, 128), BF16)
    grads = lax.dot_general(ones, high, NT, preferred_element_type=F32)
    grads = grads + lax.dot_general(ones, low, NT, preferred_element_type=F32)
    row = lax.broadcasted_iota(jnp.int32, (count, count), 0)
    col = lax.broadcasted_iota(jnp.int32, (count, count), 1)
    held = (row // SLOT == col // SLOT) & (row % SLOT == SLOT - 2)
    spread = jnp.where(held, grads[0:1, :], 0.0).astype(BF16)
    at_row = lax.broadcasted_iota(jnp.int32, (count, 128), 0)
    at_col = lax.broadcasted_iota(jnp.int32, (count, 128), 1)
    pick = (at_row % SLOT == at_col).astype(F32).astype(BF16)
    grad_rows = jnp.dot(spread, pick, preferred_element_type=F32)
    step = 512
    for at in range(0, width, step):
        cols = slice(at, at + step)
        there = slice(width + at, width + at + step)
        weights = (
            jnp.concatenate([wg[cols, :], wu[cols, :]], axis=1),
            jnp.concatenate([other[cols, :], other[there, :]], axis=1),
        )
        part = None
        for grad, weight in zip(back, weights):
            term = lax.dot_general(grad, weight, NT, preferred_element_type=F32)
            part = term if part is None else part + term
        if at == 0:
            part = jnp.concatenate([part[:, :128] + grad_rows, part[:, 128:]], axis=1)
        store_parts(part, cols, keep1, send1, keep2, send2)


def mixed_rows(masks, weight_ref, parts):
    weights = columns(weight_ref)
    spread = jnp.where(masks[0][0], weights[0], 0.0) + jnp.where(masks[1][0], weights[1], 0.0)
    high = spread.astype(BF16)
    rest = spread - high.astype(F32)
    middle = rest.astype(BF16)
    low = (rest - middle.astype(F32)).astype(BF16)
    tokens = spread.shape[0]
    pieces = jnp.concatenate([high, middle, low], axis=0)
    product = jnp.dot(pieces, jnp.concatenate(parts, axis=0), preferred_element_type=F32)
    return product[:tokens] + product[tokens : 2 * tokens] + product[2 * tokens :]


def last_kernel(
    info_ref, xa_ref, ra_ref, wa_ref, x_ref, route_ref, weight_ref, cot_ref, gain_ref, *rest
):
    width = x_ref.shape[1]
    arrived = [rest[0], rest[1], rest[3], rest[2]]
    parts_a = [ref[:, :width] for ref in arrived]
    parts = [ref[:, width:] for ref in arrived]
    out_a_ref, out_ref, grad_ref = rest[4:]
    mixed = mixed_rows(slot_masks(info_ref, ra_ref), wa_ref, parts_a)
    out_a_ref[...] = (xa_ref[...].astype(F32) + mixed).astype(BF16)
    masks = slot_masks(info_ref, route_ref)
    d_normed = mixed_rows(masks, weight_ref, parts)
    unit, scale = normalized(x_ref[...])
    q_term = d_normed * gain_ref[...]
    mean = jnp.mean(q_term * unit, axis=-1, keepdims=True)
    d_input = cot_ref[...].astype(F32) + scale * (q_term - unit * mean)
    out_ref[...] = d_input.astype(BF16)
    tokens = x_ref.shape[0]
    lanes = lax.broadcasted_iota(jnp.int32, (tokens, 128), 1)
    grads = []
    for _, rel, rank in masks:
        held = jnp.zeros((tokens, 128), F32)
        for j, part in enumerate(parts):
            row = part[:, :128].astype(F32)[SLOT - 2 : SLOT - 1, :]
            held = held + jnp.where(rel == j, row, 0.0)
        grads.append(jnp.sum(jnp.where(lanes == rank, held, 0.0), axis=1, keepdims=True))
    pair = lax.broadcasted_iota(jnp.int32, (tokens, 2), 1)
    grad_ref[...] = jnp.where(pair == 0, grads[0], grads[1]).astype(BF16)


def spread_rows(own, a, b, c):
    got_a, got_b, got_c = hop(a, HOP_A), hop(b, HOP_B), hop(c, HOP_C)
    half1 = jnp.concatenate([got_b, got_c], axis=0)
    half2 = jnp.concatenate([own, got_a], axis=0)
    q1 = hop(half1, HOP_X3)
    p2 = hop(half2, HOP_X1)
    c1 = jnp.concatenate([half1, q1], axis=0)
    c2 = jnp.concatenate([half2, p2], axis=0)
    return c1, hop(c1, HOP_X1), c2, hop(c2, HOP_X3)


def return_x(keep1, send1, keep2, send2):
    sum1 = keep1 + hop(send1, HOP_X3).astype(F32)
    sum2 = keep2 + hop(send2, HOP_X1).astype(F32)
    full1 = sum1[:32] + hop(sum1[32:].astype(BF16), HOP_X1).astype(F32)
    full2 = sum2[:32] + hop(sum2[32:].astype(BF16), HOP_X3).astype(F32)
    return full1.astype(BF16), full2.astype(BF16)


def return_z(full1, full2):
    back_c = hop(full2[SLOT:], HOP_C)
    back_b = hop(full2[:SLOT], HOP_B_BACK)
    back_a = hop(full1[SLOT:], HOP_A)
    return full1[:SLOT], back_a, back_c, back_b


def body(
    act_fwd,
    route_fwd,
    weight_fwd,
    act_bwd,
    route_bwd,
    weight_bwd,
    cot_bwd,
    norm_gain,
    w_gate,
    w_up,
    w_down,
):
    tokens, width = act_fwd.shape[1:]
    index = lax.axis_index("expert")
    info = jnp.stack([index >> 3, (index >> 2) & 1]).astype(jnp.int32)
    weights = (w_gate[0, 0], w_up[0, 0], w_down[0, 0])
    units = w_down.shape[2]
    (merged,) = local_copy_call(
        merge_kernel,
        [((3 * width, units), BF16)],
        0,
        [pltpu.VMEM((units, width), BF16), pltpu.SemaphoreType.DMA((3,))],
    )(*weights)
    other = hop(merged, HOP_W)
    wide = [((SLOT, 3 * width), BF16)] * 4
    sent = local_copy_call(
        pack_kernel,
        wide,
        3,
        [pltpu.VMEM((tokens, width), BF16), pltpu.VMEM((1, width), F32)]
        + [pltpu.VMEM((tokens, width), BF16)] * 2
        + [pltpu.SemaphoreType.DMA((4,))],
    )(info, route_fwd[0].T, route_bwd[0].T, act_fwd[0], norm_gain, act_bwd[0], cot_bwd[0])
    rows = spread_rows(*sent)
    outs = [((64, width), F32), ((64, width), BF16)] * 2
    scratch = pltpu.VMEM((256, width), BF16)
    part_a = kernel_call(fwd_kernel, outs, 8, [scratch], info=False)(*rows, *weights, other)
    part_b = kernel_call(bwd_kernel, outs, 9, [scratch] * 2, info=False)(
        *rows, *weights, other, part_a[1]
    )
    halves = zip(return_x(*part_a), return_x(*part_b))
    back = return_z(*[jnp.concatenate(pair, axis=1) for pair in halves])
    layer_out, d_input, gate_grad = kernel_call(
        last_kernel, [((tokens, width), BF16)] * 2 + [((tokens, 2), BF16)], 12
    )(
        info,
        act_fwd[0],
        route_fwd[0].T,
        weight_fwd[0].T,
        act_bwd[0],
        route_bwd[0].T,
        weight_bwd[0].T,
        cot_bwd[0],
        norm_gain,
        *back,
    )
    act_next = shifted(layer_out, "section", 1)
    cot_next = shifted(d_input, "section", -1)
    return (act_next[None], cot_next[None], gate_grad[None])


def solution(mesh):
    return jax.shard_map(
        body,
        mesh=mesh,
        in_specs=(
            P("section", "expert", None),
            P("section", "expert", None),
            P("section", "expert", None),
            P("section", "expert", None),
            P("section", "expert", None),
            P("section", "expert", None),
            P("section", "expert", None),
            P("section", None),
            P("section", "expert", None, None),
            P("section", "expert", None, None),
            P("section", "expert", None, None),
        ),
        out_specs=(
            P("section", "expert", None),
            P("section", "expert", None),
            P("section", "expert", None),
        ),
        check_vma=False,
    )
```

```python
import jax
import jax.numpy as jnp
from jax import lax
from jax.experimental import pallas as pl
from jax.experimental.pallas import tpu as pltpu
from jax.sharding import PartitionSpec as P

EXPERTS = 4
GRID_X = 4
GRID_Z = 8
SLOT = 16
F32 = jnp.float32
BF16 = jnp.bfloat16
NT = (((1,), (1,)), ((), ()))
TN = (((0,), (0,)), ((), ()))


def expert_pairs(move):
    pairs = []
    for z in range(GRID_Z):
        for x in range(GRID_X):
            to_z, to_x = move(z, x)
            pairs.append((z * GRID_X + x, to_z % GRID_Z * GRID_X + to_x))
    return pairs


def signed(z, even, odd):
    return z + (odd if z % 2 else even)


HOP_W = expert_pairs(lambda z, x: (z ^ 1, x))
HOP_A = expert_pairs(lambda z, x: (signed(z, -1, 1), x))
HOP_B = expert_pairs(lambda z, x: (signed(z, 2, -2), x))
HOP_B_BACK = expert_pairs(lambda z, x: (signed(z, -2, 2), x))
HOP_C = expert_pairs(lambda z, x: (signed(z, -3, 3), x))
HOP_X1 = expert_pairs(lambda z, x: (z, x ^ 1))
HOP_X3 = expert_pairs(lambda z, x: (z, x ^ 3))


def hop(value, pairs):
    return lax.ppermute(value, "expert", pairs)


def shifted(value, axis, by):
    devices = lax.axis_size(axis)
    pairs = [(i, i + by) for i in range(devices) if 0 <= i + by < devices]
    return lax.ppermute(value, axis, pairs)


def kernel_call(kernel, outs, n_in, scratch=(), info=True, limit=32):
    smem = pl.BlockSpec(memory_space=pltpu.SMEM)
    vmem = pl.BlockSpec(memory_space=pltpu.VMEM)
    return pl.pallas_call(
        kernel,
        out_shape=[jax.ShapeDtypeStruct(s, d) for s, d in outs],
        in_specs=[smem] * info + [vmem] * n_in,
        out_specs=[vmem] * len(outs),
        scratch_shapes=list(scratch),
        compiler_params=pltpu.CompilerParams(vmem_limit_bytes=limit * 1024 * 1024),
    )


def local_copy_call(kernel, outs, n_near, scratch):
    n_far = 4 if n_near else 3
    smem = pl.BlockSpec(memory_space=pltpu.SMEM)
    vmem = pl.BlockSpec(memory_space=pltpu.VMEM)
    near = ([smem] + [vmem] * (n_near - 1)) if n_near else []
    return pl.pallas_call(
        kernel,
        out_shape=[jax.ShapeDtypeStruct(s, d) for s, d in outs],
        in_specs=near + [pl.BlockSpec(memory_space=pl.ANY)] * n_far,
        out_specs=[vmem] * len(outs),
        scratch_shapes=scratch,
        compiler_params=pltpu.CompilerParams(vmem_limit_bytes=60 * 1024 * 1024),
    )


def columns(ref):
    count = ref.shape[1]
    row = lax.broadcasted_iota(jnp.int32, (count, count), 0)
    col = lax.broadcasted_iota(jnp.int32, (count, count), 1)
    values = ref[...].astype(F32)
    return [
        jnp.sum(jnp.where(row == col, values[k : k + 1, :], 0.0), axis=1, keepdims=True)
        for k in range(2)
    ]


def slot_masks(info_ref, route_ref):
    tokens = route_ref.shape[1]
    own, odd = info_ref[0], info_ref[1]
    lanes = lax.broadcasted_iota(jnp.int32, (tokens, 128), 1)
    route = [column.astype(jnp.int32) for column in columns(route_ref)]
    named = [(route[k] == lanes).astype(F32) for k in range(2)]
    row = lax.broadcasted_iota(jnp.int32, (tokens, tokens), 0)
    col = lax.broadcasted_iota(jnp.int32, (tokens, tokens), 1)
    earlier = (col < row).astype(BF16)
    counts = jnp.dot(earlier, (named[0] + named[1]).astype(BF16), preferred_element_type=F32)
    out = []
    for k in range(2):
        rank = jnp.sum(named[k] * counts, axis=1, keepdims=True).astype(jnp.int32)
        away = (route[k] - own) & 3
        side = jnp.where((away == 3) == (odd == 0), 1, 2)
        rel = jnp.where(away == 0, 0, jnp.where(away == 2, 3, side))
        slots = lax.broadcasted_iota(jnp.int32, (tokens, 4 * SLOT), 1)
        out.append((slots == rel * SLOT + rank, rel, rank))
    return out


def normalized(x):
    values = x.astype(F32)
    scale = lax.rsqrt(jnp.mean(values * values, axis=-1, keepdims=True) + 1e-06)
    return values * scale, scale


def pack_kernel(info_ref, ra_ref, rb_ref, xa, gain_in, xb, cot, *rest):
    outs, (xa_ref, gain_ref, xb_ref, cot_ref, sems) = rest[:4], rest[4:]
    width = xa.shape[1]
    moves = ((xa, xa_ref), (gain_in, gain_ref), (xb, xb_ref), (cot, cot_ref))
    copies = [pltpu.make_async_copy(*move, sems.at[i]) for i, move in enumerate(moves)]
    for copy in copies:
        copy.start()
    places = []
    for route_ref in (ra_ref, rb_ref):
        masks = slot_masks(info_ref, route_ref)
        places.append((masks[0][0] | masks[1][0]).astype(F32).astype(BF16))
    for copy in copies:
        copy.wait()
    gain = gain_ref[...]
    normed_a = (normalized(xa_ref[...])[0] * gain).astype(BF16)
    normed_b = (normalized(xb_ref[...])[0] * gain).astype(BF16)
    sources = ((places[0], normed_a), (places[1], normed_b), (places[1], cot_ref[...]))
    for i, (place, rows) in enumerate(sources):
        packed = lax.dot_general(place, rows, TN, preferred_element_type=F32).astype(BF16)
        for j in range(4):
            outs[j][:, i * width : (i + 1) * width] = packed[j * SLOT : (j + 1) * SLOT]


def merge_kernel(wg, wu, wd, out, down, sems):
    width, units = wg.shape
    moves = ((wd, down), (wg, out.at[pl.ds(0, width)]), (wu, out.at[pl.ds(width, width)]))
    copies = [pltpu.make_async_copy(*move, sems.at[i]) for i, move in enumerate(moves)]
    for copy in copies:
        copy.start()
    copies[0].wait()
    for at in range(0, width, units):
        out[2 * width + at : 2 * width + at + units, :] = down[:, at : at + units]
    copies[1].wait()
    copies[2].wait()


def hidden(rows, wg, wu):
    both = jnp.dot(rows, jnp.concatenate([wg, wu], axis=1), preferred_element_type=F32)
    return both[:, :128], both[:, 128:]


def down_columns(merged, at, count):
    width = merged.shape[0] // 3
    starts = range(2 * width + at, 2 * width + at + count, 128)
    return jnp.concatenate([merged[start : start + 128, :] for start in starts], axis=1)


def gather_rows(refs, at, width, scratch):
    for i, ref in enumerate(refs):
        scratch[64 * i : 64 * (i + 1), :] = ref[:, at : at + width]


def store_parts(part, cols, keep1, send1, keep2, send2):
    places = (
        (keep1, (128, 0, 160, 64)),
        (send1, (192, 32, 224, 96)),
        (keep2, (144, 16, 208, 48)),
        (send2, (176, 80, 240, 112)),
    )
    for ref, starts in places:
        for i, start in enumerate(starts):
            rows = slice(SLOT * i, SLOT * (i + 1))
            ref[rows, cols] = part[start : start + SLOT].astype(ref.dtype)


def fwd_kernel(c1, qr1, c2, pr2, wg, wu, wd, other, keep1, send1, keep2, send2, rows):
    width = rows.shape[1]
    gather_rows((c1, qr1, c2, pr2), 0, width, rows)
    inner = []
    for weights in ((wg[...], wu[...]), (other[0:width, :], other[width : 2 * width, :])):
        gate, up = hidden(rows[...], *weights)
        inner.append((gate * jax.nn.sigmoid(gate) * up).astype(BF16))
    inner = jnp.concatenate(inner, axis=1)
    step = 512
    for at in range(0, width, step):
        cols = slice(at, at + step)
        down = jnp.concatenate([wd[:, cols], down_columns(other, at, step)], axis=0)
        part = jnp.dot(inner, down, preferred_element_type=F32)
        store_parts(part, cols, keep1, send1, keep2, send2)


def bwd_kernel(
    c1, qr1, c2, pr2, wg, wu, wd, other, _, keep1, send1, keep2, send2, rows, cots
):
    width = rows.shape[1]
    gather_rows((c1, qr1, c2, pr2), width, width, rows)
    gather_rows((c1, qr1, c2, pr2), 2 * width, width, cots)
    back = []
    products = None
    sources = (
        (wg[...], wu[...], wd[...]),
        (other[0:width, :], other[width : 2 * width, :], down_columns(other, 0, width)),
    )
    for gate_w, up_w, down_w in sources:
        gate, up = hidden(rows[...], gate_w, up_w)
        d_inner = lax.dot_general(cots[...], down_w, NT, preferred_element_type=F32)
        sig = jax.nn.sigmoid(gate)
        silu = gate * sig
        inner = (silu * up).astype(BF16).astype(F32)
        d_gate = (d_inner * up * sig * (1.0 + gate * (1.0 - sig))).astype(BF16)
        d_up = (d_inner * silu).astype(BF16)
        back.append(jnp.concatenate([d_gate, d_up], axis=1))
        product = inner * d_inner
        products = product if products is None else products + product
    count = products.shape[0]
    high = products.astype(BF16)
    low = (products - high.astype(F32)).astype(BF16)
    ones = jnp.ones((16, 128), BF16)
    grads = lax.dot_general(ones, high, NT, preferred_element_type=F32)
    grads = grads + lax.dot_general(ones, low, NT, preferred_element_type=F32)
    row = lax.broadcasted_iota(jnp.int32, (count, count), 0)
    col = lax.broadcasted_iota(jnp.int32, (count, count), 1)
    held = (row // SLOT == col // SLOT) & (row % SLOT == SLOT - 2)
    spread = jnp.where(held, grads[0:1, :], 0.0).astype(BF16)
    at_row = lax.broadcasted_iota(jnp.int32, (count, 128), 0)
    at_col = lax.broadcasted_iota(jnp.int32, (count, 128), 1)
    pick = (at_row % SLOT == at_col).astype(F32).astype(BF16)
    grad_rows = jnp.dot(spread, pick, preferred_element_type=F32)
    step = 512
    for at in range(0, width, step):
        cols = slice(at, at + step)
        there = slice(width + at, width + at + step)
        weights = (
            jnp.concatenate([wg[cols, :], wu[cols, :]], axis=1),
            jnp.concatenate([other[cols, :], other[there, :]], axis=1),
        )
        part = None
        for grad, weight in zip(back, weights):
            term = lax.dot_general(grad, weight, NT, preferred_element_type=F32)
            part = term if part is None else part + term
        if at == 0:
            part = jnp.concatenate([part[:, :128] + grad_rows, part[:, 128:]], axis=1)
        store_parts(part, cols, keep1, send1, keep2, send2)


def mixed_rows(masks, weight_ref, parts):
    weights = columns(weight_ref)
    spread = jnp.where(masks[0][0], weights[0], 0.0) + jnp.where(masks[1][0], weights[1], 0.0)
    high = spread.astype(BF16)
    rest = spread - high.astype(F32)
    middle = rest.astype(BF16)
    low = (rest - middle.astype(F32)).astype(BF16)
    tokens = spread.shape[0]
    pieces = jnp.concatenate([high, middle, low], axis=0)
    product = jnp.dot(pieces, jnp.concatenate(parts, axis=0), preferred_element_type=F32)
    return product[:tokens] + product[tokens : 2 * tokens] + product[2 * tokens :]


def last_kernel(
    info_ref, xa_ref, ra_ref, wa_ref, x_ref, route_ref, weight_ref, cot_ref, gain_ref, *rest
):
    width = x_ref.shape[1]
    arrived = [rest[0], rest[1], rest[3], rest[2]]
    parts_a = [ref[:, :width] for ref in arrived]
    parts = [ref[:, width:] for ref in arrived]
    out_a_ref, out_ref, grad_ref = rest[4:]
    mixed = mixed_rows(slot_masks(info_ref, ra_ref), wa_ref, parts_a)
    out_a_ref[...] = (xa_ref[...].astype(F32) + mixed).astype(BF16)
    masks = slot_masks(info_ref, route_ref)
    d_normed = mixed_rows(masks, weight_ref, parts)
    unit, scale = normalized(x_ref[...])
    q_term = d_normed * gain_ref[...]
    mean = jnp.mean(q_term * unit, axis=-1, keepdims=True)
    d_input = cot_ref[...].astype(F32) + scale * (q_term - unit * mean)
    out_ref[...] = d_input.astype(BF16)
    tokens = x_ref.shape[0]
    lanes = lax.broadcasted_iota(jnp.int32, (tokens, 128), 1)
    grads = []
    for _, rel, rank in masks:
        held = jnp.zeros((tokens, 128), F32)
        for j, part in enumerate(parts):
            row = part[:, :128].astype(F32)[SLOT - 2 : SLOT - 1, :]
            held = held + jnp.where(rel == j, row, 0.0)
        grads.append(jnp.sum(jnp.where(lanes == rank, held, 0.0), axis=1, keepdims=True))
    pair = lax.broadcasted_iota(jnp.int32, (tokens, 2), 1)
    grad_ref[...] = jnp.where(pair == 0, grads[0], grads[1]).astype(BF16)


def spread_rows(own, a, b, c):
    got_a, got_b, got_c = hop(a, HOP_A), hop(b, HOP_B), hop(c, HOP_C)
    half1 = jnp.concatenate([got_b, got_c], axis=0)
    half2 = jnp.concatenate([own, got_a], axis=0)
    q1 = hop(half1, HOP_X3)
    p2 = hop(half2, HOP_X1)
    c1 = jnp.concatenate([half1, q1], axis=0)
    c2 = jnp.concatenate([half2, p2], axis=0)
    return c1, hop(c1, HOP_X1), c2, hop(c2, HOP_X3)


def return_x(keep1, send1, keep2, send2):
    sum1 = keep1 + hop(send1, HOP_X3).astype(F32)
    sum2 = keep2 + hop(send2, HOP_X1).astype(F32)
    full1 = sum1[:32] + hop(sum1[32:].astype(BF16), HOP_X1).astype(F32)
    full2 = sum2[:32] + hop(sum2[32:].astype(BF16), HOP_X3).astype(F32)
    return full1.astype(BF16), full2.astype(BF16)


def return_z(full1, full2):
    back_a = hop(full2[:SLOT], HOP_A)
    back_c = hop(full2[SLOT:], HOP_C)
    back_b = hop(full1[SLOT:], HOP_B_BACK)
    return full1[:SLOT], back_a, back_c, back_b


def body(
    act_fwd,
    route_fwd,
    weight_fwd,
    act_bwd,
    route_bwd,
    weight_bwd,
    cot_bwd,
    norm_gain,
    w_gate,
    w_up,
    w_down,
):
    tokens, width = act_fwd.shape[1:]
    index = lax.axis_index("expert")
    info = jnp.stack([index >> 3, (index >> 2) & 1]).astype(jnp.int32)
    weights = (w_gate[0, 0], w_up[0, 0], w_down[0, 0])
    units = w_down.shape[2]
    (merged,) = local_copy_call(
        merge_kernel,
        [((3 * width, units), BF16)],
        0,
        [pltpu.VMEM((units, width), BF16), pltpu.SemaphoreType.DMA((3,))],
    )(*weights)
    other = hop(merged, HOP_W)
    wide = [((SLOT, 3 * width), BF16)] * 4
    sent = local_copy_call(
        pack_kernel,
        wide,
        3,
        [pltpu.VMEM((tokens, width), BF16), pltpu.VMEM((1, width), F32)]
        + [pltpu.VMEM((tokens, width), BF16)] * 2
        + [pltpu.SemaphoreType.DMA((4,))],
    )(info, route_fwd[0].T, route_bwd[0].T, act_fwd[0], norm_gain, act_bwd[0], cot_bwd[0])
    rows = spread_rows(*sent)
    outs = [((64, width), F32), ((64, width), BF16)] * 2
    scratch = pltpu.VMEM((256, width), BF16)
    part_a = kernel_call(fwd_kernel, outs, 8, [scratch], info=False)(*rows, *weights, other)
    part_b = kernel_call(bwd_kernel, outs, 9, [scratch] * 2, info=False)(
        *rows, *weights, other, part_a[1]
    )
    halves = zip(return_x(*part_a), return_x(*part_b))
    back = return_z(*[jnp.concatenate(pair, axis=1) for pair in halves])
    layer_out, d_input, gate_grad = kernel_call(
        last_kernel, [((tokens, width), BF16)] * 2 + [((tokens, 2), BF16)], 12
    )(
        info,
        act_fwd[0],
        route_fwd[0].T,
        weight_fwd[0].T,
        act_bwd[0],
        route_bwd[0].T,
        weight_bwd[0].T,
        cot_bwd[0],
        norm_gain,
        *back,
    )
    act_next = shifted(layer_out, "section", 1)
    cot_next = shifted(d_input, "section", -1)
    return (act_next[None], cot_next[None], gate_grad[None])


def solution(mesh):
    return jax.shard_map(
        body,
        mesh=mesh,
        in_specs=(
            P("section", "expert", None),
            P("section", "expert", None),
            P("section", "expert", None),
            P("section", "expert", None),
            P("section", "expert", None),
            P("section", "expert", None),
            P("section", "expert", None),
            P("section", None),
            P("section", "expert", None, None),
            P("section", "expert", None, None),
            P("section", "expert", None, None),
        ),
        out_specs=(
            P("section", "expert", None),
            P("section", "expert", None),
            P("section", "expert", None),
        ),
        check_vma=False,
    )
```

```python
import jax
import jax.numpy as jnp
from jax import lax
from jax.experimental import pallas as pl
from jax.experimental.pallas import tpu as pltpu
from jax.sharding import PartitionSpec as P

EXPERTS = 4
GRID_X = 4
GRID_Z = 8
SLOT = 16
F32 = jnp.float32
BF16 = jnp.bfloat16
NT = (((1,), (1,)), ((), ()))
TN = (((0,), (0,)), ((), ()))


def expert_pairs(move):
    pairs = []
    for z in range(GRID_Z):
        for x in range(GRID_X):
            to_z, to_x = move(z, x)
            pairs.append((z * GRID_X + x, to_z % GRID_Z * GRID_X + to_x))
    return pairs


def signed(z, even, odd):
    return z + (odd if z % 2 else even)


HOP_W = expert_pairs(lambda z, x: (z ^ 1, x))
HOP_A = expert_pairs(lambda z, x: (signed(z, -1, 1), x))
HOP_B = expert_pairs(lambda z, x: (signed(z, 2, -2), x))
HOP_B_BACK = expert_pairs(lambda z, x: (signed(z, -2, 2), x))
HOP_C = expert_pairs(lambda z, x: (signed(z, -3, 3), x))
HOP_X1 = expert_pairs(lambda z, x: (z, x ^ 1))
HOP_X3 = expert_pairs(lambda z, x: (z, x ^ 3))


def hop(value, pairs):
    return lax.ppermute(value, "expert", pairs)


def shifted(value, axis, by):
    devices = lax.axis_size(axis)
    pairs = [(i, i + by) for i in range(devices) if 0 <= i + by < devices]
    return lax.ppermute(value, axis, pairs)


def kernel_call(kernel, outs, n_in, scratch=(), info=True, limit=32):
    smem = pl.BlockSpec(memory_space=pltpu.SMEM)
    vmem = pl.BlockSpec(memory_space=pltpu.VMEM)
    return pl.pallas_call(
        kernel,
        out_shape=[jax.ShapeDtypeStruct(s, d) for s, d in outs],
        in_specs=[smem] * info + [vmem] * n_in,
        out_specs=[vmem] * len(outs),
        scratch_shapes=list(scratch),
        compiler_params=pltpu.CompilerParams(vmem_limit_bytes=limit * 1024 * 1024),
    )


def local_copy_call(kernel, outs, n_near, scratch):
    n_far = 4 if n_near else 2
    smem = pl.BlockSpec(memory_space=pltpu.SMEM)
    vmem = pl.BlockSpec(memory_space=pltpu.VMEM)
    near = ([smem] + [vmem] * (n_near - 1)) if n_near else []
    return pl.pallas_call(
        kernel,
        out_shape=[jax.ShapeDtypeStruct(s, d) for s, d in outs],
        in_specs=near + [pl.BlockSpec(memory_space=pl.ANY)] * n_far,
        out_specs=[vmem] * len(outs),
        scratch_shapes=scratch,
        compiler_params=pltpu.CompilerParams(vmem_limit_bytes=60 * 1024 * 1024),
    )


def columns(ref):
    count = ref.shape[1]
    row = lax.broadcasted_iota(jnp.int32, (count, count), 0)
    col = lax.broadcasted_iota(jnp.int32, (count, count), 1)
    values = ref[...].astype(F32)
    return [
        jnp.sum(jnp.where(row == col, values[k : k + 1, :], 0.0), axis=1, keepdims=True)
        for k in range(2)
    ]


def slot_masks(info_ref, route_ref):
    tokens = route_ref.shape[1]
    own, odd = info_ref[0], info_ref[1]
    lanes = lax.broadcasted_iota(jnp.int32, (tokens, 128), 1)
    route = [column.astype(jnp.int32) for column in columns(route_ref)]
    named = [(route[k] == lanes).astype(F32) for k in range(2)]
    row = lax.broadcasted_iota(jnp.int32, (tokens, tokens), 0)
    col = lax.broadcasted_iota(jnp.int32, (tokens, tokens), 1)
    earlier = (col < row).astype(BF16)
    counts = jnp.dot(earlier, (named[0] + named[1]).astype(BF16), preferred_element_type=F32)
    out = []
    for k in range(2):
        rank = jnp.sum(named[k] * counts, axis=1, keepdims=True).astype(jnp.int32)
        away = (route[k] - own) & 3
        side = jnp.where((away == 3) == (odd == 0), 1, 2)
        rel = jnp.where(away == 0, 0, jnp.where(away == 2, 3, side))
        slots = lax.broadcasted_iota(jnp.int32, (tokens, 4 * SLOT), 1)
        out.append((slots == rel * SLOT + rank, rel, rank))
    return out


def normalized(x):
    values = x.astype(F32)
    scale = lax.rsqrt(jnp.mean(values * values, axis=-1, keepdims=True) + 1e-06)
    return values * scale, scale


def pack_kernel(info_ref, ra_ref, rb_ref, xa, gain_in, xb, cot, *rest):
    outs, (xa_ref, gain_ref, xb_ref, cot_ref, sems) = rest[:4], rest[4:]
    width = xa.shape[1]
    moves = ((xa, xa_ref), (gain_in, gain_ref), (xb, xb_ref), (cot, cot_ref))
    copies = [pltpu.make_async_copy(*move, sems.at[i]) for i, move in enumerate(moves)]
    for copy in copies:
        copy.start()
    places = []
    for route_ref in (ra_ref, rb_ref):
        masks = slot_masks(info_ref, route_ref)
        places.append((masks[0][0] | masks[1][0]).astype(F32).astype(BF16))
    for copy in copies:
        copy.wait()
    gain = gain_ref[...]
    normed_a = (normalized(xa_ref[...])[0] * gain).astype(BF16)
    normed_b = (normalized(xb_ref[...])[0] * gain).astype(BF16)
    sources = ((places[0], normed_a), (places[1], normed_b), (places[1], cot_ref[...]))
    for i, (place, rows) in enumerate(sources):
        packed = lax.dot_general(place, rows, TN, preferred_element_type=F32).astype(BF16)
        for j in range(4):
            outs[j][:, i * width : (i + 1) * width] = packed[j * SLOT : (j + 1) * SLOT]


def merge_kernel(wg, wu, out, sems):
    width = wg.shape[0]
    copies = [
        pltpu.make_async_copy(wg, out.at[pl.ds(0, width)], sems.at[0]),
        pltpu.make_async_copy(wu, out.at[pl.ds(width, width)], sems.at[1]),
    ]
    for copy in copies:
        copy.start()
    for copy in copies:
        copy.wait()


def near_kernel(half, got, _, out):
    count = half.shape[0]
    out[0:count, :] = half[...]
    out[count : 2 * count, :] = got[...]


def hidden(rows, wg, wu):
    both = jnp.dot(rows, jnp.concatenate([wg, wu], axis=1), preferred_element_type=F32)
    return both[:, :128], both[:, 128:]


X1_FIRST = (0, 32, 64, 96)
X3_FIRST = (0, 64, 32, 96)
LEFT = (X3_FIRST, X1_FIRST)
RIGHT = (X1_FIRST, X3_FIRST)


def gather_rows(refs, orders, at, to, width, scratch):
    cols, into = slice(at, at + width), slice(to, to + width)
    for half in range(2):
        for i, start in enumerate(orders[half]):
            ref, row = refs[2 * half + i // 2], 32 * (i % 2)
            base = 128 * half + start
            scratch[base : base + 32, into] = ref[row : row + 32, cols]


def store_parts(part, cols, keep1, send1, keep2, send2):
    places = (
        (keep1, (128, 0, 160, 32)),
        (send1, (192, 64, 224, 96)),
        (keep2, (144, 16, 208, 80)),
        (send2, (176, 48, 240, 112)),
    )
    for ref, starts in places:
        for i, start in enumerate(starts):
            rows = slice(SLOT * i, SLOT * (i + 1))
            ref[rows, cols] = part[start : start + SLOT].astype(ref.dtype)


def fwd_kernel(l1, l2, l3, l4, wg, wu, wd, other, vd, keep1, send1, keep2, send2, rows):
    width = rows.shape[1]
    gather_rows((l1, l2, l3, l4), LEFT, 0, 0, width, rows)
    inner = []
    for weights in ((wg[...], wu[...]), (other[0:width, :], other[width : 2 * width, :])):
        gate, up = hidden(rows[...], *weights)
        inner.append((gate * jax.nn.sigmoid(gate) * up).astype(BF16))
    inner = jnp.concatenate(inner, axis=1)
    step = 512
    for at in range(0, width, step):
        cols = slice(at, at + step)
        down = jnp.concatenate([wd[:, cols], vd[:, cols]], axis=0)
        part = jnp.dot(inner, down, preferred_element_type=F32)
        store_parts(part, cols, keep1, send1, keep2, send2)


def bwd_kernel(
    l1, l2, l3, l4, r1, r2, r3, r4, wg, wu, wd, other, vd, _, keep1, send1, keep2, send2, rows, cots
):
    width = rows.shape[1]
    half = width // 2
    lefts, rights = (l1, l2, l3, l4), (r1, r2, r3, r4)
    gather_rows(lefts, LEFT, width, 0, half, rows)
    gather_rows(rights, RIGHT, 0, half, half, rows)
    gather_rows(rights, RIGHT, half, 0, width, cots)
    back = []
    products = None
    sources = (
        (wg[...], wu[...], wd[...]),
        (other[0:width, :], other[width : 2 * width, :], vd[...]),
    )
    for gate_w, up_w, down_w in sources:
        gate, up = hidden(rows[...], gate_w, up_w)
        d_inner = lax.dot_general(cots[...], down_w, NT, preferred_element_type=F32)
        sig = jax.nn.sigmoid(gate)
        silu = gate * sig
        inner = (silu * up).astype(BF16).astype(F32)
        d_gate = (d_inner * up * sig * (1.0 + gate * (1.0 - sig))).astype(BF16)
        d_up = (d_inner * silu).astype(BF16)
        back.append(jnp.concatenate([d_gate, d_up], axis=1))
        product = inner * d_inner
        products = product if products is None else products + product
    count = products.shape[0]
    high = products.astype(BF16)
    low = (products - high.astype(F32)).astype(BF16)
    ones = jnp.ones((16, 128), BF16)
    grads = lax.dot_general(ones, high, NT, preferred_element_type=F32)
    grads = grads + lax.dot_general(ones, low, NT, preferred_element_type=F32)
    row = lax.broadcasted_iota(jnp.int32, (count, count), 0)
    col = lax.broadcasted_iota(jnp.int32, (count, count), 1)
    held = (row // SLOT == col // SLOT) & (row % SLOT == SLOT - 2)
    spread = jnp.where(held, grads[0:1, :], 0.0).astype(BF16)
    at_row = lax.broadcasted_iota(jnp.int32, (count, 128), 0)
    at_col = lax.broadcasted_iota(jnp.int32, (count, 128), 1)
    pick = (at_row % SLOT == at_col).astype(F32).astype(BF16)
    grad_rows = jnp.dot(spread, pick, preferred_element_type=F32)
    step = 512
    for at in range(0, width, step):
        cols = slice(at, at + step)
        there = slice(width + at, width + at + step)
        weights = (
            jnp.concatenate([wg[cols, :], wu[cols, :]], axis=1),
            jnp.concatenate([other[cols, :], other[there, :]], axis=1),
        )
        part = None
        for grad, weight in zip(back, weights):
            term = lax.dot_general(grad, weight, NT, preferred_element_type=F32)
            part = term if part is None else part + term
        if at == 0:
            part = jnp.concatenate([part[:, :128] + grad_rows, part[:, 128:]], axis=1)
        store_parts(part, cols, keep1, send1, keep2, send2)


def mixed_rows(masks, weight_ref, parts):
    weights = columns(weight_ref)
    spread = jnp.where(masks[0][0], weights[0], 0.0) + jnp.where(masks[1][0], weights[1], 0.0)
    high = spread.astype(BF16)
    rest = spread - high.astype(F32)
    middle = rest.astype(BF16)
    low = (rest - middle.astype(F32)).astype(BF16)
    tokens = spread.shape[0]
    pieces = jnp.concatenate([high, middle, low], axis=0)
    product = jnp.dot(pieces, jnp.concatenate(parts, axis=0), preferred_element_type=F32)
    return product[:tokens] + product[tokens : 2 * tokens] + product[2 * tokens :]


def last_kernel(
    info_ref, xa_ref, ra_ref, wa_ref, x_ref, route_ref, weight_ref, cot_ref, gain_ref, *rest
):
    width = x_ref.shape[1]
    arrived = [rest[0], rest[1], rest[3], rest[2]]
    parts_a = [ref[:, :width] for ref in arrived]
    parts = [ref[:, width:] for ref in arrived]
    out_a_ref, out_ref, grad_ref = rest[4:]
    mixed = mixed_rows(slot_masks(info_ref, ra_ref), wa_ref, parts_a)
    out_a_ref[...] = (xa_ref[...].astype(F32) + mixed).astype(BF16)
    masks = slot_masks(info_ref, route_ref)
    d_normed = mixed_rows(masks, weight_ref, parts)
    unit, scale = normalized(x_ref[...])
    q_term = d_normed * gain_ref[...]
    mean = jnp.mean(q_term * unit, axis=-1, keepdims=True)
    d_input = cot_ref[...].astype(F32) + scale * (q_term - unit * mean)
    out_ref[...] = d_input.astype(BF16)
    tokens = x_ref.shape[0]
    lanes = lax.broadcasted_iota(jnp.int32, (tokens, 128), 1)
    grads = []
    for _, rel, rank in masks:
        held = jnp.zeros((tokens, 128), F32)
        for j, part in enumerate(parts):
            row = part[:, :128].astype(F32)[SLOT - 2 : SLOT - 1, :]
            held = held + jnp.where(rel == j, row, 0.0)
        grads.append(jnp.sum(jnp.where(lanes == rank, held, 0.0), axis=1, keepdims=True))
    pair = lax.broadcasted_iota(jnp.int32, (tokens, 2), 1)
    grad_ref[...] = jnp.where(pair == 0, grads[0], grads[1]).astype(BF16)


def spread_x(value, first, second, ready=None):
    got = hop(value, first)
    if ready is None:
        near = jnp.concatenate([value, got], axis=0)
    else:
        vmem = pl.BlockSpec(memory_space=pltpu.VMEM)
        near = pl.pallas_call(
            near_kernel,
            out_shape=jax.ShapeDtypeStruct((2 * value.shape[0], value.shape[1]), BF16),
            in_specs=[vmem, vmem, pl.BlockSpec(memory_space=pl.ANY)],
            out_specs=vmem,
        )(value, got, ready)
    return near, hop(near, second)


def spread_rows(own, a, b, c, other_down):
    got_a, got_b, got_c = hop(a, HOP_A), hop(b, HOP_B), hop(c, HOP_C)
    early = jnp.concatenate([own, got_a], axis=0)
    late = jnp.concatenate([got_b, got_c], axis=0)
    middle = own.shape[1] // 2
    late_left = spread_x(late[:, :middle], HOP_X3, HOP_X1, other_down)
    late_right = spread_x(late[:, middle:], HOP_X1, HOP_X3)
    early_left = spread_x(early[:, :middle], HOP_X1, HOP_X3)
    early_right = spread_x(early[:, middle:], HOP_X3, HOP_X1)
    return late_left + early_left, late_right + early_right


def return_x(keep1, send1, keep2, send2):
    sum1 = keep1 + hop(send1, HOP_X3).astype(F32)
    sum2 = keep2 + hop(send2, HOP_X1).astype(F32)
    full1 = sum1[:32] + hop(sum1[32:].astype(BF16), HOP_X1).astype(F32)
    full2 = sum2[:32] + hop(sum2[32:].astype(BF16), HOP_X3).astype(F32)
    return full1.astype(BF16), full2.astype(BF16)


def return_z(full1, full2):
    back_a = hop(full2[:SLOT], HOP_A)
    back_c = hop(full2[SLOT:], HOP_C)
    back_b = hop(full1[SLOT:], HOP_B_BACK)
    return full1[:SLOT], back_a, back_c, back_b


def body(
    act_fwd,
    route_fwd,
    weight_fwd,
    act_bwd,
    route_bwd,
    weight_bwd,
    cot_bwd,
    norm_gain,
    w_gate,
    w_up,
    w_down,
):
    tokens, width = act_fwd.shape[1:]
    index = lax.axis_index("expert")
    info = jnp.stack([index >> 3, (index >> 2) & 1]).astype(jnp.int32)
    weights = (w_gate[0, 0], w_up[0, 0], w_down[0, 0])
    units = w_down.shape[2]
    (merged,) = local_copy_call(
        merge_kernel,
        [((2 * width, units), BF16)],
        0,
        [pltpu.SemaphoreType.DMA((2,))],
    )(*weights[:2])
    other_down = hop(weights[2], HOP_W)
    other = hop(merged, HOP_W)
    wide = [((SLOT, 3 * width), BF16)] * 4
    sent = local_copy_call(
        pack_kernel,
        wide,
        3,
        [pltpu.VMEM((tokens, width), BF16), pltpu.VMEM((1, width), F32)]
        + [pltpu.VMEM((tokens, width), BF16)] * 2
        + [pltpu.SemaphoreType.DMA((4,))],
    )(info, route_fwd[0].T, route_bwd[0].T, act_fwd[0], norm_gain, act_bwd[0], cot_bwd[0])
    lefts, rights = spread_rows(*sent, other_down)
    weights += (other, other_down)
    outs = [((64, width), F32), ((64, width), BF16)] * 2
    scratch = pltpu.VMEM((256, width), BF16)
    part_a = kernel_call(fwd_kernel, outs, 9, [scratch], info=False)(*lefts, *weights)
    part_b = kernel_call(bwd_kernel, outs, 14, [scratch] * 2, info=False)(
        *lefts, *rights, *weights, part_a[1]
    )
    halves = zip(return_x(*part_a), return_x(*part_b))
    back = return_z(*[jnp.concatenate(pair, axis=1) for pair in halves])
    layer_out, d_input, gate_grad = kernel_call(
        last_kernel, [((tokens, width), BF16)] * 2 + [((tokens, 2), BF16)], 12
    )(
        info,
        act_fwd[0],
        route_fwd[0].T,
        weight_fwd[0].T,
        act_bwd[0],
        route_bwd[0].T,
        weight_bwd[0].T,
        cot_bwd[0],
        norm_gain,
        *back,
    )
    act_next = shifted(layer_out, "section", 1)
    cot_next = shifted(d_input, "section", -1)
    return (act_next[None], cot_next[None], gate_grad[None])


def solution(mesh):
    return jax.shard_map(
        body,
        mesh=mesh,
        in_specs=(
            P("section", "expert", None),
            P("section", "expert", None),
            P("section", "expert", None),
            P("section", "expert", None),
            P("section", "expert", None),
            P("section", "expert", None),
            P("section", "expert", None),
            P("section", None),
            P("section", "expert", None, None),
            P("section", "expert", None, None),
            P("section", "expert", None, None),
        ),
        out_specs=(
            P("section", "expert", None),
            P("section", "expert", None),
            P("section", "expert", None),
        ),
        check_vma=False,
    )
```

```python
import jax
import jax.numpy as jnp
from jax import lax
from jax.experimental import pallas as pl
from jax.experimental.pallas import tpu as pltpu
from jax.sharding import PartitionSpec as P

EXPERTS = 4
GRID_X = 4
GRID_Z = 8
SLOT = 16
F32 = jnp.float32
BF16 = jnp.bfloat16
NT = (((1,), (1,)), ((), ()))
TN = (((0,), (0,)), ((), ()))


def expert_pairs(move):
    pairs = []
    for z in range(GRID_Z):
        for x in range(GRID_X):
            to_z, to_x = move(z, x)
            pairs.append((z * GRID_X + x, to_z % GRID_Z * GRID_X + to_x))
    return pairs


def signed(z, even, odd):
    return z + (odd if z % 2 else even)


HOP_W = expert_pairs(lambda z, x: (z ^ 1, x))
HOP_A = expert_pairs(lambda z, x: (signed(z, -1, 1), x))
HOP_B = expert_pairs(lambda z, x: (signed(z, 2, -2), x))
HOP_B_BACK = expert_pairs(lambda z, x: (signed(z, -2, 2), x))
HOP_C = expert_pairs(lambda z, x: (signed(z, -3, 3), x))
HOP_X1 = expert_pairs(lambda z, x: (z, x ^ 1))
HOP_X3 = expert_pairs(lambda z, x: (z, x ^ 3))


def hop(value, pairs):
    return lax.ppermute(value, "expert", pairs)


def shifted(value, axis, by):
    devices = lax.axis_size(axis)
    pairs = [(i, i + by) for i in range(devices) if 0 <= i + by < devices]
    return lax.ppermute(value, axis, pairs)


def kernel_call(kernel, outs, n_in, scratch=(), info=True, limit=32):
    smem = pl.BlockSpec(memory_space=pltpu.SMEM)
    vmem = pl.BlockSpec(memory_space=pltpu.VMEM)
    return pl.pallas_call(
        kernel,
        out_shape=[jax.ShapeDtypeStruct(s, d) for s, d in outs],
        in_specs=[smem] * info + [vmem] * n_in,
        out_specs=[vmem] * len(outs),
        scratch_shapes=list(scratch),
        compiler_params=pltpu.CompilerParams(vmem_limit_bytes=limit * 1024 * 1024),
    )


def local_copy_call(kernel, scalars, arrays, outs, scratch):
    arrays = [pltpu.with_memory_space_constraint(array, pltpu.HBM) for array in arrays]
    return pl.pallas_call(
        kernel,
        out_shape=[jax.ShapeDtypeStruct(s, d) for s, d in outs],
        in_specs=[pl.BlockSpec(memory_space=pltpu.SMEM)] * len(scalars)
        + [pl.BlockSpec(memory_space=pltpu.HBM)] * len(arrays),
        out_specs=[pl.BlockSpec(memory_space=pltpu.VMEM)] * len(outs),
        scratch_shapes=scratch + [pltpu.SemaphoreType.DMA((len(arrays),))],
        compiler_params=pltpu.CompilerParams(vmem_limit_bytes=16 * 1024 * 1024),
    )(*scalars, *arrays)


def columns(ref):
    count = ref.shape[1]
    row = lax.broadcasted_iota(jnp.int32, (count, count), 0)
    col = lax.broadcasted_iota(jnp.int32, (count, count), 1)
    values = ref[...].astype(F32)
    return [
        jnp.sum(jnp.where(row == col, values[k : k + 1, :], 0.0), axis=1, keepdims=True)
        for k in range(2)
    ]


def slot_masks(info_ref, route_ref):
    tokens = route_ref.shape[1]
    own, odd = info_ref[0], info_ref[1]
    lanes = lax.broadcasted_iota(jnp.int32, (tokens, 128), 1)
    route = [column.astype(jnp.int32) for column in columns(route_ref)]
    named = [(route[k] == lanes).astype(F32) for k in range(2)]
    row = lax.broadcasted_iota(jnp.int32, (tokens, tokens), 0)
    col = lax.broadcasted_iota(jnp.int32, (tokens, tokens), 1)
    earlier = (col < row).astype(BF16)
    counts = jnp.dot(earlier, (named[0] + named[1]).astype(BF16), preferred_element_type=F32)
    out = []
    for k in range(2):
        rank = jnp.sum(named[k] * counts, axis=1, keepdims=True).astype(jnp.int32)
        away = (route[k] - own) & 3
        side = jnp.where((away == 3) == (odd == 0), 1, 2)
        rel = jnp.where(away == 0, 0, jnp.where(away == 2, 3, side))
        slots = lax.broadcasted_iota(jnp.int32, (tokens, 4 * SLOT), 1)
        out.append((slots == rel * SLOT + rank, rel, rank))
    return out


def normalized(x):
    values = x.astype(F32)
    scale = lax.rsqrt(jnp.mean(values * values, axis=-1, keepdims=True) + 1e-06)
    return values * scale, scale


def pack_kernel(info_ref, ra, rb, xa, gain_in, xb, cot, *rest):
    outs, (ra_ref, rb_ref, xa_ref, gain_ref, xb_ref, cot_ref, sems) = rest[:4], rest[4:]
    width = xa.shape[1]
    moves = (
        (ra, ra_ref),
        (rb, rb_ref),
        (xa, xa_ref),
        (gain_in, gain_ref),
        (xb, xb_ref),
        (cot, cot_ref),
    )
    copies = [pltpu.make_async_copy(*move, sems.at[i]) for i, move in enumerate(moves)]
    for copy in copies:
        copy.start()
    for copy in copies[:2]:
        copy.wait()
    places = []
    for route_ref in (ra_ref, rb_ref):
        masks = slot_masks(info_ref, route_ref)
        places.append((masks[0][0] | masks[1][0]).astype(F32).astype(BF16))
    for copy in copies[2:]:
        copy.wait()
    gain = gain_ref[...]
    normed_a = (normalized(xa_ref[...])[0] * gain).astype(BF16)
    normed_b = (normalized(xb_ref[...])[0] * gain).astype(BF16)
    sources = ((places[0], normed_a), (places[1], normed_b), (places[1], cot_ref[...]))
    for i, (place, rows) in enumerate(sources):
        packed = lax.dot_general(place, rows, TN, preferred_element_type=F32).astype(BF16)
        for j in range(4):
            outs[j][:, i * width : (i + 1) * width] = packed[j * SLOT : (j + 1) * SLOT]


def merge_kernel(wg, wu, wd, out, down, sems):
    width, units = wg.shape
    moves = ((wd, down), (wg, out.at[pl.ds(0, width)]), (wu, out.at[pl.ds(width, width)]))
    copies = [pltpu.make_async_copy(*move, sems.at[i]) for i, move in enumerate(moves)]
    for copy in copies:
        copy.start()
    copies[0].wait()
    for at in range(0, width, units):
        out[2 * width + at : 2 * width + at + units, :] = down[:, at : at + units]
    copies[1].wait()
    copies[2].wait()


def hidden(rows, wg, wu):
    both = jnp.dot(rows, jnp.concatenate([wg, wu], axis=1), preferred_element_type=F32)
    return both[:, :128], both[:, 128:]


def down_columns(merged, at, count):
    width = merged.shape[0] // 3
    starts = range(2 * width + at, 2 * width + at + count, 128)
    return jnp.concatenate([merged[start : start + 128, :] for start in starts], axis=1)


def gather_rows(refs, at, width, scratch):
    for i, ref in enumerate(refs):
        scratch[64 * i : 64 * (i + 1), :] = ref[:, at : at + width]


def store_parts(part, cols, keep1, send1, keep2, send2):
    places = (
        (keep1, (128, 0, 160, 64)),
        (send1, (192, 32, 224, 96)),
        (keep2, (144, 16, 208, 48)),
        (send2, (176, 80, 240, 112)),
    )
    for ref, starts in places:
        for i, start in enumerate(starts):
            rows = slice(SLOT * i, SLOT * (i + 1))
            ref[rows, cols] = part[start : start + SLOT].astype(ref.dtype)


def fwd_kernel(c1, qr1, c2, pr2, wg, wu, wd, other, keep1, send1, keep2, send2, rows):
    width = rows.shape[1]
    gather_rows((c1, qr1, c2, pr2), 0, width, rows)
    inner = []
    for weights in ((wg[...], wu[...]), (other[0:width, :], other[width : 2 * width, :])):
        gate, up = hidden(rows[...], *weights)
        inner.append((gate * jax.nn.sigmoid(gate) * up).astype(BF16))
    inner = jnp.concatenate(inner, axis=1)
    step = 512
    for at in range(0, width, step):
        cols = slice(at, at + step)
        down = jnp.concatenate([wd[:, cols], down_columns(other, at, step)], axis=0)
        part = jnp.dot(inner, down, preferred_element_type=F32)
        store_parts(part, cols, keep1, send1, keep2, send2)


def bwd_kernel(
    c1, qr1, c2, pr2, wg, wu, wd, other, _, keep1, send1, keep2, send2, rows, cots
):
    width = rows.shape[1]
    gather_rows((c1, qr1, c2, pr2), width, width, rows)
    gather_rows((c1, qr1, c2, pr2), 2 * width, width, cots)
    back = []
    products = None
    sources = (
        (wg[...], wu[...], wd[...]),
        (other[0:width, :], other[width : 2 * width, :], down_columns(other, 0, width)),
    )
    for gate_w, up_w, down_w in sources:
        gate, up = hidden(rows[...], gate_w, up_w)
        d_inner = lax.dot_general(cots[...], down_w, NT, preferred_element_type=F32)
        sig = jax.nn.sigmoid(gate)
        silu = gate * sig
        inner = (silu * up).astype(BF16).astype(F32)
        d_gate = (d_inner * up * sig * (1.0 + gate * (1.0 - sig))).astype(BF16)
        d_up = (d_inner * silu).astype(BF16)
        back.append(jnp.concatenate([d_gate, d_up], axis=1))
        product = inner * d_inner
        products = product if products is None else products + product
    count = products.shape[0]
    high = products.astype(BF16)
    low = (products - high.astype(F32)).astype(BF16)
    ones = jnp.ones((16, 128), BF16)
    grads = lax.dot_general(ones, high, NT, preferred_element_type=F32)
    grads = grads + lax.dot_general(ones, low, NT, preferred_element_type=F32)
    row = lax.broadcasted_iota(jnp.int32, (count, count), 0)
    col = lax.broadcasted_iota(jnp.int32, (count, count), 1)
    held = (row // SLOT == col // SLOT) & (row % SLOT == SLOT - 2)
    spread = jnp.where(held, grads[0:1, :], 0.0).astype(BF16)
    at_row = lax.broadcasted_iota(jnp.int32, (count, 128), 0)
    at_col = lax.broadcasted_iota(jnp.int32, (count, 128), 1)
    pick = (at_row % SLOT == at_col).astype(F32).astype(BF16)
    grad_rows = jnp.dot(spread, pick, preferred_element_type=F32)
    step = 512
    for at in range(0, width, step):
        cols = slice(at, at + step)
        there = slice(width + at, width + at + step)
        weights = (
            jnp.concatenate([wg[cols, :], wu[cols, :]], axis=1),
            jnp.concatenate([other[cols, :], other[there, :]], axis=1),
        )
        part = None
        for grad, weight in zip(back, weights):
            term = lax.dot_general(grad, weight, NT, preferred_element_type=F32)
            part = term if part is None else part + term
        if at == 0:
            part = jnp.concatenate([part[:, :128] + grad_rows, part[:, 128:]], axis=1)
        store_parts(part, cols, keep1, send1, keep2, send2)


def mixed_rows(masks, weight_ref, parts):
    weights = columns(weight_ref)
    spread = jnp.where(masks[0][0], weights[0], 0.0) + jnp.where(masks[1][0], weights[1], 0.0)
    high = spread.astype(BF16)
    rest = spread - high.astype(F32)
    middle = rest.astype(BF16)
    low = (rest - middle.astype(F32)).astype(BF16)
    tokens = spread.shape[0]
    pieces = jnp.concatenate([high, middle, low], axis=0)
    product = jnp.dot(pieces, jnp.concatenate(parts, axis=0), preferred_element_type=F32)
    return product[:tokens] + product[tokens : 2 * tokens] + product[2 * tokens :]


def last_kernel(
    info_ref, xa_ref, ra_ref, wa_ref, x_ref, route_ref, weight_ref, cot_ref, gain_ref, *rest
):
    width = x_ref.shape[1]
    arrived = [rest[0], rest[1], rest[3], rest[2]]
    parts_a = [ref[:, :width] for ref in arrived]
    parts = [ref[:, width:] for ref in arrived]
    out_a_ref, out_ref, grad_ref = rest[4:]
    mixed = mixed_rows(slot_masks(info_ref, ra_ref), wa_ref, parts_a)
    out_a_ref[...] = (xa_ref[...].astype(F32) + mixed).astype(BF16)
    masks = slot_masks(info_ref, route_ref)
    d_normed = mixed_rows(masks, weight_ref, parts)
    unit, scale = normalized(x_ref[...])
    q_term = d_normed * gain_ref[...]
    mean = jnp.mean(q_term * unit, axis=-1, keepdims=True)
    d_input = cot_ref[...].astype(F32) + scale * (q_term - unit * mean)
    out_ref[...] = d_input.astype(BF16)
    tokens = x_ref.shape[0]
    lanes = lax.broadcasted_iota(jnp.int32, (tokens, 128), 1)
    grads = []
    for _, rel, rank in masks:
        held = jnp.zeros((tokens, 128), F32)
        for j, part in enumerate(parts):
            row = part[:, :128].astype(F32)[SLOT - 2 : SLOT - 1, :]
            held = held + jnp.where(rel == j, row, 0.0)
        grads.append(jnp.sum(jnp.where(lanes == rank, held, 0.0), axis=1, keepdims=True))
    pair = lax.broadcasted_iota(jnp.int32, (tokens, 2), 1)
    grad_ref[...] = jnp.where(pair == 0, grads[0], grads[1]).astype(BF16)


def spread_rows(own, a, b, c):
    got_a, got_b, got_c = hop(a, HOP_A), hop(b, HOP_B), hop(c, HOP_C)
    half1 = jnp.concatenate([got_b, got_c], axis=0)
    half2 = jnp.concatenate([own, got_a], axis=0)
    q1 = hop(half1, HOP_X3)
    p2 = hop(half2, HOP_X1)
    c1 = jnp.concatenate([half1, q1], axis=0)
    c2 = jnp.concatenate([half2, p2], axis=0)
    return c1, hop(c1, HOP_X1), c2, hop(c2, HOP_X3)


def return_x(keep1, send1, keep2, send2):
    sum1 = keep1 + hop(send1, HOP_X3).astype(F32)
    sum2 = keep2 + hop(send2, HOP_X1).astype(F32)
    full1 = sum1[:32] + hop(sum1[32:].astype(BF16), HOP_X1).astype(F32)
    full2 = sum2[:32] + hop(sum2[32:].astype(BF16), HOP_X3).astype(F32)
    return full1.astype(BF16), full2.astype(BF16)


def return_z(full1, full2):
    back_a = hop(full2[:SLOT], HOP_A)
    back_c = hop(full2[SLOT:], HOP_C)
    back_b = hop(full1[SLOT:], HOP_B_BACK)
    return full1[:SLOT], back_a, back_c, back_b


def body(
    act_fwd,
    route_fwd,
    weight_fwd,
    act_bwd,
    route_bwd,
    weight_bwd,
    cot_bwd,
    norm_gain,
    w_gate,
    w_up,
    w_down,
):
    tokens, width = act_fwd.shape[1:]
    index = lax.axis_index("expert")
    info = jnp.stack([index >> 3, (index >> 2) & 1]).astype(jnp.int32)
    weights = (w_gate[0, 0], w_up[0, 0], w_down[0, 0])
    units = w_down.shape[2]
    (merged,) = local_copy_call(
        merge_kernel, (), weights, [((3 * width, units), BF16)], [pltpu.VMEM((units, width), BF16)]
    )
    other = hop(merged, HOP_W)
    wide = [((SLOT, 3 * width), BF16)] * 4
    sources = (
        route_fwd[0].T,
        route_bwd[0].T,
        act_fwd[0],
        norm_gain,
        act_bwd[0],
        cot_bwd[0],
    )
    sent = local_copy_call(
        pack_kernel, (info,), sources, wide, [pltpu.VMEM(v.shape, v.dtype) for v in sources]
    )
    rows = spread_rows(*sent)
    outs = [((64, width), F32), ((64, width), BF16)] * 2
    scratch = pltpu.VMEM((256, width), BF16)
    part_a = kernel_call(fwd_kernel, outs, 8, [scratch], info=False)(*rows, *weights, other)
    part_b = kernel_call(bwd_kernel, outs, 9, [scratch] * 2, info=False)(
        *rows, *weights, other, part_a[1]
    )
    halves = zip(return_x(*part_a), return_x(*part_b))
    back = return_z(*[jnp.concatenate(pair, axis=1) for pair in halves])
    layer_out, d_input, gate_grad = kernel_call(
        last_kernel, [((tokens, width), BF16)] * 2 + [((tokens, 2), BF16)], 12
    )(
        info,
        act_fwd[0],
        route_fwd[0].T,
        weight_fwd[0].T,
        act_bwd[0],
        route_bwd[0].T,
        weight_bwd[0].T,
        cot_bwd[0],
        norm_gain,
        *back,
    )
    act_next = shifted(layer_out, "section", 1)
    cot_next = shifted(d_input, "section", -1)
    return (act_next[None], cot_next[None], gate_grad[None])


def solution(mesh):
    return jax.shard_map(
        body,
        mesh=mesh,
        in_specs=(
            P("section", "expert", None),
            P("section", "expert", None),
            P("section", "expert", None),
            P("section", "expert", None),
            P("section", "expert", None),
            P("section", "expert", None),
            P("section", "expert", None),
            P("section", None),
            P("section", "expert", None, None),
            P("section", "expert", None, None),
            P("section", "expert", None, None),
        ),
        out_specs=(
            P("section", "expert", None),
            P("section", "expert", None),
            P("section", "expert", None),
        ),
        check_vma=False,
    )
```

```python
import jax
import jax.numpy as jnp
from jax import lax
from jax.experimental import pallas as pl
from jax.experimental.pallas import tpu as pltpu
from jax.sharding import PartitionSpec as P

EXPERTS = 4
GRID_X = 4
GRID_Z = 8
SLOT = 16
F32 = jnp.float32
BF16 = jnp.bfloat16
NT = (((1,), (1,)), ((), ()))
TN = (((0,), (0,)), ((), ()))


def expert_pairs(move):
    pairs = []
    for z in range(GRID_Z):
        for x in range(GRID_X):
            to_z, to_x = move(z, x)
            pairs.append((z * GRID_X + x, to_z % GRID_Z * GRID_X + to_x))
    return pairs


def signed(z, even, odd):
    return z + (odd if z % 2 else even)


HOP_W = expert_pairs(lambda z, x: (z ^ 1, x))
HOP_A = expert_pairs(lambda z, x: (signed(z, -1, 1), x))
HOP_B = expert_pairs(lambda z, x: (signed(z, 2, -2), x))
HOP_B_BACK = expert_pairs(lambda z, x: (signed(z, -2, 2), x))
HOP_C = expert_pairs(lambda z, x: (signed(z, -3, 3), x))
HOP_X1 = expert_pairs(lambda z, x: (z, x ^ 1))
HOP_X3 = expert_pairs(lambda z, x: (z, x ^ 3))


def hop(value, pairs):
    return lax.ppermute(value, "expert", pairs)


def shifted(value, axis, by):
    devices = lax.axis_size(axis)
    pairs = [(i, i + by) for i in range(devices) if 0 <= i + by < devices]
    return lax.ppermute(value, axis, pairs)


def kernel_call(kernel, outs, n_in, scratch=(), info=True, limit=32):
    smem = pl.BlockSpec(memory_space=pltpu.SMEM)
    vmem = pl.BlockSpec(memory_space=pltpu.VMEM)
    return pl.pallas_call(
        kernel,
        out_shape=[jax.ShapeDtypeStruct(s, d) for s, d in outs],
        in_specs=[smem] * info + [vmem] * n_in,
        out_specs=[vmem] * len(outs),
        scratch_shapes=list(scratch),
        compiler_params=pltpu.CompilerParams(vmem_limit_bytes=limit * 1024 * 1024),
    )


def local_copy_call(kernel, scalars, arrays, outs, scratch):
    arrays = [pltpu.with_memory_space_constraint(array, pltpu.HBM) for array in arrays]
    return pl.pallas_call(
        kernel,
        out_shape=[jax.ShapeDtypeStruct(s, d) for s, d in outs],
        in_specs=[pl.BlockSpec(memory_space=pltpu.SMEM)] * len(scalars)
        + [pl.BlockSpec(memory_space=pltpu.HBM)] * len(arrays),
        out_specs=[pl.BlockSpec(memory_space=pltpu.VMEM)] * len(outs),
        scratch_shapes=scratch + [pltpu.SemaphoreType.DMA((len(arrays),))],
        compiler_params=pltpu.CompilerParams(vmem_limit_bytes=16 * 1024 * 1024),
    )(*scalars, *arrays)


def columns(ref):
    count = ref.shape[1]
    row = lax.broadcasted_iota(jnp.int32, (count, count), 0)
    col = lax.broadcasted_iota(jnp.int32, (count, count), 1)
    values = ref[...].astype(F32)
    return [
        jnp.sum(jnp.where(row == col, values[k : k + 1, :], 0.0), axis=1, keepdims=True)
        for k in range(2)
    ]


def slot_masks(info_ref, route_ref):
    tokens = route_ref.shape[1]
    own, odd = info_ref[0], info_ref[1]
    lanes = lax.broadcasted_iota(jnp.int32, (tokens, 128), 1)
    route = [column.astype(jnp.int32) for column in columns(route_ref)]
    named = [(route[k] == lanes).astype(F32) for k in range(2)]
    row = lax.broadcasted_iota(jnp.int32, (tokens, tokens), 0)
    col = lax.broadcasted_iota(jnp.int32, (tokens, tokens), 1)
    earlier = (col < row).astype(BF16)
    counts = jnp.dot(earlier, (named[0] + named[1]).astype(BF16), preferred_element_type=F32)
    out = []
    for k in range(2):
        rank = jnp.sum(named[k] * counts, axis=1, keepdims=True).astype(jnp.int32)
        away = (route[k] - own) & 3
        side = jnp.where((away == 3) == (odd == 0), 1, 2)
        rel = jnp.where(away == 0, 0, jnp.where(away == 2, 3, side))
        slots = lax.broadcasted_iota(jnp.int32, (tokens, 4 * SLOT), 1)
        out.append((slots == rel * SLOT + rank, rel, rank))
    return out


def normalized(x):
    values = x.astype(F32)
    scale = lax.rsqrt(jnp.mean(values * values, axis=-1, keepdims=True) + 1e-06)
    return values * scale, scale


def first_kernel(info_ref, ra, rb, xa, gain_in, xb, cot, wg, wu, wd, *rest):
    outs, merged, scratch = rest[:4], rest[4], rest[5:]
    ra_ref, rb_ref, xa_ref, gain_ref, xb_ref, cot_ref, down, sems = scratch
    width, units = wg.shape
    moves = (
        (ra, ra_ref),
        (rb, rb_ref),
        (xa, xa_ref),
        (gain_in, gain_ref),
        (xb, xb_ref),
        (cot, cot_ref),
        (wd, down),
        (wg, merged.at[pl.ds(0, width)]),
        (wu, merged.at[pl.ds(width, width)]),
    )
    copies = [pltpu.make_async_copy(*move, sems.at[i]) for i, move in enumerate(moves)]
    for copy in copies:
        copy.start()
    for copy in copies[:2]:
        copy.wait()
    places = []
    for route_ref in (ra_ref, rb_ref):
        masks = slot_masks(info_ref, route_ref)
        places.append((masks[0][0] | masks[1][0]).astype(F32).astype(BF16))
    for copy in copies[2:6]:
        copy.wait()
    gain = gain_ref[...]
    normed_a = (normalized(xa_ref[...])[0] * gain).astype(BF16)
    normed_b = (normalized(xb_ref[...])[0] * gain).astype(BF16)
    sources = ((places[0], normed_a), (places[1], normed_b), (places[1], cot_ref[...]))
    for i, (place, rows) in enumerate(sources):
        packed = lax.dot_general(place, rows, TN, preferred_element_type=F32).astype(BF16)
        for j in range(4):
            outs[j][:, i * width : (i + 1) * width] = packed[j * SLOT : (j + 1) * SLOT]
    copies[6].wait()
    for at in range(0, width, units):
        merged[2 * width + at : 2 * width + at + units, :] = down[:, at : at + units]
    copies[7].wait()
    copies[8].wait()


def hidden(rows, wg, wu):
    both = jnp.dot(rows, jnp.concatenate([wg, wu], axis=1), preferred_element_type=F32)
    return both[:, :128], both[:, 128:]


def down_columns(merged, at, count):
    width = merged.shape[0] // 3
    starts = range(2 * width + at, 2 * width + at + count, 128)
    return jnp.concatenate([merged[start : start + 128, :] for start in starts], axis=1)


def gather_rows(refs, at, width, scratch):
    for i, ref in enumerate(refs):
        scratch[64 * i : 64 * (i + 1), :] = ref[:, at : at + width]


def store_parts(part, cols, keep1, send1, keep2, send2):
    places = (
        (keep1, (128, 0, 160, 64)),
        (send1, (192, 32, 224, 96)),
        (keep2, (144, 16, 208, 48)),
        (send2, (176, 80, 240, 112)),
    )
    for ref, starts in places:
        for i, start in enumerate(starts):
            rows = slice(SLOT * i, SLOT * (i + 1))
            ref[rows, cols] = part[start : start + SLOT].astype(ref.dtype)


def fwd_kernel(c1, qr1, c2, pr2, wg, wu, wd, other, keep1, send1, keep2, send2, rows):
    width = rows.shape[1]
    gather_rows((c1, qr1, c2, pr2), 0, width, rows)
    inner = []
    for weights in ((wg[...], wu[...]), (other[0:width, :], other[width : 2 * width, :])):
        gate, up = hidden(rows[...], *weights)
        inner.append((gate * jax.nn.sigmoid(gate) * up).astype(BF16))
    inner = jnp.concatenate(inner, axis=1)
    step = 512
    for at in range(0, width, step):
        cols = slice(at, at + step)
        down = jnp.concatenate([wd[:, cols], down_columns(other, at, step)], axis=0)
        part = jnp.dot(inner, down, preferred_element_type=F32)
        store_parts(part, cols, keep1, send1, keep2, send2)


def bwd_kernel(
    c1, qr1, c2, pr2, wg, wu, wd, other, _, keep1, send1, keep2, send2, rows, cots
):
    width = rows.shape[1]
    gather_rows((c1, qr1, c2, pr2), width, width, rows)
    gather_rows((c1, qr1, c2, pr2), 2 * width, width, cots)
    back = []
    products = None
    sources = (
        (wg[...], wu[...], wd[...]),
        (other[0:width, :], other[width : 2 * width, :], down_columns(other, 0, width)),
    )
    for gate_w, up_w, down_w in sources:
        gate, up = hidden(rows[...], gate_w, up_w)
        d_inner = lax.dot_general(cots[...], down_w, NT, preferred_element_type=F32)
        sig = jax.nn.sigmoid(gate)
        silu = gate * sig
        inner = (silu * up).astype(BF16).astype(F32)
        d_gate = (d_inner * up * sig * (1.0 + gate * (1.0 - sig))).astype(BF16)
        d_up = (d_inner * silu).astype(BF16)
        back.append(jnp.concatenate([d_gate, d_up], axis=1))
        product = inner * d_inner
        products = product if products is None else products + product
    count = products.shape[0]
    high = products.astype(BF16)
    low = (products - high.astype(F32)).astype(BF16)
    ones = jnp.ones((16, 128), BF16)
    grads = lax.dot_general(ones, high, NT, preferred_element_type=F32)
    grads = grads + lax.dot_general(ones, low, NT, preferred_element_type=F32)
    row = lax.broadcasted_iota(jnp.int32, (count, count), 0)
    col = lax.broadcasted_iota(jnp.int32, (count, count), 1)
    held = (row // SLOT == col // SLOT) & (row % SLOT == SLOT - 2)
    spread = jnp.where(held, grads[0:1, :], 0.0).astype(BF16)
    at_row = lax.broadcasted_iota(jnp.int32, (count, 128), 0)
    at_col = lax.broadcasted_iota(jnp.int32, (count, 128), 1)
    pick = (at_row % SLOT == at_col).astype(F32).astype(BF16)
    grad_rows = jnp.dot(spread, pick, preferred_element_type=F32)
    step = 512
    for at in range(0, width, step):
        cols = slice(at, at + step)
        there = slice(width + at, width + at + step)
        weights = (
            jnp.concatenate([wg[cols, :], wu[cols, :]], axis=1),
            jnp.concatenate([other[cols, :], other[there, :]], axis=1),
        )
        part = None
        for grad, weight in zip(back, weights):
            term = lax.dot_general(grad, weight, NT, preferred_element_type=F32)
            part = term if part is None else part + term
        if at == 0:
            part = jnp.concatenate([part[:, :128] + grad_rows, part[:, 128:]], axis=1)
        store_parts(part, cols, keep1, send1, keep2, send2)


def mixed_rows(masks, weight_ref, parts):
    weights = columns(weight_ref)
    spread = jnp.where(masks[0][0], weights[0], 0.0) + jnp.where(masks[1][0], weights[1], 0.0)
    high = spread.astype(BF16)
    rest = spread - high.astype(F32)
    middle = rest.astype(BF16)
    low = (rest - middle.astype(F32)).astype(BF16)
    tokens = spread.shape[0]
    pieces = jnp.concatenate([high, middle, low], axis=0)
    product = jnp.dot(pieces, jnp.concatenate(parts, axis=0), preferred_element_type=F32)
    return product[:tokens] + product[tokens : 2 * tokens] + product[2 * tokens :]


def last_kernel(
    info_ref, xa_ref, ra_ref, wa_ref, x_ref, route_ref, weight_ref, cot_ref, gain_ref, *rest
):
    width = x_ref.shape[1]
    arrived = [rest[0], rest[1], rest[3], rest[2]]
    parts_a = [ref[:, :width] for ref in arrived]
    parts = [ref[:, width:] for ref in arrived]
    out_a_ref, out_ref, grad_ref = rest[4:]
    mixed = mixed_rows(slot_masks(info_ref, ra_ref), wa_ref, parts_a)
    out_a_ref[...] = (xa_ref[...].astype(F32) + mixed).astype(BF16)
    masks = slot_masks(info_ref, route_ref)
    d_normed = mixed_rows(masks, weight_ref, parts)
    unit, scale = normalized(x_ref[...])
    q_term = d_normed * gain_ref[...]
    mean = jnp.mean(q_term * unit, axis=-1, keepdims=True)
    d_input = cot_ref[...].astype(F32) + scale * (q_term - unit * mean)
    out_ref[...] = d_input.astype(BF16)
    tokens = x_ref.shape[0]
    lanes = lax.broadcasted_iota(jnp.int32, (tokens, 128), 1)
    grads = []
    for _, rel, rank in masks:
        held = jnp.zeros((tokens, 128), F32)
        for j, part in enumerate(parts):
            row = part[:, :128].astype(F32)[SLOT - 2 : SLOT - 1, :]
            held = held + jnp.where(rel == j, row, 0.0)
        grads.append(jnp.sum(jnp.where(lanes == rank, held, 0.0), axis=1, keepdims=True))
    pair = lax.broadcasted_iota(jnp.int32, (tokens, 2), 1)
    grad_ref[...] = jnp.where(pair == 0, grads[0], grads[1]).astype(BF16)


def spread_rows(own, a, b, c):
    got_a, got_b, got_c = hop(a, HOP_A), hop(b, HOP_B), hop(c, HOP_C)
    half1 = jnp.concatenate([got_b, got_c], axis=0)
    half2 = jnp.concatenate([own, got_a], axis=0)
    q1 = hop(half1, HOP_X3)
    p2 = hop(half2, HOP_X1)
    c1 = jnp.concatenate([half1, q1], axis=0)
    c2 = jnp.concatenate([half2, p2], axis=0)
    return c1, hop(c1, HOP_X1), c2, hop(c2, HOP_X3)


def return_x(keep1, send1, keep2, send2):
    sum1 = keep1 + hop(send1, HOP_X3).astype(F32)
    sum2 = keep2 + hop(send2, HOP_X1).astype(F32)
    full1 = sum1[:32] + hop(sum1[32:].astype(BF16), HOP_X1).astype(F32)
    full2 = sum2[:32] + hop(sum2[32:].astype(BF16), HOP_X3).astype(F32)
    return full1.astype(BF16), full2.astype(BF16)


def return_z(full1, full2):
    back_a = hop(full2[:SLOT], HOP_A)
    back_c = hop(full2[SLOT:], HOP_C)
    back_b = hop(full1[SLOT:], HOP_B_BACK)
    return full1[:SLOT], back_a, back_c, back_b


def body(
    act_fwd,
    route_fwd,
    weight_fwd,
    act_bwd,
    route_bwd,
    weight_bwd,
    cot_bwd,
    norm_gain,
    w_gate,
    w_up,
    w_down,
):
    tokens, width = act_fwd.shape[1:]
    index = lax.axis_index("expert")
    info = jnp.stack([index >> 3, (index >> 2) & 1]).astype(jnp.int32)
    weights = (w_gate[0, 0], w_up[0, 0], w_down[0, 0])
    units = w_down.shape[2]
    wide = [((SLOT, 3 * width), BF16)] * 4 + [((3 * width, units), BF16)]
    sources = (
        route_fwd[0].T,
        route_bwd[0].T,
        act_fwd[0],
        norm_gain,
        act_bwd[0],
        cot_bwd[0],
    )
    scratch = [pltpu.VMEM(v.shape, v.dtype) for v in (*sources, weights[2])]
    *sent, merged = local_copy_call(first_kernel, (info,), (*sources, *weights), wide, scratch)
    other = hop(merged, HOP_W)
    rows = spread_rows(*sent)
    outs = [((64, width), F32), ((64, width), BF16)] * 2
    scratch = pltpu.VMEM((256, width), BF16)
    part_a = kernel_call(fwd_kernel, outs, 8, [scratch], info=False)(*rows, *weights, other)
    part_b = kernel_call(bwd_kernel, outs, 9, [scratch] * 2, info=False)(
        *rows, *weights, other, part_a[1]
    )
    halves = zip(return_x(*part_a), return_x(*part_b))
    back = return_z(*[jnp.concatenate(pair, axis=1) for pair in halves])
    layer_out, d_input, gate_grad = kernel_call(
        last_kernel, [((tokens, width), BF16)] * 2 + [((tokens, 2), BF16)], 12
    )(
        info,
        act_fwd[0],
        route_fwd[0].T,
        weight_fwd[0].T,
        act_bwd[0],
        route_bwd[0].T,
        weight_bwd[0].T,
        cot_bwd[0],
        norm_gain,
        *back,
    )
    act_next = shifted(layer_out, "section", 1)
    cot_next = shifted(d_input, "section", -1)
    return (act_next[None], cot_next[None], gate_grad[None])


def solution(mesh):
    return jax.shard_map(
        body,
        mesh=mesh,
        in_specs=(
            P("section", "expert", None),
            P("section", "expert", None),
            P("section", "expert", None),
            P("section", "expert", None),
            P("section", "expert", None),
            P("section", "expert", None),
            P("section", "expert", None),
            P("section", None),
            P("section", "expert", None, None),
            P("section", "expert", None, None),
            P("section", "expert", None, None),
        ),
        out_specs=(
            P("section", "expert", None),
            P("section", "expert", None),
            P("section", "expert", None),
        ),
        check_vma=False,
    )
```

```python
import jax
import jax.numpy as jnp
from jax import lax
from jax.experimental import pallas as pl
from jax.experimental.pallas import tpu as pltpu
from jax.sharding import PartitionSpec as P

EXPERTS = 4
GRID_X = 4
GRID_Z = 8
SLOT = 16
F32 = jnp.float32
BF16 = jnp.bfloat16
NT = (((1,), (1,)), ((), ()))
TN = (((0,), (0,)), ((), ()))


def expert_pairs(move):
    pairs = []
    for z in range(GRID_Z):
        for x in range(GRID_X):
            to_z, to_x = move(z, x)
            pairs.append((z * GRID_X + x, to_z % GRID_Z * GRID_X + to_x))
    return pairs


def signed(z, even, odd):
    return z + (odd if z % 2 else even)


HOP_W = expert_pairs(lambda z, x: (z ^ 1, x))
HOP_A = expert_pairs(lambda z, x: (signed(z, -1, 1), x))
HOP_B = expert_pairs(lambda z, x: (signed(z, 2, -2), x))
HOP_B_BACK = expert_pairs(lambda z, x: (signed(z, -2, 2), x))
HOP_C = expert_pairs(lambda z, x: (signed(z, -3, 3), x))
HOP_X1 = expert_pairs(lambda z, x: (z, x ^ 1))
HOP_X3 = expert_pairs(lambda z, x: (z, x ^ 3))


def hop(value, pairs):
    return lax.ppermute(value, "expert", pairs)


def shifted(value, axis, by):
    devices = lax.axis_size(axis)
    pairs = [(i, i + by) for i in range(devices) if 0 <= i + by < devices]
    return lax.ppermute(value, axis, pairs)


def kernel_call(kernel, outs, n_in, scratch=(), info=True, limit=32):
    smem = pl.BlockSpec(memory_space=pltpu.SMEM)
    vmem = pl.BlockSpec(memory_space=pltpu.VMEM)
    return pl.pallas_call(
        kernel,
        out_shape=[jax.ShapeDtypeStruct(s, d) for s, d in outs],
        in_specs=[smem] * info + [vmem] * n_in,
        out_specs=[vmem] * len(outs),
        scratch_shapes=list(scratch),
        compiler_params=pltpu.CompilerParams(vmem_limit_bytes=limit * 1024 * 1024),
    )


def local_copy_call(kernel, scalars, arrays, outs, scratch):
    arrays = [pltpu.with_memory_space_constraint(array, pltpu.HBM) for array in arrays]
    return pl.pallas_call(
        kernel,
        out_shape=[jax.ShapeDtypeStruct(s, d) for s, d in outs],
        in_specs=[pl.BlockSpec(memory_space=pltpu.SMEM)] * len(scalars)
        + [pl.BlockSpec(memory_space=pltpu.HBM)] * len(arrays),
        out_specs=[pl.BlockSpec(memory_space=pltpu.VMEM)] * len(outs),
        scratch_shapes=scratch + [pltpu.SemaphoreType.DMA((len(arrays),))],
        compiler_params=pltpu.CompilerParams(vmem_limit_bytes=16 * 1024 * 1024),
    )(*scalars, *arrays)


def columns(ref):
    count = ref.shape[1]
    row = lax.broadcasted_iota(jnp.int32, (count, count), 0)
    col = lax.broadcasted_iota(jnp.int32, (count, count), 1)
    values = ref[...].astype(F32)
    return [
        jnp.sum(jnp.where(row == col, values[k : k + 1, :], 0.0), axis=1, keepdims=True)
        for k in range(2)
    ]


def slot_masks(info_ref, route_ref):
    tokens = route_ref.shape[1]
    own, odd = info_ref[0], info_ref[1]
    lanes = lax.broadcasted_iota(jnp.int32, (tokens, 128), 1)
    route = [column.astype(jnp.int32) for column in columns(route_ref)]
    named = [(route[k] == lanes).astype(F32) for k in range(2)]
    row = lax.broadcasted_iota(jnp.int32, (tokens, tokens), 0)
    col = lax.broadcasted_iota(jnp.int32, (tokens, tokens), 1)
    earlier = (col < row).astype(BF16)
    counts = jnp.dot(earlier, (named[0] + named[1]).astype(BF16), preferred_element_type=F32)
    out = []
    for k in range(2):
        rank = jnp.sum(named[k] * counts, axis=1, keepdims=True).astype(jnp.int32)
        away = (route[k] - own) & 3
        side = jnp.where((away == 3) == (odd == 0), 1, 2)
        rel = jnp.where(away == 0, 0, jnp.where(away == 2, 3, side))
        slots = lax.broadcasted_iota(jnp.int32, (tokens, 4 * SLOT), 1)
        out.append((slots == rel * SLOT + rank, rel, rank))
    return out


def normalized(x):
    values = x.astype(F32)
    scale = lax.rsqrt(jnp.mean(values * values, axis=-1, keepdims=True) + 1e-06)
    return values * scale, scale


def first_kernel(info_ref, ra, rb, xa, gain_in, xb, cot, wg, wu, wd, *rest):
    outs, merged, scratch = rest[:4], rest[4], rest[5:]
    ra_ref, rb_ref, xa_ref, gain_ref, xb_ref, cot_ref, down, sems = scratch
    width, units = wg.shape
    moves = (
        (ra, ra_ref),
        (rb, rb_ref),
        (xa, xa_ref),
        (gain_in, gain_ref),
        (xb, xb_ref),
        (cot, cot_ref),
        (wd, down),
        (wg, merged.at[pl.ds(0, width)]),
        (wu, merged.at[pl.ds(width, width)]),
    )
    copies = [pltpu.make_async_copy(*move, sems.at[i]) for i, move in enumerate(moves)]
    for copy in copies:
        copy.start()
    for copy in copies[:2]:
        copy.wait()
    places = []
    for route_ref in (ra_ref, rb_ref):
        masks = slot_masks(info_ref, route_ref)
        places.append((masks[0][0] | masks[1][0]).astype(F32).astype(BF16))
    for copy in copies[2:6]:
        copy.wait()
    gain = gain_ref[...]
    normed_a = (normalized(xa_ref[...])[0] * gain).astype(BF16)
    normed_b = (normalized(xb_ref[...])[0] * gain).astype(BF16)
    sources = ((places[0], normed_a), (places[1], normed_b), (places[1], cot_ref[...]))
    for i, (place, rows) in enumerate(sources):
        packed = lax.dot_general(place, rows, TN, preferred_element_type=F32).astype(BF16)
        for j in range(4):
            outs[j][:, i * width : (i + 1) * width] = packed[j * SLOT : (j + 1) * SLOT]
    copies[6].wait()
    for at in range(0, width, units):
        merged[2 * width + at : 2 * width + at + units, :] = down[:, at : at + units]
    copies[7].wait()
    copies[8].wait()


def hidden(rows, wg, wu):
    both = jnp.dot(rows, jnp.concatenate([wg, wu], axis=1), preferred_element_type=F32)
    return both[:, :128], both[:, 128:]


def down_columns(merged, at, count):
    width = merged.shape[0] // 3
    starts = range(2 * width + at, 2 * width + at + count, 128)
    return jnp.concatenate([merged[start : start + 128, :] for start in starts], axis=1)


def gather_rows(refs, at, width, scratch):
    for i, ref in enumerate(refs):
        scratch[64 * i : 64 * (i + 1), :] = ref[:, at : at + width]


def store_parts(part, cols, keep1, send1, keep2, send2):
    places = (
        (keep1, (128, 0, 160, 64)),
        (send1, (192, 32, 224, 96)),
        (keep2, (144, 16, 208, 48)),
        (send2, (176, 80, 240, 112)),
    )
    for ref, starts in places:
        for i, start in enumerate(starts):
            rows = slice(SLOT * i, SLOT * (i + 1))
            ref[rows, cols] = part[start : start + SLOT].astype(ref.dtype)


def fwd_kernel(c1, qr1, c2, pr2, wg, wu, wd, other, keep1, send1, keep2, send2, rows):
    width = rows.shape[1]
    gather_rows((c1, qr1, c2, pr2), 0, width, rows)
    inner = []
    for weights in ((wg[...], wu[...]), (other[0:width, :], other[width : 2 * width, :])):
        gate, up = hidden(rows[...], *weights)
        inner.append((gate * jax.nn.sigmoid(gate) * up).astype(BF16))
    inner = jnp.concatenate(inner, axis=1)
    step = 512
    for at in range(0, width, step):
        cols = slice(at, at + step)
        down = jnp.concatenate([wd[:, cols], down_columns(other, at, step)], axis=0)
        part = jnp.dot(inner, down, preferred_element_type=F32)
        store_parts(part, cols, keep1, send1, keep2, send2)


def bwd_kernel(
    c1, qr1, c2, pr2, wg, wu, wd, other, _, keep1, send1, keep2, send2, rows, cots
):
    width = rows.shape[1]
    gather_rows((c1, qr1, c2, pr2), width, width, rows)
    gather_rows((c1, qr1, c2, pr2), 2 * width, width, cots)
    back = []
    products = None
    sources = (
        (wg[...], wu[...], wd[...]),
        (other[0:width, :], other[width : 2 * width, :], down_columns(other, 0, width)),
    )
    for gate_w, up_w, down_w in sources:
        gate, up = hidden(rows[...], gate_w, up_w)
        d_inner = lax.dot_general(cots[...], down_w, NT, preferred_element_type=F32)
        sig = jax.nn.sigmoid(gate)
        silu = gate * sig
        inner = (silu * up).astype(BF16).astype(F32)
        d_gate = (d_inner * up * sig * (1.0 + gate * (1.0 - sig))).astype(BF16)
        d_up = (d_inner * silu).astype(BF16)
        back.append(jnp.concatenate([d_gate, d_up], axis=1))
        product = inner * d_inner
        products = product if products is None else products + product
    count = products.shape[0]
    high = products.astype(BF16)
    low = (products - high.astype(F32)).astype(BF16)
    ones = jnp.ones((16, 128), BF16)
    grads = lax.dot_general(ones, high, NT, preferred_element_type=F32)
    grads = grads + lax.dot_general(ones, low, NT, preferred_element_type=F32)
    row = lax.broadcasted_iota(jnp.int32, (count, count), 0)
    col = lax.broadcasted_iota(jnp.int32, (count, count), 1)
    held = (row // SLOT == col // SLOT) & (row % SLOT == SLOT - 2)
    spread = jnp.where(held, grads[0:1, :], 0.0).astype(BF16)
    at_row = lax.broadcasted_iota(jnp.int32, (count, 128), 0)
    at_col = lax.broadcasted_iota(jnp.int32, (count, 128), 1)
    pick = (at_row % SLOT == at_col).astype(F32).astype(BF16)
    grad_rows = jnp.dot(spread, pick, preferred_element_type=F32)
    step = 512
    for at in range(0, width, step):
        cols = slice(at, at + step)
        there = slice(width + at, width + at + step)
        weights = (
            jnp.concatenate([wg[cols, :], wu[cols, :]], axis=1),
            jnp.concatenate([other[cols, :], other[there, :]], axis=1),
        )
        part = None
        for grad, weight in zip(back, weights):
            term = lax.dot_general(grad, weight, NT, preferred_element_type=F32)
            part = term if part is None else part + term
        if at == 0:
            part = jnp.concatenate([part[:, :128] + grad_rows, part[:, 128:]], axis=1)
        store_parts(part, cols, keep1, send1, keep2, send2)


def mixed_rows(masks, weight_ref, parts):
    weights = columns(weight_ref)
    spread = jnp.where(masks[0][0], weights[0], 0.0) + jnp.where(masks[1][0], weights[1], 0.0)
    high = spread.astype(BF16)
    rest = spread - high.astype(F32)
    middle = rest.astype(BF16)
    low = (rest - middle.astype(F32)).astype(BF16)
    tokens = spread.shape[0]
    pieces = jnp.concatenate([high, middle, low], axis=0)
    product = jnp.dot(pieces, jnp.concatenate(parts, axis=0), preferred_element_type=F32)
    return product[:tokens] + product[tokens : 2 * tokens] + product[2 * tokens :]


def last_kernel(
    info_ref, xa_ref, ra_ref, wa_ref, x_ref, route_ref, weight_ref, cot_ref, gain_ref, *rest
):
    width = x_ref.shape[1]
    arrived = [rest[0], rest[1], rest[3], rest[2]]
    parts_a = [ref[:, :width] for ref in arrived]
    parts = [ref[:, width:] for ref in arrived]
    out_a_ref, out_ref, grad_ref = rest[4:]
    mixed = mixed_rows(slot_masks(info_ref, ra_ref), wa_ref, parts_a)
    out_a_ref[...] = (xa_ref[...].astype(F32) + mixed).astype(BF16)
    masks = slot_masks(info_ref, route_ref)
    d_normed = mixed_rows(masks, weight_ref, parts)
    unit, scale = normalized(x_ref[...])
    q_term = d_normed * gain_ref[...]
    mean = jnp.mean(q_term * unit, axis=-1, keepdims=True)
    d_input = cot_ref[...].astype(F32) + scale * (q_term - unit * mean)
    out_ref[...] = d_input.astype(BF16)
    tokens = x_ref.shape[0]
    lanes = lax.broadcasted_iota(jnp.int32, (tokens, 128), 1)
    grads = []
    for _, rel, rank in masks:
        held = jnp.zeros((tokens, 128), F32)
        for j, part in enumerate(parts):
            row = part[:, :128].astype(F32)[SLOT - 2 : SLOT - 1, :]
            held = held + jnp.where(rel == j, row, 0.0)
        grads.append(jnp.sum(jnp.where(lanes == rank, held, 0.0), axis=1, keepdims=True))
    pair = lax.broadcasted_iota(jnp.int32, (tokens, 2), 1)
    grad_ref[...] = jnp.where(pair == 0, grads[0], grads[1]).astype(BF16)


def spread_rows(own, a, b, c):
    got_a, got_b, got_c = hop(a, HOP_A), hop(b, HOP_B), hop(c, HOP_C)
    c1 = jnp.concatenate([got_b, got_c, hop(got_b, HOP_X3), hop(got_c, HOP_X3)], axis=0)
    c2 = jnp.concatenate([own, got_a, hop(own, HOP_X1), hop(got_a, HOP_X1)], axis=0)
    return c1, hop(c1, HOP_X1), c2, hop(c2, HOP_X3)


def return_x(keep1, send1, keep2, send2):
    sum1 = keep1 + hop(send1, HOP_X3).astype(F32)
    sum2 = keep2 + hop(send2, HOP_X1).astype(F32)
    full1 = sum1[:32] + hop(sum1[32:].astype(BF16), HOP_X1).astype(F32)
    full2 = sum2[:32] + hop(sum2[32:].astype(BF16), HOP_X3).astype(F32)
    return full1.astype(BF16), full2.astype(BF16)


def return_z(full1, full2):
    back_a = hop(full2[:SLOT], HOP_A)
    back_c = hop(full2[SLOT:], HOP_C)
    back_b = hop(full1[SLOT:], HOP_B_BACK)
    return full1[:SLOT], back_a, back_c, back_b


def body(
    act_fwd,
    route_fwd,
    weight_fwd,
    act_bwd,
    route_bwd,
    weight_bwd,
    cot_bwd,
    norm_gain,
    w_gate,
    w_up,
    w_down,
):
    tokens, width = act_fwd.shape[1:]
    index = lax.axis_index("expert")
    info = jnp.stack([index >> 3, (index >> 2) & 1]).astype(jnp.int32)
    weights = (w_gate[0, 0], w_up[0, 0], w_down[0, 0])
    units = w_down.shape[2]
    wide = [((SLOT, 3 * width), BF16)] * 4 + [((3 * width, units), BF16)]
    sources = (
        route_fwd[0].T,
        route_bwd[0].T,
        act_fwd[0],
        norm_gain,
        act_bwd[0],
        cot_bwd[0],
    )
    scratch = [pltpu.VMEM(v.shape, v.dtype) for v in (*sources, weights[2])]
    *sent, merged = local_copy_call(first_kernel, (info,), (*sources, *weights), wide, scratch)
    other = hop(merged, HOP_W)
    rows = spread_rows(*sent)
    outs = [((64, width), F32), ((64, width), BF16)] * 2
    scratch = pltpu.VMEM((256, width), BF16)
    part_a = kernel_call(fwd_kernel, outs, 8, [scratch], info=False)(*rows, *weights, other)
    part_b = kernel_call(bwd_kernel, outs, 9, [scratch] * 2, info=False)(
        *rows, *weights, other, part_a[1]
    )
    halves = zip(return_x(*part_a), return_x(*part_b))
    back = return_z(*[jnp.concatenate(pair, axis=1) for pair in halves])
    layer_out, d_input, gate_grad = kernel_call(
        last_kernel, [((tokens, width), BF16)] * 2 + [((tokens, 2), BF16)], 12
    )(
        info,
        act_fwd[0],
        route_fwd[0].T,
        weight_fwd[0].T,
        act_bwd[0],
        route_bwd[0].T,
        weight_bwd[0].T,
        cot_bwd[0],
        norm_gain,
        *back,
    )
    act_next = shifted(layer_out, "section", 1)
    cot_next = shifted(d_input, "section", -1)
    return (act_next[None], cot_next[None], gate_grad[None])


def solution(mesh):
    return jax.shard_map(
        body,
        mesh=mesh,
        in_specs=(
            P("section", "expert", None),
            P("section", "expert", None),
            P("section", "expert", None),
            P("section", "expert", None),
            P("section", "expert", None),
            P("section", "expert", None),
            P("section", "expert", None),
            P("section", None),
            P("section", "expert", None, None),
            P("section", "expert", None, None),
            P("section", "expert", None, None),
        ),
        out_specs=(
            P("section", "expert", None),
            P("section", "expert", None),
            P("section", "expert", None),
        ),
        check_vma=False,
    )
```
